32 devices in a mesh: obs: 4 (over z), cell: 8 (over y, x, core).
Axes of the slice: x: 2, y: 2, z: 4, core: 2. Of those that a mesh axis runs over, the one named last changes fastest.
Arguments:
- start: float32 [4, 384, 128], P('obs', 'cell'), may hold values from -6 to 6
- lat_mats: float32 [384, 128, 128], P('cell'), may hold values from -0.5 to 0.5
- footprints: bfloat16 [64, 128, 768], P(('obs', 'cell')), may hold values from -0.21875 to 0.21875
- blk_sub: int32 [64], P(('obs', 'cell')), may hold values from 0 to 7
- blk_off: int32 [64], P(('obs', 'cell')), may hold values from 0 to 31, as said below
- counts: int32 [32], P('obs'), may hold values from 64 to 128
- rinv: float32 [4096], P('obs'), may hold values from 0.25 to 4
Outputs:
- krylov: float32 [4, 4, 384, 128], P(None, 'obs', 'cell')
- coeffs: float32 [2, 3], replicated
The draws below stay inside these ranges and needn't reach their ends.
Inputs may be any that keep to these rules, and one draw needn't show every extreme that they name: `blk_off`: of the 2 footprint blocks of one device, at most 1 read cell blocks in the periods of any one obs index (cell blocks k with the same k div (32 / 4)); on every device some obs index receives exactly 1.
All inputs are finite; a program needn't handle non-finite values.
Results may differ from the reference program's by a relative error of at most 0.009.
Values may be sent and summed in bfloat16 or wider, within the bound.
No kernel may reach another device: no remote copies, remote signals or barrier semaphores. Data moves between devices by JAX's collectives and lax.ppermute only.
A program may use at most 64 MiB of HBM per device.

```python
import math
import jax
import jax.numpy as jnp
from jax import lax

LAT = 128
LON = 384
PER_DEV = 1
OB = 128
NOB = 8
NB_DEV = 2
CR = 2
STEPS = 3
PERIODS = 4
BLOCKS = 64
SUBS = 32
N_OBS = 4
N_CELL = 8


def draw_blk_off(key, part):
    key = jax.random.fold_in(key, 3)
    devices = N_OBS * N_CELL
    span = PER_DEV * (LAT // (N_CELL * CR))
    keys = jax.random.split(key, devices + 1)
    orders = jax.vmap(lambda single: jax.random.permutation(single, N_OBS))(keys[:devices])
    position = jnp.arange(NB_DEV, dtype=jnp.int32) % N_OBS
    holder = orders[:, position]
    inside = jax.random.randint(keys[devices], (devices, NB_DEV), 0, span)
    return (holder * span + inside).reshape(devices * NB_DEV).astype(jnp.int32)


def touch_ends(entries, own_key, smallest, top_value):
    index_at = [jax.random.randint(jax.random.fold_in(own_key, axis), (), 0, length) for axis, length in enumerate(entries.shape)]
    widest = entries.shape.index(max(entries.shape))
    next_to = index_at[:widest] + [(index_at[widest] + 1) % entries.shape[widest]] + index_at[widest + 1:]
    return entries.at[tuple(index_at)].set(smallest).at[tuple(next_to)].set(top_value)


def shard_levels(own_key, shape, shards, low, high):
    level, own = 1.0, jax.random.fold_in(own_key, 6)
    for axis_at, shards_of in shards:
        steps = jnp.exp(jax.random.uniform(jax.random.fold_in(own, axis_at), (shards_of,), jnp.float32, low / len(shards), high / len(shards)))
        level = level * jnp.repeat(steps, shape[axis_at] // shards_of).reshape([-1 if axis == axis_at else 1 for axis in range(len(shape))])
    return level


def normal_values(key, dims, scale, limit, pieces=(), held_as=jnp.bfloat16):
    loudness = shard_levels(key, dims, pieces, -0.22, 0.18) if pieces else 1.0
    entries = jax.random.normal(key, dims, jnp.float32) * scale * loudness
    return jnp.minimum(jnp.maximum(entries, -limit), limit).astype(held_as)


def setup_inputs(seed: int = 0) -> dict:
    streams_of = jax.random.split(jax.random.key(seed), 8)
    return {
        "start": normal_values(streams_of[0], (PERIODS, LON, LAT), 1.0, 6.0, ((0, 4), (1, 8)), jnp.float32),
        "lat_mats": normal_values(streams_of[1], (LON, LAT, LAT), LAT ** -0.5, 0.5, ((0, 8),), jnp.float32),
        "footprints": normal_values(streams_of[2], (BLOCKS, OB, CR * LON), (CR * LON) ** -0.5, 0.21875, ((0, 32),)),
        "blk_sub": touch_ends(jax.random.randint(streams_of[3], (BLOCKS,), 0, NOB), jax.random.fold_in(streams_of[3], 1), 0, NOB - 1).astype(jnp.int32),
        "blk_off": draw_blk_off(jax.random.fold_in(streams_of[7], 71), 0),
        "counts": touch_ends(jax.random.randint(streams_of[5], (SUBS,), OB // 2, OB + 1), jax.random.fold_in(streams_of[5], 1), OB // 2, OB).astype(jnp.int32),
        "rinv": jnp.clip(jnp.exp(math.log(4.0) - 2.7725887 * jax.random.uniform(streams_of[6], (SUBS * OB,), jnp.float32) ** shard_levels(streams_of[6], (SUBS * OB,), ((0, 4),), -0.2, 0.2)), 0.25, 4.0),
    }


HIGH = lax.Precision.HIGHEST

def lon_table(order):
    index = jnp.arange(order, dtype=jnp.int32)
    mode = index[:, None]
    point = index[None, :]
    half = order // 2
    freq = jnp.where(mode <= half, mode, mode - half)
    phase = (freq * point % order).astype(jnp.float32) * (2.0 * math.pi / order)
    factor = jnp.where((mode == 0) | (mode == half), math.sqrt(1.0 / order), math.sqrt(2.0 / order))
    return jnp.where(mode <= half, jnp.cos(phase), jnp.sin(phase)) * factor

def reference(start, lat_mats, footprints, blk_sub, blk_off, counts, rinv):
    table = lon_table(LON)
    band = LAT // N_CELL
    groups = band // CR
    ncbd = PERIODS * groups
    devices = N_OBS * N_CELL
    width = CR * LON
    owner = jnp.arange(BLOCKS, dtype=jnp.int32) // NB_DEV
    glob_sub = owner // N_CELL * NOB + blk_sub
    glob_off = owner % N_CELL * ncbd + blk_off
    valid = (jnp.arange(OB, dtype=jnp.int32)[None, :] < counts[:, None]).astype(jnp.float32)
    weights = rinv.reshape(SUBS, OB) * valid
    foot_dev = footprints.reshape(devices, NB_DEV, OB, width)

    def forward_one(pair):
        wts, vec = pair
        return jnp.einsum('bok,bk->bo', wts.astype(jnp.float32), vec.astype(jnp.float32), precision=HIGH)

    def adjoint_one(pair):
        wts, vec = pair
        return jnp.einsum('bok,bo->bk', wts.astype(jnp.float32), vec.astype(jnp.float32), precision=HIGH)

    def hessian(field):
        spread = jnp.einsum('mab,pmb->pma', lat_mats, field, precision=HIGH)
        grid = jnp.einsum('pma,mn->pan', spread, table, precision=HIGH).astype(jnp.bfloat16)
        blocks = grid.reshape(PERIODS, N_CELL, groups, width).transpose(1, 0, 2, 3).reshape(N_CELL * ncbd, width)
        picked = blocks[glob_off].reshape(devices, NB_DEV, width)
        prod = lax.map(forward_one, (foot_dev, picked)).reshape(BLOCKS, OB)
        sim = jax.ops.segment_sum(prod, glob_sub, SUBS)
        weighted = (weights * sim).astype(jnp.bfloat16)
        chosen = weighted[glob_sub].reshape(devices, NB_DEV, OB)
        terms = lax.map(adjoint_one, (foot_dev, chosen)).reshape(BLOCKS, width)
        summed = jax.ops.segment_sum(terms, glob_off, N_CELL * ncbd)
        back = summed.reshape(N_CELL, PERIODS, groups, width).transpose(1, 0, 2, 3).reshape(PERIODS, LAT, LON)
        coef = jnp.einsum('pan,mn->pam', back, table, precision=HIGH)
        return field + jnp.einsum('mab,pam->pmb', lat_mats, coef, precision=HIGH)
    first = jnp.sqrt(jnp.sum(start * start))
    current = start / first
    previous = jnp.zeros_like(start)
    beta = jnp.float32(0.0)
    vectors = [current]
    alphas = []
    betas = []
    for step in range(STEPS):
        image = hessian(current) - beta * previous
        alpha = jnp.sum(current * image)
        direction = image - alpha * current
        beta = jnp.sqrt(jnp.sum(direction * direction))
        previous = current
        current = direction / beta
        vectors.append(current)
        alphas.append(alpha)
        betas.append(beta)
    factor = jnp.sqrt(jnp.float32(PERIODS * LON * LAT))
    krylov = jnp.stack(vectors) * factor
    coeffs = jnp.stack([jnp.stack(alphas), jnp.stack(betas)]).astype(jnp.float32)
    return (krylov, coeffs)
```

```python
import functools
import math

import jax
import jax.numpy as jnp
import ml_dtypes
import numpy as np
from jax import lax
from jax.experimental import pallas as pl
from jax.experimental.pallas import tpu as pltpu
from jax.sharding import PartitionSpec as P

CR = 2
STEPS = 3
ROWS = 8
VMEM = pl.BlockSpec(memory_space=pltpu.VMEM)
SMEM = pl.BlockSpec(memory_space=pltpu.SMEM)
F32 = jnp.float32
BF16 = jnp.bfloat16


def lon_table(order, parts, padded):
    index = np.arange(order)
    half = order // 2
    freq = np.where(index <= half, index, index - half)[:, None]
    phase = (freq * index[None, :] % order) * (2.0 * math.pi / order)
    factor = np.where((index == 0) | (index == half), math.sqrt(1.0 / order), math.sqrt(2.0 / order))
    table = np.where(index[:, None] <= half, np.cos(phase), np.sin(phase)) * factor[:, None]
    table = table.reshape(parts, order // parts, order)
    table = np.pad(table, ((0, 0), (0, padded - order // parts), (0, 0))).reshape(parts * padded, order)
    high = table.astype(np.float32).astype(ml_dtypes.bfloat16)
    low = (table - high.astype(np.float64)).astype(np.float32).astype(ml_dtypes.bfloat16)
    return high, low


def call(kernel, outs, specs, *args, scratch=()):
    return pl.pallas_call(
        kernel,
        out_shape=outs,
        in_specs=specs,
        out_specs=jax.tree.map(lambda _: VMEM, outs),
        scratch_shapes=scratch,
        compiler_params=pltpu.CompilerParams(vmem_limit_bytes=16 * 1024 * 1024),
    )(*args)


def transform_kernel(dims, high_ref, low_ref, foot_ref, off_ref, sub_ref, out_ref):
    nc, nb, modes, groups, band = dims
    ob = foot_ref.shape[1]
    lon = high_ref.shape[1]
    contract = (((1,), (1,)), ((), ()))
    for b in range(nb):
        for r in range(CR):
            foot = foot_ref[b, :, r * lon:(r + 1) * lon]
            hat = lax.dot_general(high_ref[...], foot, contract, preferred_element_type=F32)
            hat += lax.dot_general(low_ref[...], foot, contract, preferred_element_type=F32)
            hat = hat.astype(BF16)
            at = (b * CR + r) * modes
            for c in range(nc):
                out_ref[c, at:at + modes, :] = hat[c * modes:(c + 1) * modes, :]
    lane = lax.broadcasted_iota(jnp.int32, (16, ob), 1)
    ids = jnp.zeros((16, ob), F32)
    for b in range(nb):
        ids = jnp.where(lane == b, off_ref[b].astype(F32), ids)
        ids = jnp.where(lane == nb + b, sub_ref[b].astype(F32), ids)
    ids = ids.astype(BF16)
    for c in range(nc):
        out_ref[c, nb * CR * modes:, :] = ids


def fold(ref):
    periods, modes, _ = ref.shape
    total = jnp.zeros((ROWS, ref.shape[2]), F32)
    for p in range(periods):
        for at in range(0, modes, ROWS):
            part = ref[p, at:at + ROWS, :]
            total += part * part
    return total


def forward(dims, field_ref, lat_ref, foot_ref, ids_ref, sim_ref, out_ref):
    nc, nb, modes, groups, band = dims
    subs = sim_ref.shape[0] - ROWS
    sim_ref[...] = jnp.zeros_like(sim_ref)
    for j in range(nc):
        for b in range(nb):
            off = ids_ref[j, b]
            sub = ids_ref[j, nb + b]
            period = off // groups
            row = j * band + off % groups * CR
            total = None
            for r in range(CR):
                column = jnp.sum(lat_ref[row + r] * field_ref[period], axis=1, keepdims=True)
                at = (b * CR + r) * modes
                term = foot_ref[j, at:at + modes, :].astype(F32) * column
                total = term if total is None else total + term
            sim_ref[pl.ds(sub, 1), :] += jnp.sum(total, axis=0, keepdims=True)
    sim_ref[subs:, :] = fold(field_ref)
    for c in range(nc):
        out_ref[c] = sim_ref[...]


def first_kernel(dims, near_ref, lat_ref, foot_ref, ids_ref, out_ref, field_ref, sim_ref):
    modes = dims[2]
    per_dev = field_ref.shape[0] // near_ref.shape[0]
    for i in range(near_ref.shape[0]):
        for l in range(per_dev):
            field_ref[i * per_dev + l] = near_ref[i, l * modes:(l + 1) * modes, :]
    forward(dims, field_ref, lat_ref, foot_ref, ids_ref, sim_ref, out_ref)


def adjoint_kernel(dims, sim_ref, weight_ref, foot_ref, ids_ref, out_ref, norm_ref, weighted_ref):
    nc, nb, modes, groups, band = dims
    subs = weight_ref.shape[0]
    mine = nc * nb
    total = sim_ref[0]
    for c in range(1, nc):
        total += sim_ref[c]
    norm = jnp.sqrt(jnp.sum(total[subs:], keepdims=True))
    norm_ref[...] = jnp.broadcast_to(norm, norm_ref.shape)
    sim = total[:subs] / norm
    weighted = sim * weight_ref[...]
    weighted_ref[...] = weighted
    lane = lax.broadcasted_iota(jnp.int32, (modes, 128), 1)
    parts = [jnp.zeros((modes, 128), F32) for _ in range(CR)]
    for j in range(nc):
        for b in range(nb):
            chosen = weighted_ref[pl.ds(ids_ref[j, nb + b], 1), :]
            for r in range(CR):
                at = (b * CR + r) * modes
                column = jnp.sum(foot_ref[j, at:at + modes, :].astype(F32) * chosen, axis=1, keepdims=True)
                parts[r] = jnp.where(lane == j * nb + b, column, parts[r])
    rest = 128 - CR * modes
    if rest:
        parts.append(jnp.zeros((rest, 128), F32))
    rows = jnp.concatenate(parts, axis=0).T
    power = sim * weighted
    for i in range(out_ref.shape[0]):
        out_ref[i, :mine, :] = rows[:mine]
        out_ref[i, mine:, :] = power


def image_kernel(dims, first, last, *refs):
    if first:
        coef_ref, norm_ref, field_ref, lat_ref, foot_ref, ids_ref, all_ref, *refs = refs
        prior_ref = None
    else:
        coef_ref, norm_ref, field_ref, prior_ref, lat_ref, foot_ref, ids_ref, all_ref, *refs = refs
    out_ref, vector_ref, next_ref, alpha_ref, sim_ref = refs
    nc, nb, modes, groups, band = dims
    mine = nc * nb
    no = coef_ref.shape[0]
    periods = field_ref.shape[0]
    power = coef_ref[0, mine:, :]
    for i in range(1, no):
        power += coef_ref[i, mine:, :]
    gain = jnp.sum(power, keepdims=True)
    alpha_ref[...] = jnp.broadcast_to(1.0 + gain, alpha_ref.shape)
    norm = norm_ref[0:1, :]
    for p in range(periods):
        vector = field_ref[p] / norm
        vector_ref[p] = vector
        rest = vector * -gain
        if not first:
            rest -= prior_ref[p] * norm
        next_ref[p] = rest

    def group(i, carry):
        coef = coef_ref[i, :mine, :].T
        for j in range(nc):
            for b in range(nb):
                off = all_ref[i, j * 2 * nb + b]
                period = off // groups
                row = j * band + off % groups * CR
                at = j * nb + b
                total = next_ref[period]
                for r in range(CR):
                    total += coef[r * modes:(r + 1) * modes, at:at + 1] * lat_ref[row + r]
                next_ref[period] = total
        return carry

    if no <= 4:
        for i in range(no):
            group(i, 0)
    else:
        lax.fori_loop(0, no, group, 0)
    if last:
        total = fold(next_ref)
        for c in range(nc):
            out_ref[c] = total
    else:
        forward(dims, next_ref, lat_ref, foot_ref, ids_ref, sim_ref, out_ref)


def finish_kernel(factor, own_ref, sum_ref, *refs):
    vectors, refs = refs[:STEPS], refs[STEPS:]
    field_ref, refs = refs[0], refs[1:]
    alphas, refs = refs[:STEPS], refs[STEPS:]
    norms, refs = refs[:STEPS - 1], refs[STEPS - 1:]
    out_ref, coef_ref = refs
    per_dev = out_ref.shape[1]
    total = sum_ref[0]
    for c in range(1, sum_ref.shape[0]):
        total += sum_ref[c]
    norm = jnp.sqrt(jnp.sum(total, keepdims=True))
    for l in range(per_dev):
        at = own_ref[0] * per_dev + l
        for k in range(STEPS):
            out_ref[k, l] = vectors[k][at] * factor
        out_ref[STEPS, l] = field_ref[at] / norm * factor
    row = lax.broadcasted_iota(jnp.int32, coef_ref.shape, 0)
    col = lax.broadcasted_iota(jnp.int32, coef_ref.shape, 1)
    coefs = jnp.zeros(coef_ref.shape, F32)
    for k in range(STEPS):
        beta = norms[k][0:1, 0:1] if k < STEPS - 1 else norm
        coefs = jnp.where((row == 0) & (col == k), alphas[k][0:1, 0:1], coefs)
        coefs = jnp.where((row == 1) & (col == k), beta, coefs)
    coef_ref[...] = coefs


def swap(array, axis):
    return lax.all_to_all(array, axis, split_axis=0, concat_axis=0, tiled=True)


def body(start, lat_mats, footprints, blk_sub, blk_off, counts, rinv):
    per_dev, held, lat_rows = start.shape
    nc = lax.axis_size("cell")
    no = lax.axis_size("obs")
    lon_cols = held * nc
    band = lat_rows // nc
    groups = band // CR
    nb, ob, _ = footprints.shape
    subs = counts.shape[0]
    modes = -(-held // 16) * 16
    mine = nc * nb
    periods = per_dev * no
    dims = (nc, nb, modes, groups, band)
    shape = functools.partial(jax.ShapeDtypeStruct, dtype=F32)

    valid = (jnp.arange(ob, dtype=jnp.int32)[None, :] < counts[:, None]).astype(F32)
    weights = rinv.reshape(subs, ob) * valid
    high, low = lon_table(lon_cols, nc, modes)
    if modes != held:
        start = jnp.pad(start, ((0, 0), (0, modes - held), (0, 0)))
        lat_mats = jnp.pad(lat_mats, ((0, modes - held), (0, 0), (0, 0)))
    lat = lat_mats.transpose(1, 0, 2)

    foot_rows = nb * CR * modes
    hats = call(
        functools.partial(transform_kernel, dims),
        jax.ShapeDtypeStruct((nc, foot_rows + 16, ob), BF16),
        [VMEM, VMEM, VMEM, SMEM, SMEM],
        jnp.asarray(high), jnp.asarray(low), footprints, blk_off, blk_sub,
    )
    foot = swap(hats, "cell")
    ids = foot[:, foot_rows, :2 * nb].astype(F32)
    tail = jnp.pad(ids.reshape(1, -1), ((0, ROWS - 1), (0, lat_rows - 2 * mine)))
    ids = ids.astype(jnp.int32)
    near = jnp.concatenate([start.reshape(per_dev * modes, lat_rows), tail], axis=0)
    near = swap(jnp.broadcast_to(near[None], (no,) + near.shape), "obs")
    every = near[:, per_dev * modes, :2 * mine].astype(jnp.int32)

    field_shape = shape((periods, modes, lat_rows))
    small = shape((ROWS, 128))
    sim_scratch = pltpu.VMEM((subs + ROWS, ob), F32)
    sims, field = call(
        functools.partial(first_kernel, dims),
        (shape((nc, subs + ROWS, ob)), field_shape),
        [VMEM, VMEM, VMEM, SMEM],
        near, lat, foot, ids,
        scratch=[sim_scratch],
    )
    vectors, alphas, norms = [], [], []
    for step in range(STEPS):
        last = step == STEPS - 1
        sims = swap(sims, "cell")
        coefs, norm = call(
            functools.partial(adjoint_kernel, dims),
            (shape((no, mine + subs, 128)), small),
            [VMEM, VMEM, VMEM, SMEM],
            sims, weights, foot, ids,
            scratch=[pltpu.VMEM((subs, ob), F32)],
        )
        coefs = swap(coefs, "obs")
        before = [vectors[-1]] if step else []
        sims, vector, field, alpha = call(
            functools.partial(image_kernel, dims, step == 0, last),
            (
                shape((nc, ROWS if last else subs + ROWS, 128)),
                field_shape,
                field_shape,
                small,
            ),
            [VMEM] * (5 + len(before)) + [SMEM, SMEM],
            coefs, norm, field, *before, lat, foot, ids, every,
            scratch=[sim_scratch],
        )
        vectors.append(vector)
        alphas.append(alpha)
        norms.append(norm)
    sums = swap(sims, "cell")
    factor = math.sqrt(periods * lon_cols * lat_rows)
    own = lax.axis_index("obs").astype(jnp.int32).reshape(1)
    krylov, coeffs = call(
        functools.partial(finish_kernel, factor),
        (shape((STEPS + 1, per_dev, modes, lat_rows)), shape((2, STEPS))),
        [SMEM] + [VMEM] * (1 + STEPS + 1 + STEPS + STEPS - 1),
        own, sums, *vectors, field, *alphas, *norms[1:],
    )
    return krylov[:, :, :held], coeffs


def solution(mesh):
    placed = (
        P("obs", "cell", None),
        P("cell", None, None),
        P(("obs", "cell"), None, None),
        P(("obs", "cell")),
        P(("obs", "cell")),
        P("obs"),
        P("obs"),
    )
    return jax.shard_map(
        body,
        mesh=mesh,
        in_specs=placed,
        out_specs=(P(None, "obs", "cell", None), P()),
        check_vma=False,
    )
```

```python
import functools
import math

import jax
import jax.numpy as jnp
import ml_dtypes
import numpy as np
from jax import lax
from jax.experimental import pallas as pl
from jax.experimental.pallas import tpu as pltpu
from jax.sharding import PartitionSpec as P

CR = 2
STEPS = 3
ROWS = 8
VMEM = pl.BlockSpec(memory_space=pltpu.VMEM)
ANY = pl.BlockSpec(memory_space=pl.ANY)
SMEM = pl.BlockSpec(memory_space=pltpu.SMEM)
F32 = jnp.float32
BF16 = jnp.bfloat16


def lon_table(order, parts, padded):
    index = np.arange(order)
    half = order // 2
    freq = np.where(index <= half, index, index - half)[:, None]
    phase = (freq * index[None, :] % order) * (2.0 * math.pi / order)
    factor = np.where((index == 0) | (index == half), math.sqrt(1.0 / order), math.sqrt(2.0 / order))
    table = np.where(index[:, None] <= half, np.cos(phase), np.sin(phase)) * factor[:, None]
    table = table.reshape(parts, order // parts, order)
    table = np.pad(table, ((0, 0), (0, padded - order // parts), (0, 0))).reshape(parts * padded, order)
    high = table.astype(np.float32).astype(ml_dtypes.bfloat16)
    low = (table - high.astype(np.float64)).astype(np.float32).astype(ml_dtypes.bfloat16)
    return high, low


def call(kernel, outs, specs, *args, scratch=()):
    return pl.pallas_call(
        kernel,
        out_shape=outs,
        in_specs=specs,
        out_specs=jax.tree.map(lambda _: VMEM, outs),
        scratch_shapes=scratch,
        compiler_params=pltpu.CompilerParams(vmem_limit_bytes=8 * 1024 * 1024),
    )(*args)


def tree_sum(parts):
    parts = list(parts)
    while len(parts) > 1:
        parts = [sum(parts[at:at + 2][1:], parts[at]) for at in range(0, len(parts), 2)]
    return parts[0]


def transform_kernel(dims, own_ref, high_any, low_any, foot_any, off_any, sub_any, *refs):
    nc, nb, modes, groups, band = dims
    outs, refs = refs[:nc], refs[nc:]
    high_ref, low_ref, foot_ref, off_ref, sub_ref, hats_ref, sems = refs
    copies = [
        pltpu.make_async_copy(source, target, sems.at[at])
        for at, (source, target) in enumerate(
            [
                (foot_any, foot_ref),
                (high_any, high_ref),
                (low_any, low_ref),
                (off_any, off_ref),
                (sub_any, sub_ref),
            ]
        )
    ]
    for copy in copies:
        copy.start()
    for copy in copies:
        copy.wait()
    ob = foot_ref.shape[1]
    lon = high_ref.shape[1]
    contract = (((1,), (1,)), ((), ()))
    for b in range(nb):
        for r in range(CR):
            foot = foot_ref[b, :, r * lon:(r + 1) * lon]
            hat = lax.dot_general(high_ref[...], foot, contract, preferred_element_type=F32)
            hat += lax.dot_general(low_ref[...], foot, contract, preferred_element_type=F32)
            hat = hat.astype(BF16)
            at = (b * CR + r) * modes
            for c in range(nc):
                hats_ref[c, at:at + modes, :] = hat[c * modes:(c + 1) * modes, :]
    lane = lax.broadcasted_iota(jnp.int32, (16, ob), 1)
    ids = jnp.zeros((16, ob), F32)
    for b in range(nb):
        ids = jnp.where(lane == b, off_ref[b].astype(F32), ids)
        ids = jnp.where(lane == nb + b, sub_ref[b].astype(F32), ids)
    ids = ids.astype(BF16)
    for s in range(nc):
        outs[s][:nb * CR * modes, :] = hats_ref[own_ref[1] ^ s]
        outs[s][nb * CR * modes:, :] = ids


def fold(ref):
    periods, modes, _ = ref.shape
    total = jnp.zeros((ROWS, ref.shape[2]), F32)
    for p in range(periods):
        for at in range(0, modes, ROWS):
            part = ref[p, at:at + ROWS, :]
            total += part * part
    return total


def forward(dims, own_ref, field_ref, lat_ref, foot_refs, ids_ref, out_ref):
    nc, nb, modes, groups, band = dims
    subs = out_ref.shape[0] - ROWS
    out_ref[:subs] = jnp.zeros((subs, out_ref.shape[1]), F32)
    for s in range(nc):
        for b in range(nb):
            off = ids_ref[s, b]
            sub = ids_ref[s, nb + b]
            period = off // groups
            row = (own_ref[1] ^ s) * band + off % groups * CR
            total = None
            for r in range(CR):
                column = jnp.sum(lat_ref[row + r] * field_ref[period], axis=1, keepdims=True)
                at = (b * CR + r) * modes
                term = foot_refs[s][at:at + modes, :].astype(F32) * column
                total = term if total is None else total + term
            out_ref[pl.ds(sub, 1), :] += jnp.sum(total, axis=0, keepdims=True)
    out_ref[subs:, :] = fold(field_ref)


def first_kernel(dims, no, own_ref, ids_ref, lat_ref, *refs):
    nc, _, modes, _, _ = dims
    near_refs, refs = refs[:no], refs[no:]
    foot_refs, refs = refs[:nc], refs[nc:]
    out_ref, field_ref = refs
    per_dev = field_ref.shape[0] // no
    for s in range(no):
        for l in range(per_dev):
            field_ref[(own_ref[0] ^ s) * per_dev + l] = near_refs[s][l]
    forward(dims, own_ref, field_ref, lat_ref, foot_refs, ids_ref, out_ref)


def adjoint_kernel(dims, tails, ids_ref, weight_ref, *refs):
    nc, nb, modes, groups, band = dims
    sim_refs, refs = refs[:nc], refs[nc:]
    foot_refs, refs = refs[:nc], refs[nc:]
    tail_refs, refs = refs[:tails], refs[tails:]
    out_ref, norm_ref, weighted_ref = refs
    subs = weight_ref.shape[0]
    mine = nc * nb
    total = tree_sum(ref[...] for ref in sim_refs)
    norm = jnp.sqrt(jnp.sum(total[subs:], keepdims=True))
    norm_ref[...] = jnp.broadcast_to(norm, norm_ref.shape)
    sim = total[:subs] / norm
    weighted = sim * weight_ref[...]
    weighted_ref[...] = weighted
    lane = lax.broadcasted_iota(jnp.int32, (modes, 128), 1)
    parts = [jnp.zeros((modes, 128), F32) for _ in range(CR)]
    for s in range(nc):
        for b in range(nb):
            chosen = weighted_ref[pl.ds(ids_ref[s, nb + b], 1), :]
            for r in range(CR):
                at = (b * CR + r) * modes
                column = jnp.sum(foot_refs[s][at:at + modes, :].astype(F32) * chosen, axis=1, keepdims=True)
                parts[r] = jnp.where(lane == s * nb + b, column, parts[r])
    rest = 128 - CR * modes
    if rest:
        parts.append(jnp.zeros((rest, 128), F32))
    rows = jnp.concatenate(parts, axis=0).T
    out_ref[:mine, :] = rows[:mine]
    out_ref[mine:mine + subs, :] = sim * weighted
    for tail_ref in tail_refs:
        out_ref[mine + subs:, :] = tail_ref[...]


def image_kernel(dims, no, first, last, own_ref, ids_ref, all_ref, lat_ref, norm_ref, field_ref, *refs):
    nc, nb, modes, groups, band = dims
    if not first:
        prior_ref, refs = refs[0], refs[1:]
    coef_refs, refs = refs[:no], refs[no:]
    foot_refs, refs = refs[:nc], refs[nc:]
    out_ref, vector_ref, next_ref, alpha_ref, held_ref = refs
    mine = nc * nb
    periods = field_ref.shape[0]
    subs = ROWS
    for s in range(no):
        held_ref[s] = coef_refs[s][:mine, :]
    gain = jnp.sum(tree_sum(ref[mine:mine + subs, :] for ref in coef_refs), keepdims=True)
    alpha_ref[...] = jnp.broadcast_to(1.0 + gain, alpha_ref.shape)
    norm = norm_ref[0:1, :]
    for p in range(periods):
        vector = field_ref[p] / norm
        vector_ref[p] = vector
        rest = vector * -gain
        if not first:
            rest -= prior_ref[p] * norm
        next_ref[p] = rest

    def group(i, carry):
        at_i = own_ref[0] ^ i
        coef = held_ref[at_i].T
        for s in range(nc):
            for b in range(nb):
                at = s * nb + b
                off = all_ref[at_i, s * 2 * nb + b]
                period = off // groups
                row = (own_ref[1] ^ s) * band + off % groups * CR
                total = next_ref[period]
                for r in range(CR):
                    total += coef[r * modes:(r + 1) * modes, at:at + 1] * lat_ref[row + r]
                next_ref[period] = total
        return carry

    if no <= 4:
        for i in range(no):
            group(i, 0)
    else:
        lax.fori_loop(0, no, group, 0)
    if last:
        out_ref[...] = fold(next_ref)
    else:
        forward(dims, own_ref, next_ref, lat_ref, foot_refs, ids_ref, out_ref)


def finish_kernel(factor, nc, own_ref, *refs):
    sum_refs, refs = refs[:nc], refs[nc:]
    vectors, refs = refs[:STEPS], refs[STEPS:]
    field_ref, refs = refs[0], refs[1:]
    alphas, refs = refs[:STEPS], refs[STEPS:]
    norms, refs = refs[:STEPS - 1], refs[STEPS - 1:]
    out_ref, coef_ref = refs
    per_dev = out_ref.shape[1]
    norm = jnp.sqrt(jnp.sum(tree_sum(ref[...] for ref in sum_refs), keepdims=True))
    for l in range(per_dev):
        at = own_ref[2] * per_dev + l
        for k in range(STEPS):
            out_ref[k, l] = vectors[k][at] * factor
        out_ref[STEPS, l] = field_ref[at] / norm * factor
    row = lax.broadcasted_iota(jnp.int32, coef_ref.shape, 0)
    col = lax.broadcasted_iota(jnp.int32, coef_ref.shape, 1)
    coefs = jnp.zeros(coef_ref.shape, F32)
    for k in range(STEPS):
        beta = norms[k][0:1, 0:1] if k < STEPS - 1 else norm
        coefs = jnp.where((row == 0) & (col == k), alphas[k][0:1, 0:1], coefs)
        coefs = jnp.where((row == 1) & (col == k), beta, coefs)
    coef_ref[...] = coefs


def permuted(size):
    return size <= 8 and size & (size - 1) == 0


def share(arrays, axis):
    size = lax.axis_size(axis)
    arrays = arrays if isinstance(arrays, (list, tuple)) else [arrays] * size
    if permuted(size):
        return [
            arrays[s] if s == 0 else lax.ppermute(arrays[s], axis, [(d, d ^ s) for d in range(size)])
            for s in range(size)
        ]
    swapped = lax.all_to_all(jnp.stack(arrays), axis, split_axis=0, concat_axis=0, tiled=True)
    return [swapped[s] for s in range(size)]


def body(start, lat_mats, footprints, blk_sub, blk_off, counts, rinv):
    per_dev, held, lat_rows = start.shape
    nc = lax.axis_size("cell")
    no = lax.axis_size("obs")
    lon_cols = held * nc
    band = lat_rows // nc
    groups = band // CR
    nb, ob, _ = footprints.shape
    subs = counts.shape[0]
    modes = -(-held // 16) * 16
    mine = nc * nb
    periods = per_dev * no
    dims = (nc, nb, modes, groups, band)
    shape = functools.partial(jax.ShapeDtypeStruct, dtype=F32)

    valid = (jnp.arange(ob, dtype=jnp.int32)[None, :] < counts[:, None]).astype(F32)
    weights = rinv.reshape(subs, ob) * valid
    high, low = lon_table(lon_cols, nc, modes)
    if modes != held:
        start = jnp.pad(start, ((0, 0), (0, modes - held), (0, 0)))
        lat_mats = jnp.pad(lat_mats, ((0, modes - held), (0, 0), (0, 0)))
    lat = lat_mats.transpose(1, 0, 2)
    at_obs = lax.axis_index("obs").astype(jnp.int32)
    at_cell = lax.axis_index("cell").astype(jnp.int32)
    own = jnp.stack([at_obs if permuted(no) else 0 * at_obs, at_cell if permuted(nc) else 0 * at_cell, at_obs])

    near = share(start, "obs")
    foot_rows = nb * CR * modes
    hats = call(
        functools.partial(transform_kernel, dims),
        [jax.ShapeDtypeStruct((foot_rows + 16, ob), BF16)] * nc,
        [SMEM] + [ANY] * 5,
        own, jnp.asarray(high), jnp.asarray(low), footprints, blk_off, blk_sub,
        scratch=[
            pltpu.VMEM(high.shape, BF16),
            pltpu.VMEM(low.shape, BF16),
            pltpu.VMEM(footprints.shape, BF16),
            pltpu.SMEM((nb,), jnp.int32),
            pltpu.SMEM((nb,), jnp.int32),
            pltpu.VMEM((nc, foot_rows, ob), BF16),
            pltpu.SemaphoreType.DMA((5,)),
        ],
    )
    foot = share(hats, "cell")
    ids = jnp.stack([part[foot_rows, :2 * nb] for part in foot]).astype(F32)
    tail = jnp.pad(ids.reshape(1, -1), ((0, ROWS - 1), (0, 128 - 2 * mine)))
    ids = ids.astype(jnp.int32)

    field_shape = shape((periods, modes, lat_rows))
    small = shape((ROWS, 128))
    sims, field = call(
        functools.partial(first_kernel, dims, no),
        (shape((subs + ROWS, ob)), field_shape),
        [SMEM, SMEM] + [VMEM] * (1 + no + nc),
        own, ids, lat, *near, *foot,
    )
    vectors, alphas, norms = [], [], []
    for step in range(STEPS):
        last = step == STEPS - 1
        tails = [] if step else [tail]
        coefs, norm = call(
            functools.partial(adjoint_kernel, dims, len(tails)),
            (shape((mine + subs + ROWS * len(tails), 128)), small),
            [SMEM] + [VMEM] * (1 + 2 * nc + len(tails)),
            ids, weights, *share(sims, "cell"), *foot, *tails,
            scratch=[pltpu.VMEM((subs, ob), F32)],
        )
        coefs = share(coefs, "obs")
        if step == 0:
            every = jnp.stack([part[mine + subs, :2 * mine] for part in coefs]).astype(jnp.int32)
        before = [vectors[-1]] if step else []
        sims, vector, field, alpha = call(
            functools.partial(image_kernel, dims, no, step == 0, last),
            (
                shape((ROWS if last else subs + ROWS, 128)),
                field_shape,
                field_shape,
                small,
            ),
            [SMEM] * 3 + [VMEM] * (3 + len(before) + no + nc),
            own, ids, every, lat, norm, field, *before, *coefs, *foot,
            scratch=[pltpu.VMEM((no, mine, 128), F32)],
        )
        vectors.append(vector)
        alphas.append(alpha)
        norms.append(norm)
    factor = math.sqrt(periods * lon_cols * lat_rows)
    krylov, coeffs = call(
        functools.partial(finish_kernel, factor, nc),
        (shape((STEPS + 1, per_dev, modes, lat_rows)), shape((2, STEPS))),
        [SMEM] + [VMEM] * (nc + STEPS + 1 + STEPS + STEPS - 1),
        own, *share(sims, "cell"), *vectors, field, *alphas, *norms[1:],
    )
    return krylov[:, :, :held], coeffs


def solution(mesh):
    placed = (
        P("obs", "cell", None),
        P("cell", None, None),
        P(("obs", "cell"), None, None),
        P(("obs", "cell")),
        P(("obs", "cell")),
        P("obs"),
        P("obs"),
    )
    return jax.shard_map(
        body,
        mesh=mesh,
        in_specs=placed,
        out_specs=(P(None, "obs", "cell", None), P()),
        check_vma=False,
    )
```

```python
import functools
import math

import jax
import jax.numpy as jnp
import ml_dtypes
import numpy as np
from jax import lax
from jax.experimental import pallas as pl
from jax.experimental.pallas import tpu as pltpu
from jax.sharding import PartitionSpec as P

CR = 2
STEPS = 3
ROWS = 8
VMEM = pl.BlockSpec(memory_space=pltpu.VMEM)
HBM = pl.BlockSpec(memory_space=pltpu.HBM)
SMEM = pl.BlockSpec(memory_space=pltpu.SMEM)
F32 = jnp.float32
BF16 = jnp.bfloat16


def lon_table(order, parts, padded):
    index = np.arange(order)
    half = order // 2
    freq = np.where(index <= half, index, index - half)[:, None]
    phase = (freq * index[None, :] % order) * (2.0 * math.pi / order)
    factor = np.where((index == 0) | (index == half), math.sqrt(1.0 / order), math.sqrt(2.0 / order))
    table = np.where(index[:, None] <= half, np.cos(phase), np.sin(phase)) * factor[:, None]
    table = table.reshape(parts, order // parts, order)
    table = np.pad(table, ((0, 0), (0, padded - order // parts), (0, 0))).reshape(parts * padded, order)
    high = table.astype(np.float32).astype(ml_dtypes.bfloat16)
    low = (table - high.astype(np.float64)).astype(np.float32).astype(ml_dtypes.bfloat16)
    return high, low


def call(kernel, outs, specs, *args, scratch=()):
    return pl.pallas_call(
        kernel,
        out_shape=outs,
        in_specs=specs,
        out_specs=jax.tree.map(lambda _: VMEM, outs),
        scratch_shapes=scratch,
        compiler_params=pltpu.CompilerParams(vmem_limit_bytes=8 * 1024 * 1024),
    )(*args)


def tree_sum(parts):
    parts = list(parts)
    while len(parts) > 1:
        parts = [sum(parts[at:at + 2][1:], parts[at]) for at in range(0, len(parts), 2)]
    return parts[0]


def transform_kernel(dims, high_any, low_any, foot_any, off_any, sub_any, count_any, rinv_any, *refs):
    nc, nb, modes, groups, band = dims
    out_ref, weight_ref, high_ref, low_ref, foot_ref, off_ref, sub_ref, count_ref, rinv_ref, sems = refs
    copies = [
        pltpu.make_async_copy(source, target, sems.at[at])
        for at, (source, target) in enumerate(
            [
                (foot_any, foot_ref),
                (high_any, high_ref),
                (low_any, low_ref),
                (off_any, off_ref),
                (sub_any, sub_ref),
                (count_any, count_ref),
                (rinv_any, rinv_ref),
            ]
        )
    ]
    for copy in copies:
        copy.start()
    for copy in copies:
        copy.wait()
    ob = foot_ref.shape[1]
    lon = high_ref.shape[1]
    contract = (((1,), (1,)), ((), ()))
    for b in range(nb):
        for r in range(CR):
            foot = foot_ref[b, :, r * lon:(r + 1) * lon]
            hat = lax.dot_general(high_ref[...], foot, contract, preferred_element_type=F32)
            hat += lax.dot_general(low_ref[...], foot, contract, preferred_element_type=F32)
            hat = hat.astype(BF16)
            at = (b * CR + r) * modes
            for c in range(nc):
                out_ref[c, at:at + modes, :] = hat[c * modes:(c + 1) * modes, :]
    lane = lax.broadcasted_iota(jnp.int32, (16, ob), 1)
    ids = jnp.zeros((16, ob), F32)
    for b in range(nb):
        ids = jnp.where(lane == b, off_ref[b].astype(F32), ids)
        ids = jnp.where(lane == nb + b, sub_ref[b].astype(F32), ids)
    ids = ids.astype(BF16)
    for c in range(nc):
        out_ref[c, nb * CR * modes:, :] = ids
    row = lax.broadcasted_iota(jnp.int32, weight_ref.shape, 0)
    limit = jnp.zeros(weight_ref.shape, jnp.int32)
    for s in range(weight_ref.shape[0]):
        limit = jnp.where(row == s, count_ref[s], limit)
    lane = lax.broadcasted_iota(jnp.int32, weight_ref.shape, 1)
    weight_ref[...] = jnp.where(lane < limit, rinv_ref[...], 0.0)


def fold(ref):
    periods, modes, _ = ref.shape
    total = jnp.zeros((ROWS, ref.shape[2]), F32)
    for p in range(periods):
        for at in range(0, modes, ROWS):
            part = ref[p, at:at + ROWS, :]
            total += part * part
    return total


def forward(dims, field_ref, lat_ref, foot_ref, ids_ref, sim_ref, out_ref):
    nc, nb, modes, groups, band = dims
    subs = sim_ref.shape[0] - ROWS
    sim_ref[...] = jnp.zeros_like(sim_ref)
    for j in range(nc):
        for b in range(nb):
            off = ids_ref[j, b]
            sub = ids_ref[j, nb + b]
            period = off // groups
            row = j * band + off % groups * CR
            total = None
            for r in range(CR):
                column = jnp.sum(lat_ref[row + r] * field_ref[period], axis=1, keepdims=True)
                at = (b * CR + r) * modes
                term = foot_ref[j, at:at + modes, :].astype(F32) * column
                total = term if total is None else total + term
            sim_ref[pl.ds(sub, 1), :] += jnp.sum(total, axis=0, keepdims=True)
    sim_ref[subs:, :] = fold(field_ref)
    for c in range(nc):
        out_ref[c] = sim_ref[...]


def pieces(refs, size, rows):
    found = []
    for ref in refs:
        found += [ref.at[at:at + rows] for at in range(0, ref.shape[0], rows)]
    assert len(found) == size
    return found


def first_kernel(dims, no, own_ref, ids_ref, lat_ref, foot_ref, *refs):
    modes = dims[2]
    near_refs, refs = refs[:-3], refs[-3:]
    out_ref, field_ref, sim_ref = refs
    per_dev = field_ref.shape[0] // no
    for s, near_ref in enumerate(pieces(near_refs, no, per_dev * modes)):
        for l in range(per_dev):
            field_ref[(own_ref[0] ^ s) * per_dev + l] = near_ref[l * modes:(l + 1) * modes, :]
    forward(dims, field_ref, lat_ref, foot_ref, ids_ref, sim_ref, out_ref)


def adjoint_kernel(dims, first, ids_ref, sim_ref, weight_ref, foot_ref, out_ref, norm_ref, weighted_ref):
    nc, nb, modes, groups, band = dims
    subs = weight_ref.shape[0]
    mine = nc * nb
    total = tree_sum(sim_ref[c] for c in range(nc))
    norm = jnp.sqrt(jnp.sum(total[subs:], keepdims=True))
    norm_ref[...] = jnp.broadcast_to(norm, norm_ref.shape)
    sim = total[:subs] / norm
    weighted = sim * weight_ref[...]
    weighted_ref[...] = weighted
    lane = lax.broadcasted_iota(jnp.int32, (modes, 128), 1)
    parts = [jnp.zeros((modes, 128), F32) for _ in range(CR)]
    for j in range(nc):
        for b in range(nb):
            chosen = weighted_ref[pl.ds(ids_ref[j, nb + b], 1), :]
            for r in range(CR):
                at = (b * CR + r) * modes
                column = jnp.sum(foot_ref[j, at:at + modes, :].astype(F32) * chosen, axis=1, keepdims=True)
                parts[r] = jnp.where(lane == j * nb + b, column, parts[r])
    rest = 128 - CR * modes
    if rest:
        parts.append(jnp.zeros((rest, 128), F32))
    rows = jnp.concatenate(parts, axis=0).T
    out_ref[:mine, :] = rows[:mine]
    out_ref[mine:mine + subs, :] = sim * weighted
    if first:
        lane = lax.broadcasted_iota(jnp.int32, (ROWS, 128), 1)
        tail = jnp.zeros((ROWS, 128), F32)
        for j in range(nc):
            for q in range(2 * nb):
                tail = jnp.where(lane == j * 2 * nb + q, ids_ref[j, q].astype(F32), tail)
        out_ref[mine + subs:, :] = tail


def every_kernel(dims, no, at, *refs):
    refs, out_ref = refs[:-1], refs[-1]
    rows = sum(ref.shape[0] for ref in refs) // no
    for s, ref in enumerate(pieces(refs, no, rows)):
        out_ref[s:s + 1, :] = ref[at:at + ROWS, :][0:1].astype(jnp.int32)


def image_kernel(dims, no, first, last, own_ref, ids_ref, all_ref, lat_ref, foot_ref, norm_ref, field_ref, *refs):
    nc, nb, modes, groups, band = dims
    if not first:
        prior_ref, refs = refs[0], refs[1:]
    coef_refs, refs = refs[:-6], refs[-6:]
    out_ref, vector_ref, next_ref, alpha_ref, held_ref, sim_ref = refs
    mine = nc * nb
    periods = field_ref.shape[0]
    subs = sim_ref.shape[0] - ROWS
    rows = sum(ref.shape[0] for ref in coef_refs) // no
    coef_refs = pieces(coef_refs, no, rows)
    for s in range(no):
        held_ref[s] = coef_refs[s][:mine, :]
    gain = jnp.sum(tree_sum(ref[mine:mine + subs, :] for ref in coef_refs), keepdims=True)
    alpha_ref[...] = jnp.broadcast_to(1.0 + gain, alpha_ref.shape)
    norm = norm_ref[0:1, :]
    for p in range(periods):
        vector = field_ref[p] / norm
        vector_ref[p] = vector
        rest = vector * -gain
        if not first:
            rest -= prior_ref[p] * norm
        next_ref[p] = rest

    def group(i, carry):
        at_i = own_ref[0] ^ i
        coef = held_ref[at_i].T
        for j in range(nc):
            for b in range(nb):
                at = j * nb + b
                off = all_ref[at_i, j * 2 * nb + b]
                period = off // groups
                row = j * band + off % groups * CR
                total = next_ref[period]
                for r in range(CR):
                    total += coef[r * modes:(r + 1) * modes, at:at + 1] * lat_ref[row + r]
                next_ref[period] = total
        return carry

    if no <= 4:
        for i in range(no):
            group(i, 0)
    else:
        lax.fori_loop(0, no, group, 0)
    if last:
        total = fold(next_ref)
        for c in range(nc):
            out_ref[c] = total
    else:
        forward(dims, next_ref, lat_ref, foot_ref, ids_ref, sim_ref, out_ref)


def finish_kernel(factor, own_ref, sum_ref, *refs):
    vectors, refs = refs[:STEPS], refs[STEPS:]
    field_ref, refs = refs[0], refs[1:]
    alphas, refs = refs[:STEPS], refs[STEPS:]
    norms, refs = refs[:STEPS - 1], refs[STEPS - 1:]
    out_ref, coef_ref = refs
    per_dev = out_ref.shape[1]
    total = tree_sum(sum_ref[c] for c in range(sum_ref.shape[0]))
    norm = jnp.sqrt(jnp.sum(total, keepdims=True))
    for l in range(per_dev):
        at = own_ref[1] * per_dev + l
        for k in range(STEPS):
            out_ref[k, l] = vectors[k][at] * factor
        out_ref[STEPS, l] = field_ref[at] / norm * factor
    row = lax.broadcasted_iota(jnp.int32, coef_ref.shape, 0)
    col = lax.broadcasted_iota(jnp.int32, coef_ref.shape, 1)
    coefs = jnp.zeros(coef_ref.shape, F32)
    for k in range(STEPS):
        beta = norms[k][0:1, 0:1] if k < STEPS - 1 else norm
        coefs = jnp.where((row == 0) & (col == k), alphas[k][0:1, 0:1], coefs)
        coefs = jnp.where((row == 1) & (col == k), beta, coefs)
    coef_ref[...] = coefs


def join_kernel(*refs):
    refs, out_ref = refs[:-1], refs[-1]
    rows = refs[0].shape[0]
    for at, ref in enumerate(refs):
        out_ref[at * rows:(at + 1) * rows, :] = ref[...]


def doubled(size):
    return size <= 4 and size & (size - 1) == 0


def share(array, axis):
    size = lax.axis_size(axis)
    if not doubled(size):
        return [swap(jnp.broadcast_to(array[None], (size,) + array.shape), axis).reshape(-1, array.shape[1])]
    found, step = array, 1
    while True:
        came = lax.ppermute(found, axis, [(d, d ^ step) for d in range(size)])
        step *= 2
        if step == size:
            return [found, came]
        rows, lanes = found.shape
        found = call(join_kernel, jax.ShapeDtypeStruct((2 * rows, lanes), F32), [VMEM] * 2, found, came)


def swap(array, axis):
    return lax.all_to_all(array, axis, split_axis=0, concat_axis=0, tiled=True)


def body(start, lat_mats, footprints, blk_sub, blk_off, counts, rinv):
    per_dev, held, lat_rows = start.shape
    nc = lax.axis_size("cell")
    no = lax.axis_size("obs")
    lon_cols = held * nc
    band = lat_rows // nc
    groups = band // CR
    nb, ob, _ = footprints.shape
    subs = counts.shape[0]
    modes = -(-held // 16) * 16
    mine = nc * nb
    periods = per_dev * no
    dims = (nc, nb, modes, groups, band)
    shape = functools.partial(jax.ShapeDtypeStruct, dtype=F32)

    high, low = lon_table(lon_cols, nc, modes)
    if modes != held:
        start = jnp.pad(start, ((0, 0), (0, modes - held), (0, 0)))
        lat_mats = jnp.pad(lat_mats, ((0, modes - held), (0, 0), (0, 0)))
    lat = lat_mats.transpose(1, 0, 2)
    at_obs = lax.axis_index("obs").astype(jnp.int32)
    own = jnp.stack([at_obs if doubled(no) else 0 * at_obs, at_obs])

    near = share(start.reshape(per_dev * modes, lat_rows), "obs")
    foot_rows = nb * CR * modes
    hats, weights = call(
        functools.partial(transform_kernel, dims),
        (jax.ShapeDtypeStruct((nc, foot_rows + 16, ob), BF16), shape((subs, ob))),
        [HBM] * 7,
        jnp.asarray(high), jnp.asarray(low), footprints, blk_off, blk_sub, counts, rinv.reshape(subs, ob),
        scratch=[
            pltpu.VMEM(high.shape, BF16),
            pltpu.VMEM(low.shape, BF16),
            pltpu.VMEM(footprints.shape, BF16),
            pltpu.SMEM((nb,), jnp.int32),
            pltpu.SMEM((nb,), jnp.int32),
            pltpu.SMEM((subs,), jnp.int32),
            pltpu.VMEM((subs, ob), F32),
            pltpu.SemaphoreType.DMA((7,)),
        ],
    )
    foot = swap(hats, "cell")
    ids = foot[:, foot_rows, :2 * nb].astype(jnp.int32)

    field_shape = shape((periods, modes, lat_rows))
    small = shape((ROWS, 128))
    sim_scratch = pltpu.VMEM((subs + ROWS, ob), F32)
    sims, field = call(
        functools.partial(first_kernel, dims, no),
        (shape((nc, subs + ROWS, ob)), field_shape),
        [SMEM, SMEM] + [VMEM] * (2 + len(near)),
        own, ids, lat, foot, *near,
        scratch=[sim_scratch],
    )
    vectors, alphas, norms = [], [], []
    for step in range(STEPS):
        first, last = step == 0, step == STEPS - 1
        coefs, norm = call(
            functools.partial(adjoint_kernel, dims, first),
            (shape((mine + subs + (ROWS if first else 0), 128)), small),
            [SMEM] + [VMEM] * 3,
            ids, swap(sims, "cell"), weights, foot,
            scratch=[pltpu.VMEM((subs, ob), F32)],
        )
        coefs = share(coefs, "obs")
        if first:
            every = call(
                functools.partial(every_kernel, dims, no, mine + subs),
                jax.ShapeDtypeStruct((no, 128), jnp.int32),
                [VMEM] * len(coefs),
                *coefs,
            )
        before = [] if first else [vectors[-1]]
        sims, vector, field, alpha = call(
            functools.partial(image_kernel, dims, no, first, last),
            (
                shape((nc, ROWS if last else subs + ROWS, 128)),
                field_shape,
                field_shape,
                small,
            ),
            [SMEM] * 3 + [VMEM] * (4 + len(before) + len(coefs)),
            own, ids, every, lat, foot, norm, field, *before, *coefs,
            scratch=[pltpu.VMEM((no, mine, 128), F32), sim_scratch],
        )
        vectors.append(vector)
        alphas.append(alpha)
        norms.append(norm)
    factor = math.sqrt(periods * lon_cols * lat_rows)
    krylov, coeffs = call(
        functools.partial(finish_kernel, factor),
        (shape((STEPS + 1, per_dev, modes, lat_rows)), shape((2, STEPS))),
        [SMEM] + [VMEM] * (1 + STEPS + 1 + STEPS + STEPS - 1),
        own, swap(sims, "cell"), *vectors, field, *alphas, *norms[1:],
    )
    return krylov[:, :, :held], coeffs


def solution(mesh):
    placed = (
        P("obs", "cell", None),
        P("cell", None, None),
        P(("obs", "cell"), None, None),
        P(("obs", "cell")),
        P(("obs", "cell")),
        P("obs"),
        P("obs"),
    )
    return jax.shard_map(
        body,
        mesh=mesh,
        in_specs=placed,
        out_specs=(P(None, "obs", "cell", None), P()),
        check_vma=False,
    )
```

```python
import functools
import math

import jax
import jax.numpy as jnp
import ml_dtypes
import numpy as np
from jax import lax
from jax.experimental import pallas as pl
from jax.experimental.pallas import tpu as pltpu
from jax.sharding import PartitionSpec as P

CR = 2
STEPS = 3
ROWS = 8
VMEM = pl.BlockSpec(memory_space=pltpu.VMEM)
ANY = pl.BlockSpec(memory_space=pl.ANY)
SMEM = pl.BlockSpec(memory_space=pltpu.SMEM)
F32 = jnp.float32
BF16 = jnp.bfloat16


def lon_table(order, parts, padded):
    index = np.arange(order)
    half = order // 2
    freq = np.where(index <= half, index, index - half)[:, None]
    phase = (freq * index[None, :] % order) * (2.0 * math.pi / order)
    factor = np.where((index == 0) | (index == half), math.sqrt(1.0 / order), math.sqrt(2.0 / order))
    table = np.where(index[:, None] <= half, np.cos(phase), np.sin(phase)) * factor[:, None]
    table = table.reshape(parts, order // parts, order)
    table = np.pad(table, ((0, 0), (0, padded - order // parts), (0, 0))).reshape(parts * padded, order)
    high = table.astype(np.float32).astype(ml_dtypes.bfloat16)
    low = (table - high.astype(np.float64)).astype(np.float32).astype(ml_dtypes.bfloat16)
    return high, low


def call(kernel, outs, specs, *args, scratch=(), limit=8):
    return pl.pallas_call(
        kernel,
        out_shape=outs,
        in_specs=specs,
        out_specs=jax.tree.map(lambda _: VMEM, outs),
        scratch_shapes=scratch,
        compiler_params=pltpu.CompilerParams(vmem_limit_bytes=limit * 1024 * 1024),
    )(*args)


def tree_sum(parts):
    parts = list(parts)
    while len(parts) > 1:
        parts = [sum(parts[at:at + 2][1:], parts[at]) for at in range(0, len(parts), 2)]
    return parts[0]


def transform_kernel(dims, high_any, low_any, foot_any, off_any, sub_any, count_any, rinv_any, *refs):
    nc, nb, modes, groups, band = dims
    out_ref, weight_ref, high_ref, low_ref, foot_ref, off_ref, sub_ref, count_ref, rinv_ref, sems = refs
    copies = [
        pltpu.make_async_copy(source, target, sems.at[at])
        for at, (source, target) in enumerate(
            [
                (foot_any, foot_ref),
                (high_any, high_ref),
                (low_any, low_ref),
                (off_any, off_ref),
                (sub_any, sub_ref),
                (count_any, count_ref),
                (rinv_any, rinv_ref),
            ]
        )
    ]
    for copy in copies:
        copy.start()
    for copy in copies:
        copy.wait()
    ob = foot_ref.shape[1]
    lon = high_ref.shape[1]
    contract = (((1,), (1,)), ((), ()))
    for b in range(nb):
        for r in range(CR):
            foot = foot_ref[b, :, r * lon:(r + 1) * lon]
            hat = lax.dot_general(high_ref[...], foot, contract, preferred_element_type=F32)
            hat += lax.dot_general(low_ref[...], foot, contract, preferred_element_type=F32)
            hat = hat.astype(BF16)
            at = (b * CR + r) * modes
            for c in range(nc):
                out_ref[c, at:at + modes, :] = hat[c * modes:(c + 1) * modes, :]
    lane = lax.broadcasted_iota(jnp.int32, (16, ob), 1)
    ids = jnp.zeros((16, ob), F32)
    for b in range(nb):
        ids = jnp.where(lane == b, off_ref[b].astype(F32), ids)
        ids = jnp.where(lane == nb + b, sub_ref[b].astype(F32), ids)
    ids = ids.astype(BF16)
    for c in range(nc):
        out_ref[c, nb * CR * modes:, :] = ids
    row = lax.broadcasted_iota(jnp.int32, weight_ref.shape, 0)
    limit = jnp.zeros(weight_ref.shape, jnp.int32)
    for s in range(weight_ref.shape[0]):
        limit = jnp.where(row == s, count_ref[s], limit)
    lane = lax.broadcasted_iota(jnp.int32, weight_ref.shape, 1)
    weight_ref[...] = jnp.where(lane < limit, rinv_ref[...], 0.0)


def fold(ref):
    periods, modes, _ = ref.shape
    total = jnp.zeros((ROWS, ref.shape[2]), F32)
    for p in range(periods):
        for at in range(0, modes, ROWS):
            part = ref[p, at:at + ROWS, :]
            total += part * part
    return total


def forward(dims, field_ref, lat_ref, foot_ref, ids_ref, sim_ref, out_ref):
    nc, nb, modes, groups, band = dims
    subs = sim_ref.shape[0] - ROWS
    sim_ref[...] = jnp.zeros_like(sim_ref)
    for j in range(nc):
        for b in range(nb):
            off = ids_ref[j, b]
            sub = ids_ref[j, nb + b]
            period = off // groups
            row = j * band + off % groups * CR
            total = None
            for r in range(CR):
                column = jnp.sum(lat_ref[row + r] * field_ref[period], axis=1, keepdims=True)
                at = (b * CR + r) * modes
                term = foot_ref[j, at:at + modes, :].astype(F32) * column
                total = term if total is None else total + term
            sim_ref[pl.ds(sub, 1), :] += jnp.sum(total, axis=0, keepdims=True)
    sim_ref[subs:, :] = fold(field_ref)
    for c in range(nc):
        out_ref[c] = sim_ref[...]


def pieces(refs, size, rows):
    found = []
    for ref in refs:
        found += [ref.at[at:at + rows] for at in range(0, ref.shape[0], rows)]
    assert len(found) == size
    return found


def first_kernel(dims, no, own_ref, lat_ref, came_ref, *refs):
    nc, nb, modes, _, _ = dims
    near_refs, refs = refs[:-7], refs[-7:]
    out_ref, field_ref, foot_ref, all_ref, sim_ref, ids_ref, sem = refs
    rows = nb * CR * modes
    for j in range(nc):
        all_ref[j:j + 1, :] = came_ref[j, rows:rows + 16, :].astype(F32)[0:1].astype(jnp.int32)
    copy = pltpu.make_async_copy(all_ref, ids_ref, sem)
    copy.start()
    for j in range(nc):
        foot_ref[j] = came_ref[j, :rows, :]
    per_dev = field_ref.shape[0] // no
    for s, near_ref in enumerate(pieces(near_refs, no, per_dev * modes)):
        for l in range(per_dev):
            field_ref[(own_ref[0] ^ s) * per_dev + l] = near_ref[l * modes:(l + 1) * modes, :]
    copy.wait()
    forward(dims, field_ref, lat_ref, foot_ref, ids_ref, sim_ref, out_ref)


def adjoint_kernel(dims, first, ids_ref, sim_ref, weight_ref, foot_ref, out_ref, norm_ref, weighted_ref):
    nc, nb, modes, groups, band = dims
    subs = weight_ref.shape[0]
    mine = nc * nb
    total = tree_sum(sim_ref[c] for c in range(nc))
    norm = jnp.sqrt(jnp.sum(total[subs:], keepdims=True))
    norm_ref[...] = jnp.broadcast_to(norm, norm_ref.shape)
    sim = total[:subs] / norm
    weighted = sim * weight_ref[...]
    weighted_ref[...] = weighted
    lane = lax.broadcasted_iota(jnp.int32, (modes, 128), 1)
    parts = [jnp.zeros((modes, 128), F32) for _ in range(CR)]
    for j in range(nc):
        for b in range(nb):
            chosen = weighted_ref[pl.ds(ids_ref[j, nb + b], 1), :]
            for r in range(CR):
                at = (b * CR + r) * modes
                column = jnp.sum(foot_ref[j, at:at + modes, :].astype(F32) * chosen, axis=1, keepdims=True)
                parts[r] = jnp.where(lane == j * nb + b, column, parts[r])
    rest = 128 - CR * modes
    if rest:
        parts.append(jnp.zeros((rest, 128), F32))
    rows = jnp.concatenate(parts, axis=0).T
    out_ref[:mine, :] = rows[:mine]
    out_ref[mine:mine + subs, :] = sim * weighted
    if first:
        lane = lax.broadcasted_iota(jnp.int32, (ROWS, 128), 1)
        tail = jnp.zeros((ROWS, 128), F32)
        for j in range(nc):
            for q in range(2 * nb):
                tail = jnp.where(lane == j * 2 * nb + q, ids_ref[j, q].astype(F32), tail)
        out_ref[mine + subs:, :] = tail


def every_kernel(dims, no, at, *refs):
    refs, out_ref = refs[:-1], refs[-1]
    rows = sum(ref.shape[0] for ref in refs) // no
    for s, ref in enumerate(pieces(refs, no, rows)):
        out_ref[s:s + 1, :] = ref[at:at + ROWS, :][0:1].astype(jnp.int32)


def image_kernel(dims, no, first, last, own_ref, ids_ref, all_ref, lat_ref, foot_ref, norm_ref, field_ref, *refs):
    nc, nb, modes, groups, band = dims
    if not first:
        prior_ref, refs = refs[0], refs[1:]
    coef_refs, refs = refs[:-7], refs[-7:]
    if last:
        out_ref, row_ref, mine_ref, alpha_ref, next_ref, held_ref, sim_ref = refs
    else:
        out_ref, row_ref, next_ref, vector_ref, alpha_ref, held_ref, sim_ref = refs
    mine = nc * nb
    periods = field_ref.shape[0]
    per_dev = row_ref.shape[0]
    subs = sim_ref.shape[0] - ROWS
    rows = sum(ref.shape[0] for ref in coef_refs) // no
    coef_refs = pieces(coef_refs, no, rows)
    for s in range(no):
        held_ref[s] = coef_refs[s][:mine, :]
    gain = jnp.sum(tree_sum(ref[mine:mine + subs, :] for ref in coef_refs), keepdims=True)
    alpha_ref[...] = jnp.broadcast_to(1.0 + gain, alpha_ref.shape)
    norm = norm_ref[0:1, :]
    scale = 1.0 / norm
    for p in range(periods):
        vector = field_ref[p] * scale
        if not last:
            vector_ref[p] = vector
        rest = vector * -gain
        if not first:
            rest -= prior_ref[p] * norm
        next_ref[p] = rest
    for l in range(per_dev):
        row_ref[l] = field_ref[own_ref[1] * per_dev + l] * scale

    def group(i, carry):
        at_i = own_ref[0] ^ i
        coef = held_ref[at_i].T
        for j in range(nc):
            for b in range(nb):
                at = j * nb + b
                off = all_ref[at_i, j * 2 * nb + b]
                period = off // groups
                row = j * band + off % groups * CR
                total = next_ref[period]
                for r in range(CR):
                    total += coef[r * modes:(r + 1) * modes, at:at + 1] * lat_ref[row + r]
                next_ref[period] = total
        return carry

    if no <= 4:
        for i in range(no):
            group(i, 0)
    else:
        lax.fori_loop(0, no, group, 0)
    if last:
        total = fold(next_ref)
        for c in range(nc):
            out_ref[c] = total
        for l in range(per_dev):
            mine_ref[l] = next_ref[own_ref[1] * per_dev + l]
    else:
        forward(dims, next_ref, lat_ref, foot_ref, ids_ref, sim_ref, out_ref)


def finish_kernel(factor, sum_ref, *refs):
    row_refs, refs = refs[:STEPS], refs[STEPS:]
    mine_ref, refs = refs[0], refs[1:]
    alphas, refs = refs[:STEPS], refs[STEPS:]
    norms, refs = refs[:STEPS - 1], refs[STEPS - 1:]
    out_ref, coef_ref = refs
    total = tree_sum(sum_ref[c] for c in range(sum_ref.shape[0]))
    norm = jnp.sqrt(jnp.sum(total, keepdims=True))
    for k in range(STEPS):
        out_ref[k] = row_refs[k][...] * factor
    out_ref[STEPS] = mine_ref[...] * (factor / norm)
    row = lax.broadcasted_iota(jnp.int32, coef_ref.shape, 0)
    col = lax.broadcasted_iota(jnp.int32, coef_ref.shape, 1)
    coefs = jnp.zeros(coef_ref.shape, F32)
    for k in range(STEPS):
        beta = norms[k][0:1, 0:1] if k < STEPS - 1 else norm
        coefs = jnp.where((row == 0) & (col == k), alphas[k][0:1, 0:1], coefs)
        coefs = jnp.where((row == 1) & (col == k), beta, coefs)
    coef_ref[...] = coefs


def permuted(size):
    return size <= 4 and size & (size - 1) == 0


def share(array, axis):
    size = lax.axis_size(axis)
    if not permuted(size):
        return [swap(jnp.broadcast_to(array[None], (size,) + array.shape), axis).reshape(-1, array.shape[1])]
    return [array] + [lax.ppermute(array, axis, [(d, d ^ s) for d in range(size)]) for s in range(1, size)]


def swap(array, axis):
    return lax.all_to_all(array, axis, split_axis=0, concat_axis=0, tiled=True)


def body(start, lat_mats, footprints, blk_sub, blk_off, counts, rinv):
    per_dev, held, lat_rows = start.shape
    nc = lax.axis_size("cell")
    no = lax.axis_size("obs")
    lon_cols = held * nc
    band = lat_rows // nc
    groups = band // CR
    nb, ob, _ = footprints.shape
    subs = counts.shape[0]
    modes = -(-held // 16) * 16
    mine = nc * nb
    periods = per_dev * no
    dims = (nc, nb, modes, groups, band)
    shape = functools.partial(jax.ShapeDtypeStruct, dtype=F32)

    high, low = lon_table(lon_cols, nc, modes)
    if modes != held:
        start = jnp.pad(start, ((0, 0), (0, modes - held), (0, 0)))
        lat_mats = jnp.pad(lat_mats, ((0, modes - held), (0, 0), (0, 0)))
    lat = lat_mats.transpose(1, 0, 2)
    at_obs = lax.axis_index("obs").astype(jnp.int32)
    own = jnp.stack([at_obs if permuted(no) else 0 * at_obs, at_obs])

    near = share(start.reshape(per_dev * modes, lat_rows), "obs")
    foot_rows = nb * CR * modes
    hats, weights = call(
        functools.partial(transform_kernel, dims),
        (jax.ShapeDtypeStruct((nc, foot_rows + 16, ob), BF16), shape((subs, ob))),
        [ANY] * 7,
        jnp.asarray(high), jnp.asarray(low), footprints, blk_off, blk_sub, counts, rinv.reshape(subs, ob),
        scratch=[
            pltpu.VMEM(high.shape, BF16),
            pltpu.VMEM(low.shape, BF16),
            pltpu.VMEM(footprints.shape, BF16),
            pltpu.SMEM((nb,), jnp.int32),
            pltpu.SMEM((nb,), jnp.int32),
            pltpu.SMEM((subs,), jnp.int32),
            pltpu.VMEM((subs, ob), F32),
            pltpu.SemaphoreType.DMA((7,)),
        ],
        limit=48,
    )
    came = swap(hats, "cell")

    field_shape = shape((periods, modes, lat_rows))
    small = shape((ROWS, 128))
    sim_scratch = pltpu.VMEM((subs + ROWS, ob), F32)
    own_shape = shape((per_dev, modes, lat_rows))
    sims, field, foot, ids = call(
        functools.partial(first_kernel, dims, no),
        (
            shape((nc, subs + ROWS, ob)),
            field_shape,
            jax.ShapeDtypeStruct((nc, foot_rows, ob), BF16),
            jax.ShapeDtypeStruct((nc, 128), jnp.int32),
        ),
        [SMEM] + [VMEM] * (2 + len(near)),
        own, lat, came, *near,
        scratch=[sim_scratch, pltpu.SMEM((nc, 128), jnp.int32), pltpu.SemaphoreType.DMA],
    )
    rows, alphas, norms = [], [], []
    vector = None
    for step in range(STEPS):
        first, last = step == 0, step == STEPS - 1
        coefs, norm = call(
            functools.partial(adjoint_kernel, dims, first),
            (shape((mine + subs + (ROWS if first else 0), 128)), small),
            [SMEM] + [VMEM] * 3,
            ids, swap(sims, "cell"), weights, foot,
            scratch=[pltpu.VMEM((subs, ob), F32)],
        )
        coefs = share(coefs, "obs")
        if first:
            every = call(
                functools.partial(every_kernel, dims, no, mine + subs),
                jax.ShapeDtypeStruct((no, 128), jnp.int32),
                [VMEM] * len(coefs),
                *coefs,
            )
        before = [] if first else [vector]
        sims, row, field, *vector, alpha = call(
            functools.partial(image_kernel, dims, no, first, last),
            (
                shape((nc, ROWS if last else subs + ROWS, 128)),
                own_shape,
                own_shape if last else field_shape,
                *([] if last else [field_shape]),
                small,
            ),
            [SMEM] * 3 + [VMEM] * (4 + len(before) + len(coefs)),
            own, ids, every, lat, foot, norm, field, *before, *coefs,
            scratch=[pltpu.VMEM(field_shape.shape, F32)] * last + [pltpu.VMEM((no, mine, 128), F32), sim_scratch],
        )
        vector = None if last else vector[0]
        rows.append(row)
        alphas.append(alpha)
        norms.append(norm)
    factor = math.sqrt(periods * lon_cols * lat_rows)
    krylov, coeffs = call(
        functools.partial(finish_kernel, factor),
        (shape((STEPS + 1, per_dev, modes, lat_rows)), shape((2, STEPS))),
        [VMEM] * (1 + STEPS + 1 + STEPS + STEPS - 1),
        swap(sims, "cell"), *rows, field, *alphas, *norms[1:],
    )
    return krylov[:, :, :held], coeffs


def solution(mesh):
    placed = (
        P("obs", "cell", None),
        P("cell", None, None),
        P(("obs", "cell"), None, None),
        P(("obs", "cell")),
        P(("obs", "cell")),
        P("obs"),
        P("obs"),
    )
    return jax.shard_map(
        body,
        mesh=mesh,
        in_specs=placed,
        out_specs=(P(None, "obs", "cell", None), P()),
        check_vma=False,
    )
```

```python
import functools
import math

import jax
import jax.numpy as jnp
import ml_dtypes
import numpy as np
from jax import lax
from jax.experimental import pallas as pl
from jax.experimental.pallas import tpu as pltpu
from jax.sharding import PartitionSpec as P

CR = 2
WAYS = 4
STEPS = 3
ROWS = 8
VMEM = pl.BlockSpec(memory_space=pltpu.VMEM)
ANY = pl.BlockSpec(memory_space=pl.ANY)
SMEM = pl.BlockSpec(memory_space=pltpu.SMEM)
F32 = jnp.float32
BF16 = jnp.bfloat16


def lon_table(order, parts, padded):
    index = np.arange(order)
    half = order // 2
    freq = np.where(index <= half, index, index - half)[:, None]
    phase = (freq * index[None, :] % order) * (2.0 * math.pi / order)
    factor = np.where((index == 0) | (index == half), math.sqrt(1.0 / order), math.sqrt(2.0 / order))
    table = np.where(index[:, None] <= half, np.cos(phase), np.sin(phase)) * factor[:, None]
    table = table.reshape(parts, order // parts, order)
    table = np.pad(table, ((0, 0), (0, padded - order // parts), (0, 0))).reshape(parts * padded, order)
    high = table.astype(np.float32).astype(ml_dtypes.bfloat16)
    low = (table - high.astype(np.float64)).astype(np.float32).astype(ml_dtypes.bfloat16)
    return high, low


def call(kernel, outs, specs, *args, scratch=(), limit=8):
    return pl.pallas_call(
        kernel,
        out_shape=outs,
        in_specs=specs,
        out_specs=jax.tree.map(lambda _: VMEM, outs),
        scratch_shapes=scratch,
        compiler_params=pltpu.CompilerParams(vmem_limit_bytes=limit * 1024 * 1024),
    )(*args)


def tree_sum(parts):
    parts = list(parts)
    while len(parts) > 1:
        parts = [sum(parts[at:at + 2][1:], parts[at]) for at in range(0, len(parts), 2)]
    return parts[0]


def transform_kernel(dims, high_any, low_any, foot_any, off_any, sub_any, count_any, rinv_any, *refs):
    nc, nb, modes, groups, band = dims
    out_ref, weight_ref, high_ref, low_ref, foot_ref, off_ref, sub_ref, count_ref, rinv_ref, sems = refs
    copies = [
        pltpu.make_async_copy(source, target, sems.at[at])
        for at, (source, target) in enumerate(
            [
                (foot_any, foot_ref),
                (high_any, high_ref),
                (low_any, low_ref),
                (off_any, off_ref),
                (sub_any, sub_ref),
                (count_any, count_ref),
                (rinv_any, rinv_ref),
            ]
        )
    ]
    for copy in copies:
        copy.start()
    for copy in copies:
        copy.wait()
    ob = foot_ref.shape[1]
    lon = high_ref.shape[1]
    contract = (((1,), (1,)), ((), ()))
    for b in range(nb):
        for r in range(CR):
            foot = foot_ref[b, :, r * lon:(r + 1) * lon]
            hat = lax.dot_general(high_ref[...], foot, contract, preferred_element_type=F32)
            hat += lax.dot_general(low_ref[...], foot, contract, preferred_element_type=F32)
            hat = hat.astype(BF16)
            at = (b * CR + r) * modes
            for c in range(nc):
                out_ref[c, at:at + modes, :] = hat[c * modes:(c + 1) * modes, :]
    lane = lax.broadcasted_iota(jnp.int32, (16, ob), 1)
    ids = jnp.zeros((16, ob), F32)
    for b in range(nb):
        ids = jnp.where(lane == b, off_ref[b].astype(F32), ids)
        ids = jnp.where(lane == nb + b, sub_ref[b].astype(F32), ids)
    ids = ids.astype(BF16)
    for c in range(nc):
        out_ref[c, nb * CR * modes:, :] = ids
    row = lax.broadcasted_iota(jnp.int32, weight_ref.shape, 0)
    limit = jnp.zeros(weight_ref.shape, jnp.int32)
    for s in range(weight_ref.shape[0]):
        limit = jnp.where(row == s, count_ref[s], limit)
    lane = lax.broadcasted_iota(jnp.int32, weight_ref.shape, 1)
    weight_ref[...] = jnp.where(lane < limit, rinv_ref[...], 0.0)


def fold(ref):
    periods, modes, _ = ref.shape
    total = jnp.zeros((ROWS, ref.shape[2]), F32)
    for p in range(periods):
        for at in range(0, modes, ROWS):
            part = ref[p, at:at + ROWS, :]
            total += part * part
    return total


def forward(dims, field_ref, lat_row, foot_ref, ids_ref, sim_ref, out_ref):
    nc, nb, modes, groups, band = dims
    subs = sim_ref.shape[0] - ROWS
    sim_ref[...] = jnp.zeros_like(sim_ref)
    for j in range(nc):
        for b in range(nb):
            off = ids_ref[j, b]
            sub = ids_ref[j, nb + b]
            period = off // groups
            row = j * band + off % groups * CR
            total = None
            for r in range(CR):
                column = jnp.sum(lat_row(row + r) * field_ref[period], axis=1, keepdims=True)
                at = (b * CR + r) * modes
                term = foot_ref[j, at:at + modes, :].astype(F32) * column
                total = term if total is None else total + term
            sim_ref[pl.ds(sub, 1), :] += jnp.sum(total, axis=0, keepdims=True)
    sim_ref[subs:, :] = fold(field_ref)
    for c in range(nc):
        out_ref[c] = sim_ref[...]


def pieces(refs, size, rows):
    found = []
    for ref in refs:
        found += [ref.at[at:at + rows] for at in range(0, ref.shape[0], rows)]
    assert len(found) == size
    return found


def first_kernel(dims, no, own_ref, lat_ref, came_ref, *refs):
    nc, nb, modes, _, _ = dims
    near_refs, refs = refs[:-7], refs[-7:]
    out_ref, field_ref, foot_ref, all_ref, sim_ref, ids_ref, sem = refs
    rows = nb * CR * modes
    for j in range(nc):
        all_ref[j:j + 1, :] = came_ref[j, rows:rows + 16, :].astype(F32)[0:1].astype(jnp.int32)
    copy = pltpu.make_async_copy(all_ref, ids_ref, sem)
    copy.start()
    for j in range(nc):
        foot_ref[j] = came_ref[j, :rows, :]
    per_dev = field_ref.shape[0] // no
    for s, near_ref in enumerate(pieces(near_refs, no, per_dev * modes)):
        for l in range(per_dev):
            field_ref[(own_ref[0] ^ s) * per_dev + l] = near_ref[l * modes:(l + 1) * modes, :]
    copy.wait()
    lat_rows = lat_ref.shape[0] // modes
    forward(
        dims, field_ref, lambda row: lat_ref[pl.ds(row, modes, stride=lat_rows), :], foot_ref, ids_ref, sim_ref, out_ref
    )


def adjoint_kernel(dims, first, ids_ref, sim_ref, weight_ref, foot_ref, out_ref, norm_ref, weighted_ref):
    nc, nb, modes, groups, band = dims
    subs = weight_ref.shape[0]
    mine = nc * nb
    total = tree_sum(sim_ref[c] for c in range(nc))
    norm = jnp.sqrt(jnp.sum(total[subs:], keepdims=True))
    norm_ref[...] = jnp.broadcast_to(norm, norm_ref.shape)
    scale = 1.0 / norm
    sim = total[:subs]
    weighted = sim * weight_ref[...]
    weighted_ref[...] = weighted
    lane = lax.broadcasted_iota(jnp.int32, (modes, 128), 1)
    parts = [jnp.zeros((modes, 128), F32) for _ in range(CR)]
    for j in range(nc):
        for b in range(nb):
            chosen = weighted_ref[pl.ds(ids_ref[j, nb + b], 1), :]
            for r in range(CR):
                at = (b * CR + r) * modes
                column = jnp.sum(foot_ref[j, at:at + modes, :].astype(F32) * chosen, axis=1, keepdims=True)
                parts[r] = jnp.where(lane == j * nb + b, column, parts[r])
    rest = 128 - CR * modes
    if rest:
        parts.append(jnp.zeros((rest, 128), F32))
    rows = jnp.concatenate(parts, axis=0).T
    out_ref[:mine, :] = rows[:mine] * scale
    out_ref[mine:mine + subs, :] = (sim * scale) * (weighted * scale)
    if first:
        lane = lax.broadcasted_iota(jnp.int32, (ROWS, 128), 1)
        tail = jnp.zeros((ROWS, 128), F32)
        for j in range(nc):
            for q in range(2 * nb):
                tail = jnp.where(lane == j * 2 * nb + q, ids_ref[j, q].astype(F32), tail)
        out_ref[mine + subs:, :] = tail


def every_kernel(dims, no, at, *refs):
    refs, out_ref = refs[:-1], refs[-1]
    rows = sum(ref.shape[0] for ref in refs) // no
    for s, ref in enumerate(pieces(refs, no, rows)):
        out_ref[s:s + 1, :] = ref[at:at + ROWS, :][0:1].astype(jnp.int32)


def image_kernel(dims, no, first, last, own_ref, ids_ref, all_ref, lat_ref, foot_ref, norm_ref, field_ref, *refs):
    nc, nb, modes, groups, band = dims
    if not first:
        prior_ref, refs = refs[0], refs[1:]
    ways = min(no, WAYS)
    kept = (6 if last else 7) + ways
    coef_refs, refs = refs[:-kept], refs[-kept:]
    sum_refs, refs = refs[-ways:], refs[:-ways]
    if last:
        out_ref, row_ref, mine_ref, alpha_ref, next_ref, held_ref = refs
    else:
        out_ref, row_ref, next_ref, vector_ref, alpha_ref, sim_ref, held_ref = refs
    mine = nc * nb
    periods = field_ref.shape[0]
    per_dev = row_ref.shape[0]
    subs = ROWS
    rows = sum(ref.shape[0] for ref in coef_refs) // no
    coef_refs = pieces(coef_refs, no, rows)
    for s in range(no):
        held_ref[s] = coef_refs[s][:mine, :]
    for sum_ref in sum_refs:
        sum_ref[...] = jnp.zeros_like(sum_ref)

    def group(at, carry):
        found = [own_ref[0] ^ (at * ways + i) for i in range(ways)]
        coefs = [held_ref[at_i].T for at_i in found]
        for j in range(nc):
            for b in range(nb):
                at_t = j * nb + b
                for at_i, coef, sum_ref in zip(found, coefs, sum_refs):
                    off = all_ref[at_i, j * 2 * nb + b]
                    period = off // groups
                    row = j * band + off % groups * CR
                    total = sum_ref[period]
                    for r in range(CR):
                        total += coef[r * modes:(r + 1) * modes, at_t:at_t + 1] * lat_ref[row + r]
                    sum_ref[period] = total
        return carry

    if no == ways:
        group(0, 0)
    else:
        lax.fori_loop(0, no // ways, group, 0)
    gain = jnp.sum(tree_sum(ref[mine:mine + subs, :] for ref in coef_refs), keepdims=True)
    alpha_ref[...] = jnp.broadcast_to(1.0 + gain, alpha_ref.shape)
    norm = norm_ref[0:1, :]
    scale = 1.0 / norm
    for p in range(periods):
        vector = field_ref[p] * scale
        if not last:
            vector_ref[p] = vector
        rest = tree_sum(sum_ref[p] for sum_ref in sum_refs) - vector * gain
        if not first:
            rest -= prior_ref[p] * norm
        next_ref[p] = rest
    for l in range(per_dev):
        row_ref[l] = field_ref[own_ref[1] * per_dev + l] * scale
    if last:
        total = fold(next_ref)
        for c in range(nc):
            out_ref[c] = total
        for l in range(per_dev):
            mine_ref[l] = next_ref[own_ref[1] * per_dev + l]
    else:
        forward(dims, next_ref, lambda row: lat_ref[row], foot_ref, ids_ref, sim_ref, out_ref)


def finish_kernel(factor, sum_ref, *refs):
    row_refs, refs = refs[:STEPS], refs[STEPS:]
    mine_ref, refs = refs[0], refs[1:]
    alphas, refs = refs[:STEPS], refs[STEPS:]
    norms, refs = refs[:STEPS - 1], refs[STEPS - 1:]
    out_ref, coef_ref = refs
    total = tree_sum(sum_ref[c] for c in range(sum_ref.shape[0]))
    norm = jnp.sqrt(jnp.sum(total, keepdims=True))
    for k in range(STEPS):
        out_ref[k] = row_refs[k][...] * factor
    out_ref[STEPS] = mine_ref[...] * (factor / norm)
    row = lax.broadcasted_iota(jnp.int32, coef_ref.shape, 0)
    col = lax.broadcasted_iota(jnp.int32, coef_ref.shape, 1)
    coefs = jnp.zeros(coef_ref.shape, F32)
    for k in range(STEPS):
        beta = norms[k][0:1, 0:1] if k < STEPS - 1 else norm
        coefs = jnp.where((row == 0) & (col == k), alphas[k][0:1, 0:1], coefs)
        coefs = jnp.where((row == 1) & (col == k), beta, coefs)
    coef_ref[...] = coefs


def permuted(size):
    return size <= 4 and size & (size - 1) == 0


def share(array, axis):
    size = lax.axis_size(axis)
    if not permuted(size):
        return [swap(jnp.broadcast_to(array[None], (size,) + array.shape), axis).reshape(-1, array.shape[1])]
    return [array] + [lax.ppermute(array, axis, [(d, d ^ s) for d in range(size)]) for s in range(1, size)]


def swap(array, axis):
    return lax.all_to_all(array, axis, split_axis=0, concat_axis=0, tiled=True)


def body(start, lat_mats, footprints, blk_sub, blk_off, counts, rinv):
    per_dev, held, lat_rows = start.shape
    nc = lax.axis_size("cell")
    no = lax.axis_size("obs")
    lon_cols = held * nc
    band = lat_rows // nc
    groups = band // CR
    nb, ob, _ = footprints.shape
    subs = counts.shape[0]
    modes = -(-held // 16) * 16
    mine = nc * nb
    periods = per_dev * no
    dims = (nc, nb, modes, groups, band)
    shape = functools.partial(jax.ShapeDtypeStruct, dtype=F32)

    high, low = lon_table(lon_cols, nc, modes)
    if modes != held:
        start = jnp.pad(start, ((0, 0), (0, modes - held), (0, 0)))
        lat_mats = jnp.pad(lat_mats, ((0, modes - held), (0, 0), (0, 0)))
    at_obs = lax.axis_index("obs").astype(jnp.int32)
    own = jnp.stack([at_obs if permuted(no) else 0 * at_obs, at_obs])

    near = share(start.reshape(per_dev * modes, lat_rows), "obs")
    foot_rows = nb * CR * modes
    hats, weights = call(
        functools.partial(transform_kernel, dims),
        (jax.ShapeDtypeStruct((nc, foot_rows + 16, ob), BF16), shape((subs, ob))),
        [ANY] * 7,
        jnp.asarray(high), jnp.asarray(low), footprints, blk_off, blk_sub, counts, rinv.reshape(subs, ob),
        scratch=[
            pltpu.VMEM(high.shape, BF16),
            pltpu.VMEM(low.shape, BF16),
            pltpu.VMEM(footprints.shape, BF16),
            pltpu.SMEM((nb,), jnp.int32),
            pltpu.SMEM((nb,), jnp.int32),
            pltpu.SMEM((subs,), jnp.int32),
            pltpu.VMEM((subs, ob), F32),
            pltpu.SemaphoreType.DMA((7,)),
        ],
        limit=60,
    )
    came = swap(hats, "cell")

    field_shape = shape((periods, modes, lat_rows))
    small = shape((ROWS, 128))
    sim_scratch = pltpu.VMEM((subs + ROWS, ob), F32)
    own_shape = shape((per_dev, modes, lat_rows))
    sims, field, foot, ids = call(
        functools.partial(first_kernel, dims, no),
        (
            shape((nc, subs + ROWS, ob)),
            field_shape,
            jax.ShapeDtypeStruct((nc, foot_rows, ob), BF16),
            jax.ShapeDtypeStruct((nc, 128), jnp.int32),
        ),
        [SMEM] + [VMEM] * (2 + len(near)),
        own, lat_mats.reshape(modes * lat_rows, lat_rows), came, *near,
        scratch=[sim_scratch, pltpu.SMEM((nc, 128), jnp.int32), pltpu.SemaphoreType.DMA],
    )
    lat_mats, sims = lax.optimization_barrier((lat_mats, sims))
    lat = lat_mats.transpose(1, 0, 2)
    ways = min(no, WAYS)
    rows, alphas, norms = [], [], []
    vector = None
    for step in range(STEPS):
        first, last = step == 0, step == STEPS - 1
        coefs, norm = call(
            functools.partial(adjoint_kernel, dims, first),
            (shape((mine + subs + (ROWS if first else 0), 128)), small),
            [SMEM] + [VMEM] * 3,
            ids, swap(sims, "cell"), weights, foot,
            scratch=[pltpu.VMEM((subs, ob), F32)],
        )
        coefs = share(coefs, "obs")
        if first:
            every = call(
                functools.partial(every_kernel, dims, no, mine + subs),
                jax.ShapeDtypeStruct((no, 128), jnp.int32),
                [VMEM] * len(coefs),
                *coefs,
            )
        before = [] if first else [vector]
        sims, row, field, *vector, alpha = call(
            functools.partial(image_kernel, dims, no, first, last),
            (
                shape((nc, ROWS if last else subs + ROWS, 128)),
                own_shape,
                own_shape if last else field_shape,
                *([] if last else [field_shape]),
                small,
            ),
            [SMEM] * 3 + [VMEM] * (4 + len(before) + len(coefs)),
            own, ids, every, lat, foot, norm, field, *before, *coefs,
            scratch=[pltpu.VMEM(field_shape.shape, F32) if last else sim_scratch]
            + [pltpu.VMEM((no, mine, 128), F32)]
            + [pltpu.VMEM(field_shape.shape, F32)] * ways,
        )
        vector = None if last else vector[0]
        rows.append(row)
        alphas.append(alpha)
        norms.append(norm)
    factor = math.sqrt(periods * lon_cols * lat_rows)
    krylov, coeffs = call(
        functools.partial(finish_kernel, factor),
        (shape((STEPS + 1, per_dev, modes, lat_rows)), shape((2, STEPS))),
        [VMEM] * (1 + STEPS + 1 + STEPS + STEPS - 1),
        swap(sims, "cell"), *rows, field, *alphas, *norms[1:],
    )
    return krylov[:, :, :held], coeffs


def solution(mesh):
    placed = (
        P("obs", "cell", None),
        P("cell", None, None),
        P(("obs", "cell"), None, None),
        P(("obs", "cell")),
        P(("obs", "cell")),
        P("obs"),
        P("obs"),
    )
    return jax.shard_map(
        body,
        mesh=mesh,
        in_specs=placed,
        out_specs=(P(None, "obs", "cell", None), P()),
        check_vma=False,
    )
```

```python
import functools
import math

import jax
import jax.numpy as jnp
import ml_dtypes
import numpy as np
from jax import lax
from jax.experimental import pallas as pl
from jax.experimental.pallas import tpu as pltpu
from jax.sharding import PartitionSpec as P

CR = 2
WAYS = 4
STEPS = 3
ROWS = 8
VMEM = pl.BlockSpec(memory_space=pltpu.VMEM)
ANY = pl.BlockSpec(memory_space=pl.ANY)
SMEM = pl.BlockSpec(memory_space=pltpu.SMEM)
F32 = jnp.float32
BF16 = jnp.bfloat16


def lon_table(order, parts, padded):
    index = np.arange(order)
    half = order // 2
    freq = np.where(index <= half, index, index - half)[:, None]
    phase = (freq * index[None, :] % order) * (2.0 * math.pi / order)
    factor = np.where((index == 0) | (index == half), math.sqrt(1.0 / order), math.sqrt(2.0 / order))
    table = np.where(index[:, None] <= half, np.cos(phase), np.sin(phase)) * factor[:, None]
    table = table.reshape(parts, order // parts, order)
    table = np.pad(table, ((0, 0), (0, padded - order // parts), (0, 0))).reshape(parts * padded, order)
    high = table.astype(np.float32).astype(ml_dtypes.bfloat16)
    low = (table - high.astype(np.float64)).astype(np.float32).astype(ml_dtypes.bfloat16)
    return high, low


def call(kernel, outs, specs, *args, scratch=(), limit=8, cost=None):
    return pl.pallas_call(
        kernel,
        out_shape=outs,
        in_specs=specs,
        out_specs=jax.tree.map(lambda _: VMEM, outs),
        scratch_shapes=scratch,
        cost_estimate=cost,
        compiler_params=pltpu.CompilerParams(vmem_limit_bytes=limit * 1024 * 1024),
    )(*args)


def tree_sum(parts):
    parts = list(parts)
    while len(parts) > 1:
        parts = [sum(parts[at:at + 2][1:], parts[at]) for at in range(0, len(parts), 2)]
    return parts[0]


def transform_kernel(dims, cell_ref, high_any, low_any, foot_any, off_any, sub_any, count_any, rinv_any, *refs):
    nc, nb, modes, groups, band = dims
    out_ref, weight_ref, high_ref, low_ref, foot_ref, off_ref, sub_ref, count_ref, rinv_ref, sems = refs
    copies = [
        pltpu.make_async_copy(source, target, sems.at[at])
        for at, (source, target) in enumerate(
            [
                (foot_any, foot_ref),
                (high_any, high_ref),
                (low_any, low_ref),
                (off_any, off_ref),
                (sub_any, sub_ref),
                (count_any, count_ref),
                (rinv_any, rinv_ref),
            ]
        )
    ]
    for copy in copies:
        copy.start()
    for copy in copies:
        copy.wait()
    ob = foot_ref.shape[1]
    lon = high_ref.shape[1]
    contract = (((1,), (1,)), ((), ()))
    for b in range(nb):
        for r in range(CR):
            foot = foot_ref[b, :, r * lon:(r + 1) * lon]
            hat = lax.dot_general(high_ref[...], foot, contract, preferred_element_type=F32)
            hat += lax.dot_general(low_ref[...], foot, contract, preferred_element_type=F32)
            hat = hat.astype(BF16)
            at = (b * CR + r) * modes
            for c in range(nc):
                out_ref[c, at:at + modes, :] = hat[c * modes:(c + 1) * modes, :]
    lane = lax.broadcasted_iota(jnp.int32, (16, ob), 1)
    ids = jnp.zeros((16, ob), F32)
    for b in range(nb):
        off = off_ref[b]
        values = (off // groups, cell_ref[0] * (band // CR) + off % groups, sub_ref[b])
        for at, value in enumerate(values):
            ids = jnp.where(lane == at * nb + b, value.astype(F32), ids)
    ids = ids.astype(BF16)
    for c in range(nc):
        out_ref[c, nb * CR * modes:, :] = ids
    row = lax.broadcasted_iota(jnp.int32, weight_ref.shape, 0)
    limit = jnp.zeros(weight_ref.shape, jnp.int32)
    for s in range(weight_ref.shape[0]):
        limit = jnp.where(row == s, count_ref[s], limit)
    lane = lax.broadcasted_iota(jnp.int32, weight_ref.shape, 1)
    weight_ref[...] = jnp.where(lane < limit, rinv_ref[...], 0.0)


def fetch_kernel(*refs):
    refs, sems = refs[:-1], refs[-1]
    half = len(refs) // 2
    copies = [pltpu.make_async_copy(refs[at], refs[half + at], sems.at[at]) for at in range(half)]
    for copy in copies:
        copy.start()
    for copy in copies:
        copy.wait()


def fold(ref):
    periods, modes, _ = ref.shape
    total = jnp.zeros((ROWS, ref.shape[2]), F32)
    for p in range(periods):
        for at in range(0, modes, ROWS):
            part = ref[p, at:at + ROWS, :]
            total += part * part
    return total


def lat_row(lat_ref, modes, row):
    return lat_ref[pl.ds(row, modes, stride=lat_ref.shape[0] // modes), :]


def forward(dims, field_ref, lat_ref, foot_ref, ids_ref, sim_ref, out_ref):
    nc, nb, modes, groups, band = dims
    subs = sim_ref.shape[0] - ROWS
    sim_ref[...] = jnp.zeros_like(sim_ref)
    for j in range(nc):
        for b in range(nb):
            period = ids_ref[j, b]
            row = ids_ref[j, nb + b] * CR
            sub = ids_ref[j, 2 * nb + b]
            total = None
            for r in range(CR):
                column = jnp.sum(lat_row(lat_ref, modes, row + r) * field_ref[period], axis=1, keepdims=True)
                at = (b * CR + r) * modes
                term = foot_ref[j, at:at + modes, :].astype(F32) * column
                total = term if total is None else total + term
            sim_ref[pl.ds(sub, 1), :] += jnp.sum(total, axis=0, keepdims=True)
    sim_ref[subs:, :] = fold(field_ref)
    for c in range(nc):
        out_ref[c] = sim_ref[...]


def pieces(refs, size, rows):
    found = []
    for ref in refs:
        found += [ref.at[at:at + rows] for at in range(0, ref.shape[0], rows)]
    assert len(found) == size
    return found


def first_kernel(dims, no, own_ref, lat_ref, came_ref, *refs):
    nc, nb, modes, _, _ = dims
    near_refs, refs = refs[:-7], refs[-7:]
    out_ref, field_ref, foot_ref, all_ref, sim_ref, ids_ref, sem = refs
    rows = nb * CR * modes
    for j in range(nc):
        all_ref[j:j + 1, :] = came_ref[j, rows:rows + 16, :].astype(F32)[0:1].astype(jnp.int32)
    copy = pltpu.make_async_copy(all_ref, ids_ref, sem)
    copy.start()
    for j in range(nc):
        foot_ref[j] = came_ref[j, :rows, :]
    per_dev = field_ref.shape[0] // no
    for s, near_ref in enumerate(pieces(near_refs, no, per_dev * modes)):
        for l in range(per_dev):
            field_ref[((own_ref[0] ^ s) if permuted(no) else s) * per_dev + l] = near_ref[l * modes:(l + 1) * modes, :]
    copy.wait()
    forward(dims, field_ref, lat_ref, foot_ref, ids_ref, sim_ref, out_ref)


def adjoint_kernel(dims, first, ids_ref, sim_ref, weight_ref, foot_ref, out_ref, norm_ref, weighted_ref):
    nc, nb, modes, groups, band = dims
    subs = weight_ref.shape[0]
    mine = nc * nb
    total = tree_sum(sim_ref[c] for c in range(nc))
    norm = jnp.sqrt(jnp.sum(total[subs:], keepdims=True))
    norm_ref[...] = jnp.broadcast_to(norm, norm_ref.shape)
    scale = 1.0 / norm
    sim = total[:subs]
    weighted = sim * weight_ref[...]
    weighted_ref[...] = weighted
    lane = lax.broadcasted_iota(jnp.int32, (modes, 128), 1)
    parts = [jnp.zeros((modes, 128), F32) for _ in range(CR)]
    for j in range(nc):
        for b in range(nb):
            chosen = weighted_ref[pl.ds(ids_ref[j, 2 * nb + b], 1), :]
            for r in range(CR):
                at = (b * CR + r) * modes
                column = jnp.sum(foot_ref[j, at:at + modes, :].astype(F32) * chosen, axis=1, keepdims=True)
                parts[r] = jnp.where(lane == j * nb + b, column, parts[r])
    rest = 128 - CR * modes
    if rest:
        parts.append(jnp.zeros((rest, 128), F32))
    rows = jnp.concatenate(parts, axis=0).T
    out_ref[:mine, :] = rows[:mine] * scale
    out_ref[mine:mine + subs, :] = (sim * scale) * (weighted * scale)
    if first:
        lane = lax.broadcasted_iota(jnp.int32, (ROWS, 128), 1)
        line = lax.broadcasted_iota(jnp.int32, (ROWS, 128), 0)
        tail = jnp.zeros((ROWS, 128), jnp.int32)
        for j in range(nc):
            for b in range(nb):
                value = jnp.where(line == 0, ids_ref[j, b], ids_ref[j, nb + b])
                tail = jnp.where(lane == j * nb + b, value, tail)
        out_ref[mine + subs:, :] = tail.astype(F32)


def every_kernel(dims, no, at, *refs):
    refs, out_ref = refs[:-1], refs[-1]
    rows = sum(ref.shape[0] for ref in refs) // no
    for s, ref in enumerate(pieces(refs, no, rows)):
        out_ref[2 * s:2 * s + 2, :] = ref[at:at + ROWS, :][0:2].astype(jnp.int32)


def image_kernel(dims, no, first, last, own_ref, ids_ref, all_ref, lat_ref, foot_ref, norm_ref, field_ref, *refs):
    nc, nb, modes, groups, band = dims
    if not first:
        prior_ref, refs = refs[0], refs[1:]
    ways = min(no, WAYS)
    kept = (6 if last else 7) + ways
    coef_refs, refs = refs[:-kept], refs[-kept:]
    sum_refs, refs = refs[-ways:], refs[:-ways]
    if last:
        out_ref, row_ref, mine_ref, alpha_ref, next_ref, held_ref = refs
    else:
        out_ref, row_ref, next_ref, vector_ref, alpha_ref, sim_ref, held_ref = refs
    mine = nc * nb
    periods = field_ref.shape[0]
    per_dev = row_ref.shape[0]
    subs = ROWS
    rows = sum(ref.shape[0] for ref in coef_refs) // no
    coef_refs = pieces(coef_refs, no, rows)
    for s in range(no):
        held_ref[s] = coef_refs[s][:mine, :]
    for sum_ref in sum_refs:
        sum_ref[...] = jnp.zeros_like(sum_ref)

    def group(at, carry):
        found = [at * ways + i for i in range(ways)]
        if permuted(no):
            found = [own_ref[0] ^ at_i for at_i in found]
        coefs = [held_ref[at_i].T for at_i in found]
        for j in range(nc):
            for b in range(nb):
                at_t = j * nb + b
                for at_i, coef, sum_ref in zip(found, coefs, sum_refs):
                    period = all_ref[2 * at_i, at_t]
                    row = all_ref[2 * at_i + 1, at_t] * CR
                    total = sum_ref[period]
                    for r in range(CR):
                        total += coef[r * modes:(r + 1) * modes, at_t:at_t + 1] * lat_row(lat_ref, modes, row + r)
                    sum_ref[period] = total
        return carry

    if no == ways:
        group(0, 0)
    else:
        lax.fori_loop(0, no // ways, group, 0)
    gain = jnp.sum(tree_sum(ref[mine:mine + subs, :] for ref in coef_refs), keepdims=True)
    alpha_ref[...] = jnp.broadcast_to(1.0 + gain, alpha_ref.shape)
    norm = norm_ref[0:1, :]
    scale = 1.0 / norm
    for p in range(periods):
        vector = field_ref[p] * scale
        if not last:
            vector_ref[p] = vector
        rest = tree_sum(sum_ref[p] for sum_ref in sum_refs) - vector * gain
        if not first:
            rest -= prior_ref[p] * norm
        next_ref[p] = rest
    for l in range(per_dev):
        row_ref[l] = field_ref[own_ref[0] * per_dev + l] * scale
    if last:
        total = fold(next_ref)
        for c in range(nc):
            out_ref[c] = total
        for l in range(per_dev):
            mine_ref[l] = next_ref[own_ref[0] * per_dev + l]
    else:
        forward(dims, next_ref, lat_ref, foot_ref, ids_ref, sim_ref, out_ref)


def finish_kernel(factor, sum_ref, *refs):
    row_refs, refs = refs[:STEPS], refs[STEPS:]
    mine_ref, refs = refs[0], refs[1:]
    alphas, refs = refs[:STEPS], refs[STEPS:]
    norms, refs = refs[:STEPS - 1], refs[STEPS - 1:]
    out_ref, coef_ref = refs
    total = tree_sum(sum_ref[c] for c in range(sum_ref.shape[0]))
    norm = jnp.sqrt(jnp.sum(total, keepdims=True))
    for k in range(STEPS):
        out_ref[k] = row_refs[k][...] * factor
    out_ref[STEPS] = mine_ref[...] * (factor / norm)
    row = lax.broadcasted_iota(jnp.int32, coef_ref.shape, 0)
    col = lax.broadcasted_iota(jnp.int32, coef_ref.shape, 1)
    coefs = jnp.zeros(coef_ref.shape, F32)
    for k in range(STEPS):
        beta = norms[k][0:1, 0:1] if k < STEPS - 1 else norm
        coefs = jnp.where((row == 0) & (col == k), alphas[k][0:1, 0:1], coefs)
        coefs = jnp.where((row == 1) & (col == k), beta, coefs)
    coef_ref[...] = coefs


def permuted(size):
    return size <= 4 and size & (size - 1) == 0


def share(array, axis):
    size = lax.axis_size(axis)
    if not permuted(size):
        return [swap(jnp.broadcast_to(array[None], (size,) + array.shape), axis).reshape(-1, array.shape[1])]
    return [array] + [lax.ppermute(array, axis, [(d, d ^ s) for d in range(size)]) for s in range(1, size)]


def swap(array, axis):
    return lax.all_to_all(array, axis, split_axis=0, concat_axis=0, tiled=True)


def body(start, lat_mats, footprints, blk_sub, blk_off, counts, rinv):
    per_dev, held, lat_rows = start.shape
    nc = lax.axis_size("cell")
    no = lax.axis_size("obs")
    lon_cols = held * nc
    band = lat_rows // nc
    groups = band // CR
    nb, ob, _ = footprints.shape
    subs = counts.shape[0]
    modes = -(-held // 16) * 16
    mine = nc * nb
    periods = per_dev * no
    dims = (nc, nb, modes, groups, band)
    shape = functools.partial(jax.ShapeDtypeStruct, dtype=F32)

    high, low = lon_table(lon_cols, nc, modes)
    if modes != held:
        start = jnp.pad(start, ((0, 0), (0, modes - held), (0, 0)))
        lat_mats = jnp.pad(lat_mats, ((0, modes - held), (0, 0), (0, 0)))
    own = lax.axis_index("obs").astype(jnp.int32).reshape(1)
    cell = lax.axis_index("cell").astype(jnp.int32).reshape(1)

    start = start.reshape(per_dev * modes, lat_rows)
    near = share(start, "obs")
    foot_rows = nb * CR * modes
    hats, weights = call(
        functools.partial(transform_kernel, dims),
        (jax.ShapeDtypeStruct((nc, foot_rows + 16, ob), BF16), shape((subs, ob))),
        [SMEM] + [ANY] * 7,
        cell, jnp.asarray(high), jnp.asarray(low), footprints, blk_off, blk_sub, counts, rinv.reshape(subs, ob),
        scratch=[
            pltpu.VMEM(high.shape, BF16),
            pltpu.VMEM(low.shape, BF16),
            pltpu.VMEM(footprints.shape, BF16),
            pltpu.SMEM((nb,), jnp.int32),
            pltpu.SMEM((nb,), jnp.int32),
            pltpu.SMEM((subs,), jnp.int32),
            pltpu.VMEM((subs, ob), F32),
            pltpu.SemaphoreType.DMA((7,)),
        ],
        limit=60,
    )
    came = swap(hats, "cell")
    lat, start, _ = lax.optimization_barrier((lat_mats.reshape(modes * lat_rows, lat_rows), start, weights))
    lat, start = call(
        fetch_kernel,
        (shape(lat.shape), shape(start.shape)),
        [ANY] * 2,
        lat, start,
        scratch=[pltpu.SemaphoreType.DMA((2,))],
        limit=50,
        cost=pl.CostEstimate(flops=0, transcendentals=0, bytes_accessed=8 * (lat.size + start.size)),
    )
    if permuted(no):
        near[0] = start

    field_shape = shape((periods, modes, lat_rows))
    small = shape((ROWS, 128))
    sim_scratch = pltpu.VMEM((subs + ROWS, ob), F32)
    own_shape = shape((per_dev, modes, lat_rows))
    sims, field, foot, ids = call(
        functools.partial(first_kernel, dims, no),
        (
            shape((nc, subs + ROWS, ob)),
            field_shape,
            jax.ShapeDtypeStruct((nc, foot_rows, ob), BF16),
            jax.ShapeDtypeStruct((nc, 128), jnp.int32),
        ),
        [SMEM] + [VMEM] * (2 + len(near)),
        own, lat, came, *near,
        scratch=[sim_scratch, pltpu.SMEM((nc, 128), jnp.int32), pltpu.SemaphoreType.DMA],
    )
    ways = min(no, WAYS)
    rows, alphas, norms = [], [], []
    vector = None
    for step in range(STEPS):
        first, last = step == 0, step == STEPS - 1
        coefs, norm = call(
            functools.partial(adjoint_kernel, dims, first),
            (shape((mine + subs + (ROWS if first else 0), 128)), small),
            [SMEM] + [VMEM] * 3,
            ids, swap(sims, "cell"), weights, foot,
            scratch=[pltpu.VMEM((subs, ob), F32)],
        )
        coefs = share(coefs, "obs")
        if first:
            every = call(
                functools.partial(every_kernel, dims, no, mine + subs),
                jax.ShapeDtypeStruct((2 * no, 128), jnp.int32),
                [VMEM] * len(coefs),
                *coefs,
            )
        before = [] if first else [vector]
        sims, row, field, *vector, alpha = call(
            functools.partial(image_kernel, dims, no, first, last),
            (
                shape((nc, ROWS if last else subs + ROWS, 128)),
                own_shape,
                own_shape if last else field_shape,
                *([] if last else [field_shape]),
                small,
            ),
            [SMEM] * 3 + [VMEM] * (4 + len(before) + len(coefs)),
            own, ids, every, lat, foot, norm, field, *before, *coefs,
            scratch=[pltpu.VMEM(field_shape.shape, F32) if last else sim_scratch]
            + [pltpu.VMEM((no, mine, 128), F32)]
            + [pltpu.VMEM(field_shape.shape, F32)] * ways,
        )
        vector = None if last else vector[0]
        rows.append(row)
        alphas.append(alpha)
        norms.append(norm)
    factor = math.sqrt(periods * lon_cols * lat_rows)
    krylov, coeffs = call(
        functools.partial(finish_kernel, factor),
        (shape((STEPS + 1, per_dev, modes, lat_rows)), shape((2, STEPS))),
        [VMEM] * (1 + STEPS + 1 + STEPS + STEPS - 1),
        swap(sims, "cell"), *rows, field, *alphas, *norms[1:],
    )
    return krylov[:, :, :held], coeffs


def solution(mesh):
    placed = (
        P("obs", "cell", None),
        P("cell", None, None),
        P(("obs", "cell"), None, None),
        P(("obs", "cell")),
        P(("obs", "cell")),
        P("obs"),
        P("obs"),
    )
    return jax.shard_map(
        body,
        mesh=mesh,
        in_specs=placed,
        out_specs=(P(None, "obs", "cell", None), P()),
        check_vma=False,
    )
```

```python
import functools
import math

import jax
import jax.numpy as jnp
import ml_dtypes
import numpy as np
from jax import lax
from jax.experimental import pallas as pl
from jax.experimental.pallas import tpu as pltpu
from jax.sharding import PartitionSpec as P

CR = 2
WAYS = 4
STEPS = 3
ROWS = 8
VMEM = pl.BlockSpec(memory_space=pltpu.VMEM)
ANY = pl.BlockSpec(memory_space=pl.ANY)
SMEM = pl.BlockSpec(memory_space=pltpu.SMEM)
F32 = jnp.float32
BF16 = jnp.bfloat16


def lon_table(order, parts, padded):
    index = np.arange(order)
    half = order // 2
    freq = np.where(index <= half, index, index - half)[:, None]
    phase = (freq * index[None, :] % order) * (2.0 * math.pi / order)
    factor = np.where((index == 0) | (index == half), math.sqrt(1.0 / order), math.sqrt(2.0 / order))
    table = np.where(index[:, None] <= half, np.cos(phase), np.sin(phase)) * factor[:, None]
    table = table.reshape(parts, order // parts, order)
    table = np.pad(table, ((0, 0), (0, padded - order // parts), (0, 0))).reshape(parts * padded, order)
    high = table.astype(np.float32).astype(ml_dtypes.bfloat16)
    low = (table - high.astype(np.float64)).astype(np.float32).astype(ml_dtypes.bfloat16)
    return high, low


def call(kernel, outs, specs, *args, scratch=(), limit=8, cost=None):
    return pl.pallas_call(
        kernel,
        out_shape=outs,
        in_specs=specs,
        out_specs=jax.tree.map(lambda _: VMEM, outs),
        scratch_shapes=scratch,
        cost_estimate=cost,
        compiler_params=pltpu.CompilerParams(vmem_limit_bytes=limit * 1024 * 1024),
    )(*args)


def tree_sum(parts):
    parts = list(parts)
    while len(parts) > 1:
        parts = [sum(parts[at:at + 2][1:], parts[at]) for at in range(0, len(parts), 2)]
    return parts[0]


def transform_kernel(dims, cell_ref, high_any, low_any, foot_any, off_any, sub_any, count_any, rinv_any, *refs):
    nc, nb, modes, groups, band = dims
    out_ref, weight_ref, high_ref, low_ref, foot_ref, off_ref, sub_ref, count_ref, rinv_ref, sems = refs
    copies = [
        pltpu.make_async_copy(source, target, sems.at[at])
        for at, (source, target) in enumerate(
            [
                (foot_any, foot_ref),
                (high_any, high_ref),
                (low_any, low_ref),
                (off_any, off_ref),
                (sub_any, sub_ref),
                (count_any, count_ref),
                (rinv_any, rinv_ref),
            ]
        )
    ]
    for copy in copies:
        copy.start()
    for copy in copies:
        copy.wait()
    ob = foot_ref.shape[1]
    lon = high_ref.shape[1]
    contract = (((1,), (1,)), ((), ()))
    for b in range(nb):
        for r in range(CR):
            foot = foot_ref[b, :, r * lon:(r + 1) * lon]
            hat = lax.dot_general(high_ref[...], foot, contract, preferred_element_type=F32)
            hat += lax.dot_general(low_ref[...], foot, contract, preferred_element_type=F32)
            hat = hat.astype(BF16)
            at = (b * CR + r) * modes
            for c in range(nc):
                out_ref[c, at:at + modes, :] = hat[c * modes:(c + 1) * modes, :]
    lane = lax.broadcasted_iota(jnp.int32, (16, ob), 1)
    ids = jnp.zeros((16, ob), F32)
    for b in range(nb):
        off = off_ref[b]
        values = (off // groups, cell_ref[0] * (band // CR) + off % groups, sub_ref[b])
        for at, value in enumerate(values):
            ids = jnp.where(lane == at * nb + b, value.astype(F32), ids)
    ids = ids.astype(BF16)
    for c in range(nc):
        out_ref[c, nb * CR * modes:, :] = ids
    row = lax.broadcasted_iota(jnp.int32, weight_ref.shape, 0)
    limit = jnp.zeros(weight_ref.shape, jnp.int32)
    for s in range(weight_ref.shape[0]):
        limit = jnp.where(row == s, count_ref[s], limit)
    lane = lax.broadcasted_iota(jnp.int32, weight_ref.shape, 1)
    weight_ref[...] = jnp.where(lane < limit, rinv_ref[...], 0.0)


def fetch_kernel(lat_any, start_any, lat_ref, start_ref, sems):
    modes = lat_any.shape[0]
    copies = [pltpu.make_async_copy(lat_any.at[m], lat_ref.at[:, m, :], sems.at[m]) for m in range(modes)]
    copies.append(pltpu.make_async_copy(start_any, start_ref, sems.at[modes]))
    for copy in copies:
        copy.start()
    for copy in copies:
        copy.wait()


def fold(ref):
    periods, modes, _ = ref.shape
    total = jnp.zeros((ROWS, ref.shape[2]), F32)
    for p in range(periods):
        for at in range(0, modes, ROWS):
            part = ref[p, at:at + ROWS, :]
            total += part * part
    return total


def forward(dims, field_ref, lat_ref, foot_ref, ids_ref, sim_ref, out_ref):
    nc, nb, modes, groups, band = dims
    subs = sim_ref.shape[0] - ROWS
    sim_ref[...] = jnp.zeros_like(sim_ref)
    for j in range(nc):
        for b in range(nb):
            period = ids_ref[j, b]
            row = ids_ref[j, nb + b] * CR
            sub = ids_ref[j, 2 * nb + b]
            total = None
            for r in range(CR):
                column = jnp.sum(lat_ref[row + r] * field_ref[period], axis=1, keepdims=True)
                at = (b * CR + r) * modes
                term = foot_ref[j, at:at + modes, :].astype(F32) * column
                total = term if total is None else total + term
            sim_ref[pl.ds(sub, 1), :] += jnp.sum(total, axis=0, keepdims=True)
    sim_ref[subs:, :] = fold(field_ref)
    for c in range(nc):
        out_ref[c] = sim_ref[...]


def pieces(refs, size, rows):
    found = []
    for ref in refs:
        found += [ref.at[at:at + rows] for at in range(0, ref.shape[0], rows)]
    assert len(found) == size
    return found


def first_kernel(dims, no, own_ref, lat_ref, came_ref, *refs):
    nc, nb, modes, _, _ = dims
    near_refs, refs = refs[:-7], refs[-7:]
    out_ref, field_ref, foot_ref, all_ref, sim_ref, ids_ref, sem = refs
    rows = nb * CR * modes
    for j in range(nc):
        all_ref[j:j + 1, :] = came_ref[j, rows:rows + 16, :].astype(F32)[0:1].astype(jnp.int32)
    copy = pltpu.make_async_copy(all_ref, ids_ref, sem)
    copy.start()
    for j in range(nc):
        foot_ref[j] = came_ref[j, :rows, :]
    per_dev = field_ref.shape[0] // no
    for s, near_ref in enumerate(pieces(near_refs, no, per_dev * modes)):
        for l in range(per_dev):
            field_ref[((own_ref[0] ^ s) if permuted(no) else s) * per_dev + l] = near_ref[l * modes:(l + 1) * modes, :]
    copy.wait()
    forward(dims, field_ref, lat_ref, foot_ref, ids_ref, sim_ref, out_ref)


def adjoint_kernel(dims, first, ids_ref, sim_ref, weight_ref, foot_ref, out_ref, norm_ref, weighted_ref):
    nc, nb, modes, groups, band = dims
    subs = weight_ref.shape[0]
    mine = nc * nb
    total = tree_sum(sim_ref[c] for c in range(nc))
    norm = jnp.sqrt(jnp.sum(total[subs:], keepdims=True))
    norm_ref[...] = jnp.broadcast_to(norm, norm_ref.shape)
    scale = 1.0 / norm
    sim = total[:subs]
    weighted = sim * weight_ref[...]
    weighted_ref[...] = weighted
    lane = lax.broadcasted_iota(jnp.int32, (modes, 128), 1)
    parts = [jnp.zeros((modes, 128), F32) for _ in range(CR)]
    for j in range(nc):
        for b in range(nb):
            chosen = weighted_ref[pl.ds(ids_ref[j, 2 * nb + b], 1), :]
            for r in range(CR):
                at = (b * CR + r) * modes
                column = jnp.sum(foot_ref[j, at:at + modes, :].astype(F32) * chosen, axis=1, keepdims=True)
                parts[r] = jnp.where(lane == j * nb + b, column, parts[r])
    rest = 128 - CR * modes
    if rest:
        parts.append(jnp.zeros((rest, 128), F32))
    rows = jnp.concatenate(parts, axis=0).T
    out_ref[:mine, :] = rows[:mine] * scale
    out_ref[mine:mine + subs, :] = (sim * scale) * (weighted * scale)
    if first:
        lane = lax.broadcasted_iota(jnp.int32, (ROWS, 128), 1)
        line = lax.broadcasted_iota(jnp.int32, (ROWS, 128), 0)
        tail = jnp.zeros((ROWS, 128), jnp.int32)
        for j in range(nc):
            for b in range(nb):
                value = jnp.where(line == 0, ids_ref[j, b], ids_ref[j, nb + b])
                tail = jnp.where(lane == j * nb + b, value, tail)
        out_ref[mine + subs:, :] = tail.astype(F32)


def every_kernel(dims, no, at, *refs):
    refs, out_ref = refs[:-1], refs[-1]
    rows = sum(ref.shape[0] for ref in refs) // no
    for s, ref in enumerate(pieces(refs, no, rows)):
        out_ref[2 * s:2 * s + 2, :] = ref[at:at + ROWS, :][0:2].astype(jnp.int32)


def image_kernel(dims, no, first, last, own_ref, ids_ref, all_ref, lat_ref, foot_ref, norm_ref, field_ref, *refs):
    nc, nb, modes, groups, band = dims
    if not first:
        prior_ref, refs = refs[0], refs[1:]
    ways = min(no, WAYS)
    kept = (6 if last else 7) + ways
    coef_refs, refs = refs[:-kept], refs[-kept:]
    sum_refs, refs = refs[-ways:], refs[:-ways]
    if last:
        out_ref, row_ref, mine_ref, alpha_ref, next_ref, held_ref = refs
    else:
        out_ref, row_ref, next_ref, vector_ref, alpha_ref, sim_ref, held_ref = refs
    mine = nc * nb
    periods = field_ref.shape[0]
    per_dev = row_ref.shape[0]
    subs = ROWS
    rows = sum(ref.shape[0] for ref in coef_refs) // no
    coef_refs = pieces(coef_refs, no, rows)
    for s in range(no):
        held_ref[s] = coef_refs[s][:mine, :]
    for sum_ref in sum_refs:
        sum_ref[...] = jnp.zeros_like(sum_ref)

    def group(at, carry):
        found = [at * ways + i for i in range(ways)]
        if permuted(no):
            found = [own_ref[0] ^ at_i for at_i in found]
        coefs = [held_ref[at_i].T for at_i in found]
        for j in range(nc):
            for b in range(nb):
                at_t = j * nb + b
                for at_i, coef, sum_ref in zip(found, coefs, sum_refs):
                    period = all_ref[2 * at_i, at_t]
                    row = all_ref[2 * at_i + 1, at_t] * CR
                    total = sum_ref[period]
                    for r in range(CR):
                        total += coef[r * modes:(r + 1) * modes, at_t:at_t + 1] * lat_ref[row + r]
                    sum_ref[period] = total
        return carry

    if no == ways:
        group(0, 0)
    else:
        lax.fori_loop(0, no // ways, group, 0)
    gain = jnp.sum(tree_sum(ref[mine:mine + subs, :] for ref in coef_refs), keepdims=True)
    alpha_ref[...] = jnp.broadcast_to(1.0 + gain, alpha_ref.shape)
    norm = norm_ref[0:1, :]
    scale = 1.0 / norm
    for p in range(periods):
        vector = field_ref[p] * scale
        if not last:
            vector_ref[p] = vector
        rest = tree_sum(sum_ref[p] for sum_ref in sum_refs) - vector * gain
        if not first:
            rest -= prior_ref[p] * norm
        next_ref[p] = rest
    for l in range(per_dev):
        row_ref[l] = field_ref[own_ref[0] * per_dev + l] * scale
    if last:
        total = fold(next_ref)
        for c in range(nc):
            out_ref[c] = total
        for l in range(per_dev):
            mine_ref[l] = next_ref[own_ref[0] * per_dev + l]
    else:
        forward(dims, next_ref, lat_ref, foot_ref, ids_ref, sim_ref, out_ref)


def finish_kernel(factor, sum_ref, *refs):
    row_refs, refs = refs[:STEPS], refs[STEPS:]
    mine_ref, refs = refs[0], refs[1:]
    alphas, refs = refs[:STEPS], refs[STEPS:]
    norms, refs = refs[:STEPS - 1], refs[STEPS - 1:]
    out_ref, coef_ref = refs
    total = tree_sum(sum_ref[c] for c in range(sum_ref.shape[0]))
    norm = jnp.sqrt(jnp.sum(total, keepdims=True))
    for k in range(STEPS):
        out_ref[k] = row_refs[k][...] * factor
    out_ref[STEPS] = mine_ref[...] * (factor / norm)
    row = lax.broadcasted_iota(jnp.int32, coef_ref.shape, 0)
    col = lax.broadcasted_iota(jnp.int32, coef_ref.shape, 1)
    coefs = jnp.zeros(coef_ref.shape, F32)
    for k in range(STEPS):
        beta = norms[k][0:1, 0:1] if k < STEPS - 1 else norm
        coefs = jnp.where((row == 0) & (col == k), alphas[k][0:1, 0:1], coefs)
        coefs = jnp.where((row == 1) & (col == k), beta, coefs)
    coef_ref[...] = coefs


def permuted(size):
    return size <= 4 and size & (size - 1) == 0


def share(array, axis):
    size = lax.axis_size(axis)
    if not permuted(size):
        return [swap(jnp.broadcast_to(array[None], (size,) + array.shape), axis).reshape(-1, array.shape[1])]
    return [array] + [lax.ppermute(array, axis, [(d, d ^ s) for d in range(size)]) for s in range(1, size)]


def swap(array, axis):
    return lax.all_to_all(array, axis, split_axis=0, concat_axis=0, tiled=True)


def body(start, lat_mats, footprints, blk_sub, blk_off, counts, rinv):
    per_dev, held, lat_rows = start.shape
    nc = lax.axis_size("cell")
    no = lax.axis_size("obs")
    lon_cols = held * nc
    band = lat_rows // nc
    groups = band // CR
    nb, ob, _ = footprints.shape
    subs = counts.shape[0]
    modes = -(-held // 16) * 16
    mine = nc * nb
    periods = per_dev * no
    dims = (nc, nb, modes, groups, band)
    shape = functools.partial(jax.ShapeDtypeStruct, dtype=F32)

    high, low = lon_table(lon_cols, nc, modes)
    if modes != held:
        start = jnp.pad(start, ((0, 0), (0, modes - held), (0, 0)))
        lat_mats = jnp.pad(lat_mats, ((0, modes - held), (0, 0), (0, 0)))
    own = lax.axis_index("obs").astype(jnp.int32).reshape(1)
    cell = lax.axis_index("cell").astype(jnp.int32).reshape(1)

    start = start.reshape(per_dev * modes, lat_rows)
    near = share(start, "obs")
    foot_rows = nb * CR * modes
    hats, weights = call(
        functools.partial(transform_kernel, dims),
        (jax.ShapeDtypeStruct((nc, foot_rows + 16, ob), BF16), shape((subs, ob))),
        [SMEM] + [ANY] * 7,
        cell, jnp.asarray(high), jnp.asarray(low), footprints, blk_off, blk_sub, counts, rinv.reshape(subs, ob),
        scratch=[
            pltpu.VMEM(high.shape, BF16),
            pltpu.VMEM(low.shape, BF16),
            pltpu.VMEM(footprints.shape, BF16),
            pltpu.SMEM((nb,), jnp.int32),
            pltpu.SMEM((nb,), jnp.int32),
            pltpu.SMEM((subs,), jnp.int32),
            pltpu.VMEM((subs, ob), F32),
            pltpu.SemaphoreType.DMA((7,)),
        ],
        limit=60,
    )
    came = swap(hats, "cell")
    lat, start, _ = lax.optimization_barrier((lat_mats, start, weights))
    lat, start = call(
        fetch_kernel,
        (shape((lat_rows, modes, lat_rows)), shape(start.shape)),
        [ANY] * 2,
        lat, start,
        scratch=[pltpu.SemaphoreType.DMA((modes + 1,))],
        limit=50,
        cost=pl.CostEstimate(flops=0, transcendentals=0, bytes_accessed=8 * (lat.size + start.size)),
    )
    if permuted(no):
        near[0] = start

    field_shape = shape((periods, modes, lat_rows))
    small = shape((ROWS, 128))
    sim_scratch = pltpu.VMEM((subs + ROWS, ob), F32)
    own_shape = shape((per_dev, modes, lat_rows))
    sims, field, foot, ids = call(
        functools.partial(first_kernel, dims, no),
        (
            shape((nc, subs + ROWS, ob)),
            field_shape,
            jax.ShapeDtypeStruct((nc, foot_rows, ob), BF16),
            jax.ShapeDtypeStruct((nc, 128), jnp.int32),
        ),
        [SMEM] + [VMEM] * (2 + len(near)),
        own, lat, came, *near,
        scratch=[sim_scratch, pltpu.SMEM((nc, 128), jnp.int32), pltpu.SemaphoreType.DMA],
    )
    ways = min(no, WAYS)
    rows, alphas, norms = [], [], []
    vector = None
    for step in range(STEPS):
        first, last = step == 0, step == STEPS - 1
        coefs, norm = call(
            functools.partial(adjoint_kernel, dims, first),
            (shape((mine + subs + (ROWS if first else 0), 128)), small),
            [SMEM] + [VMEM] * 3,
            ids, swap(sims, "cell"), weights, foot,
            scratch=[pltpu.VMEM((subs, ob), F32)],
        )
        coefs = share(coefs, "obs")
        if first:
            every = call(
                functools.partial(every_kernel, dims, no, mine + subs),
                jax.ShapeDtypeStruct((2 * no, 128), jnp.int32),
                [VMEM] * len(coefs),
                *coefs,
            )
        before = [] if first else [vector]
        sims, row, field, *vector, alpha = call(
            functools.partial(image_kernel, dims, no, first, last),
            (
                shape((nc, ROWS if last else subs + ROWS, 128)),
                own_shape,
                own_shape if last else field_shape,
                *([] if last else [field_shape]),
                small,
            ),
            [SMEM] * 3 + [VMEM] * (4 + len(before) + len(coefs)),
            own, ids, every, lat, foot, norm, field, *before, *coefs,
            scratch=[pltpu.VMEM(field_shape.shape, F32) if last else sim_scratch]
            + [pltpu.VMEM((no, mine, 128), F32)]
            + [pltpu.VMEM(field_shape.shape, F32)] * ways,
        )
        vector = None if last else vector[0]
        rows.append(row)
        alphas.append(alpha)
        norms.append(norm)
    factor = math.sqrt(periods * lon_cols * lat_rows)
    krylov, coeffs = call(
        functools.partial(finish_kernel, factor),
        (shape((STEPS + 1, per_dev, modes, lat_rows)), shape((2, STEPS))),
        [VMEM] * (1 + STEPS + 1 + STEPS + STEPS - 1),
        swap(sims, "cell"), *rows, field, *alphas, *norms[1:],
    )
    return krylov[:, :, :held], coeffs


def solution(mesh):
    placed = (
        P("obs", "cell", None),
        P("cell", None, None),
        P(("obs", "cell"), None, None),
        P(("obs", "cell")),
        P(("obs", "cell")),
        P("obs"),
        P("obs"),
    )
    return jax.shard_map(
        body,
        mesh=mesh,
        in_specs=placed,
        out_specs=(P(None, "obs", "cell", None), P()),
        check_vma=False,
    )
```

```python
import functools
import math

import jax
import jax.numpy as jnp
import ml_dtypes
import numpy as np
from jax import lax
from jax.experimental import pallas as pl
from jax.experimental.pallas import tpu as pltpu
from jax.sharding import PartitionSpec as P

CR = 2
WAYS = 4
CHUNK = 16
TERMS = 3
STEPS = 3
ROWS = 8
VMEM = pl.BlockSpec(memory_space=pltpu.VMEM)
ANY = pl.BlockSpec(memory_space=pl.ANY)
SMEM = pl.BlockSpec(memory_space=pltpu.SMEM)
F32 = jnp.float32
BF16 = jnp.bfloat16


def lon_table(order, parts, padded):
    index = np.arange(order)
    half = order // 2
    freq = np.where(index <= half, index, index - half)[:, None]
    phase = (freq * index[None, :] % order) * (2.0 * math.pi / order)
    factor = np.where((index == 0) | (index == half), math.sqrt(1.0 / order), math.sqrt(2.0 / order))
    table = np.where(index[:, None] <= half, np.cos(phase), np.sin(phase)) * factor[:, None]
    table = table.reshape(parts, order // parts, order)
    table = np.pad(table, ((0, 0), (0, padded - order // parts), (0, 0))).reshape(parts * padded, order)
    high = table.astype(np.float32).astype(ml_dtypes.bfloat16)
    low = (table - high.astype(np.float64)).astype(np.float32).astype(ml_dtypes.bfloat16)
    return high, low


def call(kernel, outs, specs, *args, scratch=(), limit=8, cost=None):
    return pl.pallas_call(
        kernel,
        out_shape=outs,
        in_specs=specs,
        out_specs=jax.tree.map(lambda _: VMEM, outs),
        scratch_shapes=scratch,
        cost_estimate=cost,
        compiler_params=pltpu.CompilerParams(vmem_limit_bytes=limit * 1024 * 1024),
    )(*args)


def tree_sum(parts):
    parts = list(parts)
    while len(parts) > 1:
        parts = [sum(parts[at:at + 2][1:], parts[at]) for at in range(0, len(parts), 2)]
    return parts[0]


def transform_kernel(dims, cell_ref, high_any, low_any, foot_any, off_any, sub_any, count_any, rinv_any, *refs):
    nc, nb, modes, groups, band = dims
    out_ref, weight_ref, high_ref, low_ref, foot_ref, off_ref, sub_ref, count_ref, rinv_ref, sems = refs
    copies = [
        pltpu.make_async_copy(source, target, sems.at[at])
        for at, (source, target) in enumerate(
            [
                (foot_any, foot_ref),
                (high_any, high_ref),
                (low_any, low_ref),
                (off_any, off_ref),
                (sub_any, sub_ref),
                (count_any, count_ref),
                (rinv_any, rinv_ref),
            ]
        )
    ]
    for copy in copies:
        copy.start()
    for copy in copies:
        copy.wait()
    ob = foot_ref.shape[1]
    lon = high_ref.shape[1]
    contract = (((1,), (1,)), ((), ()))
    for r in range(CR):
        foot = foot_ref[:, :, r * lon:(r + 1) * lon].reshape(nb * ob, lon)
        hat = lax.dot_general(high_ref[...], foot, contract, preferred_element_type=F32)
        hat += lax.dot_general(low_ref[...], foot, contract, preferred_element_type=F32)
        hat = hat.astype(BF16)
        for b in range(nb):
            at = (b * CR + r) * modes
            for c in range(nc):
                out_ref[c, at:at + modes, :] = hat[c * modes:(c + 1) * modes, b * ob:(b + 1) * ob]
    lane = lax.broadcasted_iota(jnp.int32, (16, ob), 1)
    ids = jnp.zeros((16, ob), F32)
    for b in range(nb):
        off = off_ref[b]
        values = (off // groups, cell_ref[0] * (band // CR) + off % groups, sub_ref[b])
        for at, value in enumerate(values):
            ids = jnp.where(lane == at * nb + b, value.astype(F32), ids)
    ids = ids.astype(BF16)
    for c in range(nc):
        out_ref[c, nb * CR * modes:, :] = ids
    row = lax.broadcasted_iota(jnp.int32, weight_ref.shape, 0)
    limit = jnp.zeros(weight_ref.shape, jnp.int32)
    for s in range(weight_ref.shape[0]):
        limit = jnp.where(row == s, count_ref[s], limit)
    lane = lax.broadcasted_iota(jnp.int32, weight_ref.shape, 1)
    weight_ref[...] = jnp.where(lane < limit, rinv_ref[...], 0.0)


def fetch_kernel(lat_any, start_any, lat_ref, start_ref, sems):
    modes = lat_any.shape[0]
    copies = [pltpu.make_async_copy(lat_any.at[m], lat_ref.at[:, m, :], sems.at[m]) for m in range(modes)]
    copies.append(pltpu.make_async_copy(start_any, start_ref, sems.at[modes]))
    for copy in copies:
        copy.start()
    for copy in copies:
        copy.wait()


def fold(ref):
    periods, modes, _ = ref.shape
    total = jnp.zeros((ROWS, ref.shape[2]), F32)
    for p in range(periods):
        for at in range(0, modes, ROWS):
            part = ref[p, at:at + ROWS, :]
            total += part * part
    return total


def forward(dims, field_ref, lat_ref, foot_ref, ids_ref, sim_ref, out_ref):
    nc, nb, modes, groups, band = dims
    subs = sim_ref.shape[0] - ROWS
    sim_ref[...] = jnp.zeros_like(sim_ref)
    for j in range(nc):
        for b in range(nb):
            period = ids_ref[j, b]
            row = ids_ref[j, nb + b] * CR
            sub = ids_ref[j, 2 * nb + b]
            total = None
            for r in range(CR):
                column = jnp.sum(lat_ref[row + r] * field_ref[period], axis=1, keepdims=True)
                at = (b * CR + r) * modes
                term = foot_ref[j, at:at + modes, :].astype(F32) * column
                total = term if total is None else total + term
            sim_ref[pl.ds(sub, 1), :] += jnp.sum(total, axis=0, keepdims=True)
    sim_ref[subs:, :] = fold(field_ref)
    for c in range(nc):
        out_ref[c] = sim_ref[...]


def pieces(refs, size, rows):
    found = []
    for ref in refs:
        found += [ref.at[at:at + rows] for at in range(0, ref.shape[0], rows)]
    assert len(found) == size
    return found


def first_kernel(dims, no, own_ref, lat_ref, came_ref, *refs):
    nc, nb, modes, _, _ = dims
    near_refs, refs = refs[:-7], refs[-7:]
    out_ref, field_ref, foot_ref, all_ref, sim_ref, ids_ref, sem = refs
    rows = nb * CR * modes
    for j in range(nc):
        all_ref[j:j + 1, :] = came_ref[j, rows:rows + 16, :].astype(F32)[0:1].astype(jnp.int32)
    copy = pltpu.make_async_copy(all_ref, ids_ref, sem)
    copy.start()
    for j in range(nc):
        foot_ref[j] = came_ref[j, :rows, :]
    per_dev = field_ref.shape[0] // no
    for s, near_ref in enumerate(pieces(near_refs, no, per_dev * modes)):
        for l in range(per_dev):
            field_ref[((own_ref[0] ^ s) if permuted(no) else s) * per_dev + l] = near_ref[l * modes:(l + 1) * modes, :]
    copy.wait()
    forward(dims, field_ref, lat_ref, foot_ref, ids_ref, sim_ref, out_ref)


def adjoint_kernel(dims, first, ids_ref, sim_ref, weight_ref, foot_ref, out_ref, norm_ref, weighted_ref):
    nc, nb, modes, groups, band = dims
    subs = weight_ref.shape[0]
    mine = nc * nb
    total = tree_sum(sim_ref[c] for c in range(nc))
    norm = jnp.sqrt(jnp.sum(total[subs:], keepdims=True))
    norm_ref[...] = jnp.broadcast_to(norm, norm_ref.shape)
    scale = 1.0 / norm
    sim = total[:subs]
    weighted = sim * weight_ref[...]
    weighted_ref[...] = weighted
    lane = lax.broadcasted_iota(jnp.int32, (modes, 128), 1)
    parts = [jnp.zeros((modes, 128), F32) for _ in range(CR)]
    for j in range(nc):
        for b in range(nb):
            chosen = weighted_ref[pl.ds(ids_ref[j, 2 * nb + b], 1), :]
            for r in range(CR):
                at = (b * CR + r) * modes
                column = jnp.sum(foot_ref[j, at:at + modes, :].astype(F32) * chosen, axis=1, keepdims=True)
                parts[r] = jnp.where(lane == j * nb + b, column, parts[r])
    rest = 128 - CR * modes
    if rest:
        parts.append(jnp.zeros((rest, 128), F32))
    rows = jnp.concatenate(parts, axis=0).T
    out_ref[:mine, :] = rows[:mine] * scale
    out_ref[mine:mine + subs, :] = (sim * scale) * (weighted * scale)
    if first:
        lane = lax.broadcasted_iota(jnp.int32, (ROWS, 128), 1)
        line = lax.broadcasted_iota(jnp.int32, (ROWS, 128), 0)
        tail = jnp.zeros((ROWS, 128), jnp.int32)
        for j in range(nc):
            for b in range(nb):
                value = jnp.where(line == 0, ids_ref[j, b], ids_ref[j, nb + b])
                tail = jnp.where(lane == j * nb + b, value, tail)
        out_ref[mine + subs:, :] = tail.astype(F32)


def every_kernel(dims, no, at, *refs):
    refs, out_ref = refs[:-1], refs[-1]
    rows = sum(ref.shape[0] for ref in refs) // no
    for s, ref in enumerate(pieces(refs, no, rows)):
        out_ref[2 * s:2 * s + 2, :] = ref[at:at + ROWS, :][0:2].astype(jnp.int32)


def split(values):
    terms = []
    for _ in range(TERMS):
        terms.append(values.astype(BF16))
        values = values - terms[-1].astype(F32)
    return jnp.concatenate(terms, axis=0)


def image_kernel(dims, no, first, last, own_ref, ids_ref, all_ref, lat_ref, foot_ref, norm_ref, field_ref, *refs):
    nc, nb, modes, groups, band = dims
    if not first:
        prior_ref, refs = refs[0], refs[1:]
    ways = min(no, WAYS)
    kept = (6 if last else 7) + 2 * ways
    coef_refs, refs = refs[:-kept], refs[-kept:]
    wide_refs, refs = refs[-ways:], refs[:-ways]
    sum_refs, refs = refs[-ways:], refs[:-ways]
    if last:
        out_ref, row_ref, mine_ref, alpha_ref, next_ref, held_ref = refs
    else:
        out_ref, row_ref, next_ref, vector_ref, alpha_ref, sim_ref, held_ref = refs
    mine = nc * nb
    periods = field_ref.shape[0]
    per_dev = row_ref.shape[0]
    subs = ROWS
    rows = sum(ref.shape[0] for ref in coef_refs) // no
    coef_refs = pieces(coef_refs, no, rows)
    for s in range(no):
        held_ref[s] = coef_refs[s][:mine, :]
    for sum_ref in sum_refs:
        sum_ref[...] = jnp.zeros_like(sum_ref)

    line = lax.broadcasted_iota(jnp.int32, (TERMS * CHUNK, CHUNK * 128), 0)
    lane = lax.broadcasted_iota(jnp.int32, (TERMS * CHUNK, CHUNK * 128), 1)
    pick = jnp.where(line % CHUNK == lane // 128, 1.0, 0.0).astype(BF16)

    def group(at, carry):
        found = [at * ways + i for i in range(ways)]
        if permuted(no):
            found = [own_ref[0] ^ at_i for at_i in found]
        for chunk in range(0, mine, CHUNK):
            for at_i, wide_ref in zip(found, wide_refs):
                left = split(held_ref[at_i, chunk:chunk + CHUNK, :])
                wide = lax.dot_general(left, pick, (((0,), (0,)), ((), ())), preferred_element_type=F32)
                wide_ref[...] = wide[:CR * modes]
            for at in range(CHUNK):
                for at_i, wide_ref, sum_ref in zip(found, wide_refs, sum_refs):
                    period = all_ref[2 * at_i, chunk + at]
                    row = all_ref[2 * at_i + 1, chunk + at] * CR
                    total = sum_ref[period]
                    for r in range(CR):
                        coef = wide_ref[r * modes:(r + 1) * modes, at * 128:(at + 1) * 128]
                        total += coef * lat_ref[row + r]
                    sum_ref[period] = total
        return carry

    if no == ways:
        group(0, 0)
    else:
        lax.fori_loop(0, no // ways, group, 0)
    gain = jnp.sum(tree_sum(ref[mine:mine + subs, :] for ref in coef_refs), keepdims=True)
    alpha_ref[...] = jnp.broadcast_to(1.0 + gain, alpha_ref.shape)
    norm = norm_ref[0:1, :]
    scale = 1.0 / norm
    for p in range(periods):
        vector = field_ref[p] * scale
        if not last:
            vector_ref[p] = vector
        rest = tree_sum(sum_ref[p] for sum_ref in sum_refs) - vector * gain
        if not first:
            rest -= prior_ref[p] * norm
        next_ref[p] = rest
    for l in range(per_dev):
        row_ref[l] = field_ref[own_ref[0] * per_dev + l] * scale
    if last:
        total = fold(next_ref)
        for c in range(nc):
            out_ref[c] = total
        for l in range(per_dev):
            mine_ref[l] = next_ref[own_ref[0] * per_dev + l]
    else:
        forward(dims, next_ref, lat_ref, foot_ref, ids_ref, sim_ref, out_ref)


def finish_kernel(factor, sum_ref, *refs):
    row_refs, refs = refs[:STEPS], refs[STEPS:]
    mine_ref, refs = refs[0], refs[1:]
    alphas, refs = refs[:STEPS], refs[STEPS:]
    norms, refs = refs[:STEPS - 1], refs[STEPS - 1:]
    out_ref, coef_ref = refs
    total = tree_sum(sum_ref[c] for c in range(sum_ref.shape[0]))
    norm = jnp.sqrt(jnp.sum(total, keepdims=True))
    for k in range(STEPS):
        out_ref[k] = row_refs[k][...] * factor
    out_ref[STEPS] = mine_ref[...] * (factor / norm)
    row = lax.broadcasted_iota(jnp.int32, coef_ref.shape, 0)
    col = lax.broadcasted_iota(jnp.int32, coef_ref.shape, 1)
    coefs = jnp.zeros(coef_ref.shape, F32)
    for k in range(STEPS):
        beta = norms[k][0:1, 0:1] if k < STEPS - 1 else norm
        coefs = jnp.where((row == 0) & (col == k), alphas[k][0:1, 0:1], coefs)
        coefs = jnp.where((row == 1) & (col == k), beta, coefs)
    coef_ref[...] = coefs


def permuted(size):
    return size <= 4 and size & (size - 1) == 0


def share(array, axis):
    size = lax.axis_size(axis)
    if not permuted(size):
        return [swap(jnp.broadcast_to(array[None], (size,) + array.shape), axis).reshape(-1, array.shape[1])]
    return [array] + [lax.ppermute(array, axis, [(d, d ^ s) for d in range(size)]) for s in range(1, size)]


def swap(array, axis):
    return lax.all_to_all(array, axis, split_axis=0, concat_axis=0, tiled=True)


def body(start, lat_mats, footprints, blk_sub, blk_off, counts, rinv):
    per_dev, held, lat_rows = start.shape
    nc = lax.axis_size("cell")
    no = lax.axis_size("obs")
    lon_cols = held * nc
    band = lat_rows // nc
    groups = band // CR
    nb, ob, _ = footprints.shape
    subs = counts.shape[0]
    modes = -(-held // 16) * 16
    mine = nc * nb
    periods = per_dev * no
    dims = (nc, nb, modes, groups, band)
    shape = functools.partial(jax.ShapeDtypeStruct, dtype=F32)

    high, low = lon_table(lon_cols, nc, modes)
    if modes != held:
        start = jnp.pad(start, ((0, 0), (0, modes - held), (0, 0)))
        lat_mats = jnp.pad(lat_mats, ((0, modes - held), (0, 0), (0, 0)))
    own = lax.axis_index("obs").astype(jnp.int32).reshape(1)
    cell = lax.axis_index("cell").astype(jnp.int32).reshape(1)

    start = start.reshape(per_dev * modes, lat_rows)
    near = share(start, "obs")
    foot_rows = nb * CR * modes
    hats, weights = call(
        functools.partial(transform_kernel, dims),
        (jax.ShapeDtypeStruct((nc, foot_rows + 16, ob), BF16), shape((subs, ob))),
        [SMEM] + [ANY] * 7,
        cell, jnp.asarray(high), jnp.asarray(low), footprints, blk_off, blk_sub, counts, rinv.reshape(subs, ob),
        scratch=[
            pltpu.VMEM(high.shape, BF16),
            pltpu.VMEM(low.shape, BF16),
            pltpu.VMEM(footprints.shape, BF16),
            pltpu.SMEM((nb,), jnp.int32),
            pltpu.SMEM((nb,), jnp.int32),
            pltpu.SMEM((subs,), jnp.int32),
            pltpu.VMEM((subs, ob), F32),
            pltpu.SemaphoreType.DMA((7,)),
        ],
        limit=60,
    )
    came = swap(hats, "cell")
    lat, start, _ = lax.optimization_barrier((lat_mats, start, weights))
    lat, start = call(
        fetch_kernel,
        (shape((lat_rows, modes, lat_rows)), shape(start.shape)),
        [ANY] * 2,
        lat, start,
        scratch=[pltpu.SemaphoreType.DMA((modes + 1,))],
        limit=50,
        cost=pl.CostEstimate(flops=0, transcendentals=0, bytes_accessed=8 * (lat.size + start.size)),
    )
    if permuted(no):
        near[0] = start

    field_shape = shape((periods, modes, lat_rows))
    small = shape((ROWS, 128))
    sim_scratch = pltpu.VMEM((subs + ROWS, ob), F32)
    own_shape = shape((per_dev, modes, lat_rows))
    sims, field, foot, ids = call(
        functools.partial(first_kernel, dims, no),
        (
            shape((nc, subs + ROWS, ob)),
            field_shape,
            jax.ShapeDtypeStruct((nc, foot_rows, ob), BF16),
            jax.ShapeDtypeStruct((nc, 128), jnp.int32),
        ),
        [SMEM] + [VMEM] * (2 + len(near)),
        own, lat, came, *near,
        scratch=[sim_scratch, pltpu.SMEM((nc, 128), jnp.int32), pltpu.SemaphoreType.DMA],
    )
    ways = min(no, WAYS)
    rows, alphas, norms = [], [], []
    vector = None
    for step in range(STEPS):
        first, last = step == 0, step == STEPS - 1
        coefs, norm = call(
            functools.partial(adjoint_kernel, dims, first),
            (shape((mine + subs + (ROWS if first else 0), 128)), small),
            [SMEM] + [VMEM] * 3,
            ids, swap(sims, "cell"), weights, foot,
            scratch=[pltpu.VMEM((subs, ob), F32)],
        )
        coefs = share(coefs, "obs")
        if first:
            every = call(
                functools.partial(every_kernel, dims, no, mine + subs),
                jax.ShapeDtypeStruct((2 * no, 128), jnp.int32),
                [VMEM] * len(coefs),
                *coefs,
            )
        before = [] if first else [vector]
        sims, row, field, *vector, alpha = call(
            functools.partial(image_kernel, dims, no, first, last),
            (
                shape((nc, ROWS if last else subs + ROWS, 128)),
                own_shape,
                own_shape if last else field_shape,
                *([] if last else [field_shape]),
                small,
            ),
            [SMEM] * 3 + [VMEM] * (4 + len(before) + len(coefs)),
            own, ids, every, lat, foot, norm, field, *before, *coefs,
            scratch=[pltpu.VMEM(field_shape.shape, F32) if last else sim_scratch]
            + [pltpu.VMEM((no, mine, 128), F32)]
            + [pltpu.VMEM(field_shape.shape, F32)] * ways
            + [pltpu.VMEM((CR * modes, CHUNK * 128), F32)] * ways,
            limit=16,
        )
        vector = None if last else vector[0]
        rows.append(row)
        alphas.append(alpha)
        norms.append(norm)
    factor = math.sqrt(periods * lon_cols * lat_rows)
    krylov, coeffs = call(
        functools.partial(finish_kernel, factor),
        (shape((STEPS + 1, per_dev, modes, lat_rows)), shape((2, STEPS))),
        [VMEM] * (1 + STEPS + 1 + STEPS + STEPS - 1),
        swap(sims, "cell"), *rows, field, *alphas, *norms[1:],
    )
    return krylov[:, :, :held], coeffs


def solution(mesh):
    placed = (
        P("obs", "cell", None),
        P("cell", None, None),
        P(("obs", "cell"), None, None),
        P(("obs", "cell")),
        P(("obs", "cell")),
        P("obs"),
        P("obs"),
    )
    return jax.shard_map(
        body,
        mesh=mesh,
        in_specs=placed,
        out_specs=(P(None, "obs", "cell", None), P()),
        check_vma=False,
    )
```

```python
import functools
import math

import jax
import jax.numpy as jnp
import ml_dtypes
import numpy as np
from jax import lax
from jax.experimental import pallas as pl
from jax.experimental.pallas import tpu as pltpu
from jax.sharding import PartitionSpec as P

CR = 2
WAYS = 4
CHUNK = 16
TERMS = 3
STEPS = 3
ROWS = 8
VMEM = pl.BlockSpec(memory_space=pltpu.VMEM)
ANY = pl.BlockSpec(memory_space=pl.ANY)
SMEM = pl.BlockSpec(memory_space=pltpu.SMEM)
F32 = jnp.float32
BF16 = jnp.bfloat16


def lon_table(order, parts, padded):
    index = np.arange(order)
    half = order // 2
    freq = np.where(index <= half, index, index - half)[:, None]
    phase = (freq * index[None, :] % order) * (2.0 * math.pi / order)
    factor = np.where((index == 0) | (index == half), math.sqrt(1.0 / order), math.sqrt(2.0 / order))
    table = np.where(index[:, None] <= half, np.cos(phase), np.sin(phase)) * factor[:, None]
    table = table.reshape(parts, order // parts, order)
    table = np.pad(table, ((0, 0), (0, padded - order // parts), (0, 0))).reshape(parts * padded, order)
    high = table.astype(np.float32).astype(ml_dtypes.bfloat16)
    low = (table - high.astype(np.float64)).astype(np.float32).astype(ml_dtypes.bfloat16)
    return high, low


def call(kernel, outs, specs, *args, scratch=(), limit=8, cost=None):
    return pl.pallas_call(
        kernel,
        out_shape=outs,
        in_specs=specs,
        out_specs=jax.tree.map(lambda _: VMEM, outs),
        scratch_shapes=scratch,
        cost_estimate=cost,
        compiler_params=pltpu.CompilerParams(vmem_limit_bytes=limit * 1024 * 1024),
    )(*args)


def tree_sum(parts):
    parts = list(parts)
    while len(parts) > 1:
        parts = [sum(parts[at:at + 2][1:], parts[at]) for at in range(0, len(parts), 2)]
    return parts[0]


def transform_kernel(dims, cell_ref, high_any, low_any, foot_any, off_any, sub_any, count_any, rinv_any, *refs):
    nc, nb, modes, groups, band = dims
    out_ref, weight_ref, high_ref, low_ref, foot_ref, off_ref, sub_ref, count_ref, rinv_ref, sems = refs
    copies = [
        pltpu.make_async_copy(source, target, sems.at[at])
        for at, (source, target) in enumerate(
            [
                (foot_any, foot_ref),
                (high_any, high_ref),
                (low_any, low_ref),
                (off_any, off_ref),
                (sub_any, sub_ref),
                (count_any, count_ref),
                (rinv_any, rinv_ref),
            ]
        )
    ]
    for copy in copies:
        copy.start()
    for copy in copies:
        copy.wait()
    ob = foot_ref.shape[1]
    lon = high_ref.shape[1]
    contract = (((1,), (1,)), ((), ()))
    for r in range(CR):
        foot = foot_ref[:, :, r * lon:(r + 1) * lon].reshape(nb * ob, lon)
        hat = lax.dot_general(high_ref[...], foot, contract, preferred_element_type=F32)
        hat += lax.dot_general(low_ref[...], foot, contract, preferred_element_type=F32)
        hat = hat.astype(BF16)
        for b in range(nb):
            at = (b * CR + r) * modes
            for c in range(nc):
                out_ref[c, at:at + modes, :] = hat[c * modes:(c + 1) * modes, b * ob:(b + 1) * ob]
    lane = lax.broadcasted_iota(jnp.int32, (16, ob), 1)
    ids = jnp.zeros((16, ob), F32)
    for b in range(nb):
        off = off_ref[b]
        values = (off // groups, cell_ref[0] * (band // CR) + off % groups, sub_ref[b])
        for at, value in enumerate(values):
            ids = jnp.where(lane == at * nb + b, value.astype(F32), ids)
    ids = ids.astype(BF16)
    for c in range(nc):
        out_ref[c, nb * CR * modes:, :] = ids
    row = lax.broadcasted_iota(jnp.int32, weight_ref.shape, 0)
    limit = jnp.zeros(weight_ref.shape, jnp.int32)
    for s in range(weight_ref.shape[0]):
        limit = jnp.where(row == s, count_ref[s], limit)
    lane = lax.broadcasted_iota(jnp.int32, weight_ref.shape, 1)
    weight_ref[...] = jnp.where(lane < limit, rinv_ref[...], 0.0)


def fetch_kernel(lat_any, start_any, lat_ref, start_ref, sems):
    modes = lat_any.shape[0]
    copies = [pltpu.make_async_copy(lat_any.at[m], lat_ref.at[:, m, :], sems.at[m]) for m in range(modes)]
    copies.append(pltpu.make_async_copy(start_any, start_ref, sems.at[modes]))
    for copy in copies:
        copy.start()
    for copy in copies:
        copy.wait()


def fold(ref):
    periods, modes, _ = ref.shape
    total = jnp.zeros((ROWS, ref.shape[2]), F32)
    for p in range(periods):
        for at in range(0, modes, ROWS):
            part = ref[p, at:at + ROWS, :]
            total += part * part
    return total


def forward(dims, field_ref, lat_ref, foot_ref, ids_ref, sim_ref):
    nc, nb, modes, groups, band = dims
    subs = sim_ref.shape[0] - ROWS
    sim_ref[...] = jnp.zeros_like(sim_ref)
    for j in range(nc):
        for b in range(nb):
            period = ids_ref[j, b]
            row = ids_ref[j, nb + b] * CR
            sub = ids_ref[j, 2 * nb + b]
            total = None
            for r in range(CR):
                column = jnp.sum(lat_ref[row + r] * field_ref[period], axis=1, keepdims=True)
                at = (b * CR + r) * modes
                term = foot_ref[j, at:at + modes, :].astype(F32) * column
                total = term if total is None else total + term
            sim_ref[pl.ds(sub, 1), :] += jnp.sum(total, axis=0, keepdims=True)
    sim_ref[subs:, :] = fold(field_ref)


def pieces(refs, size, rows):
    found = []
    for ref in refs:
        found += [ref.at[at:at + rows] for at in range(0, ref.shape[0], rows)]
    assert len(found) == size
    return found


def added(refs, rows):
    return tree_sum(ref[...] for ref in pieces(refs, sum(ref.shape[0] for ref in refs) // rows, rows))


def add_kernel(one_ref, other_ref, out_ref):
    out_ref[...] = one_ref[...] + other_ref[...]


def first_kernel(dims, no, own_ref, lat_ref, came_ref, *refs):
    nc, nb, modes, _, _ = dims
    near_refs, refs = refs[:-6], refs[-6:]
    out_ref, field_ref, foot_ref, all_ref, ids_ref, sem = refs
    rows = nb * CR * modes
    for j in range(nc):
        all_ref[j:j + 1, :] = came_ref[j, rows:rows + 16, :].astype(F32)[0:1].astype(jnp.int32)
    copy = pltpu.make_async_copy(all_ref, ids_ref, sem)
    copy.start()
    for j in range(nc):
        foot_ref[j] = came_ref[j, :rows, :]
    per_dev = field_ref.shape[0] // no
    for s, near_ref in enumerate(pieces(near_refs, no, per_dev * modes)):
        for l in range(per_dev):
            field_ref[((own_ref[0] ^ s) if permuted(no) else s) * per_dev + l] = near_ref[l * modes:(l + 1) * modes, :]
    copy.wait()
    forward(dims, field_ref, lat_ref, foot_ref, ids_ref, out_ref)


def adjoint_kernel(dims, first, ids_ref, weight_ref, foot_ref, *refs):
    nc, nb, modes, groups, band = dims
    sim_refs, refs = refs[:-3], refs[-3:]
    out_ref, norm_ref, weighted_ref = refs
    subs = weight_ref.shape[0]
    mine = nc * nb
    total = added(sim_refs, subs + ROWS)
    norm = jnp.sqrt(jnp.sum(total[subs:], keepdims=True))
    norm_ref[...] = jnp.broadcast_to(norm, norm_ref.shape)
    scale = 1.0 / norm
    sim = total[:subs]
    weighted = sim * weight_ref[...]
    weighted_ref[...] = weighted
    lane = lax.broadcasted_iota(jnp.int32, (modes, 128), 1)
    parts = [jnp.zeros((modes, 128), F32) for _ in range(CR)]
    for j in range(nc):
        for b in range(nb):
            chosen = weighted_ref[pl.ds(ids_ref[j, 2 * nb + b], 1), :]
            for r in range(CR):
                at = (b * CR + r) * modes
                column = jnp.sum(foot_ref[j, at:at + modes, :].astype(F32) * chosen, axis=1, keepdims=True)
                parts[r] = jnp.where(lane == j * nb + b, column, parts[r])
    rest = 128 - CR * modes
    if rest:
        parts.append(jnp.zeros((rest, 128), F32))
    rows = jnp.concatenate(parts, axis=0).T
    out_ref[:mine, :] = rows[:mine] * scale
    out_ref[mine:mine + subs, :] = (sim * scale) * (weighted * scale)
    if first:
        lane = lax.broadcasted_iota(jnp.int32, (ROWS, 128), 1)
        line = lax.broadcasted_iota(jnp.int32, (ROWS, 128), 0)
        tail = jnp.zeros((ROWS, 128), jnp.int32)
        for j in range(nc):
            for b in range(nb):
                value = jnp.where(line == 0, ids_ref[j, b], ids_ref[j, nb + b])
                tail = jnp.where(lane == j * nb + b, value, tail)
        out_ref[mine + subs:, :] = tail.astype(F32)


def every_kernel(dims, no, at, *refs):
    refs, out_ref = refs[:-1], refs[-1]
    rows = sum(ref.shape[0] for ref in refs) // no
    for s, ref in enumerate(pieces(refs, no, rows)):
        out_ref[2 * s:2 * s + 2, :] = ref[at:at + ROWS, :][0:2].astype(jnp.int32)


def split(values):
    terms = []
    for _ in range(TERMS):
        terms.append(values.astype(BF16))
        values = values - terms[-1].astype(F32)
    return jnp.concatenate(terms, axis=0)


def image_kernel(dims, no, first, last, own_ref, ids_ref, all_ref, lat_ref, foot_ref, norm_ref, field_ref, *refs):
    nc, nb, modes, groups, band = dims
    if not first:
        prior_ref, refs = refs[0], refs[1:]
    ways = min(no, WAYS)
    kept = 6 + 2 * ways
    coef_refs, refs = refs[:-kept], refs[-kept:]
    wide_refs, refs = refs[-ways:], refs[:-ways]
    sum_refs, refs = refs[-ways:], refs[:-ways]
    if last:
        out_ref, row_ref, mine_ref, alpha_ref, next_ref, held_ref = refs
    else:
        out_ref, row_ref, next_ref, vector_ref, alpha_ref, held_ref = refs
    mine = nc * nb
    periods = field_ref.shape[0]
    per_dev = row_ref.shape[0]
    subs = ROWS
    rows = sum(ref.shape[0] for ref in coef_refs) // no
    coef_refs = pieces(coef_refs, no, rows)
    for s in range(no):
        held_ref[s] = coef_refs[s][:mine, :]
    for sum_ref in sum_refs:
        sum_ref[...] = jnp.zeros_like(sum_ref)

    line = lax.broadcasted_iota(jnp.int32, (TERMS * CHUNK, CHUNK * 128), 0)
    lane = lax.broadcasted_iota(jnp.int32, (TERMS * CHUNK, CHUNK * 128), 1)
    pick = jnp.where(line % CHUNK == lane // 128, 1.0, 0.0).astype(BF16)

    def group(at, carry):
        found = [at * ways + i for i in range(ways)]
        if permuted(no):
            found = [own_ref[0] ^ at_i for at_i in found]
        for chunk in range(0, mine, CHUNK):
            for at_i, wide_ref in zip(found, wide_refs):
                left = split(held_ref[at_i, chunk:chunk + CHUNK, :])
                wide = lax.dot_general(left, pick, (((0,), (0,)), ((), ())), preferred_element_type=F32)
                wide_ref[...] = wide[:CR * modes]
            for at in range(CHUNK):
                for at_i, wide_ref, sum_ref in zip(found, wide_refs, sum_refs):
                    period = all_ref[2 * at_i, chunk + at]
                    row = all_ref[2 * at_i + 1, chunk + at] * CR
                    total = sum_ref[period]
                    for r in range(CR):
                        coef = wide_ref[r * modes:(r + 1) * modes, at * 128:(at + 1) * 128]
                        total += coef * lat_ref[row + r]
                    sum_ref[period] = total
        return carry

    if no == ways:
        group(0, 0)
    else:
        lax.fori_loop(0, no // ways, group, 0)
    gain = jnp.sum(tree_sum(ref[mine:mine + subs, :] for ref in coef_refs), keepdims=True)
    alpha_ref[...] = jnp.broadcast_to(1.0 + gain, alpha_ref.shape)
    norm = norm_ref[0:1, :]
    scale = 1.0 / norm
    for p in range(periods):
        vector = field_ref[p] * scale
        if not last:
            vector_ref[p] = vector
        rest = tree_sum(sum_ref[p] for sum_ref in sum_refs) - vector * gain
        if not first:
            rest -= prior_ref[p] * norm
        next_ref[p] = rest
    for l in range(per_dev):
        row_ref[l] = field_ref[own_ref[0] * per_dev + l] * scale
    if last:
        out_ref[...] = fold(next_ref)
        for l in range(per_dev):
            mine_ref[l] = next_ref[own_ref[0] * per_dev + l]
    else:
        forward(dims, next_ref, lat_ref, foot_ref, ids_ref, out_ref)


def finish_kernel(factor, sums, *refs):
    sum_refs, refs = refs[:sums], refs[sums:]
    row_refs, refs = refs[:STEPS], refs[STEPS:]
    mine_ref, refs = refs[0], refs[1:]
    alphas, refs = refs[:STEPS], refs[STEPS:]
    norms, refs = refs[:STEPS - 1], refs[STEPS - 1:]
    out_ref, coef_ref = refs
    norm = jnp.sqrt(jnp.sum(added(sum_refs, ROWS), keepdims=True))
    for k in range(STEPS):
        out_ref[k] = row_refs[k][...] * factor
    out_ref[STEPS] = mine_ref[...] * (factor / norm)
    row = lax.broadcasted_iota(jnp.int32, coef_ref.shape, 0)
    col = lax.broadcasted_iota(jnp.int32, coef_ref.shape, 1)
    coefs = jnp.zeros(coef_ref.shape, F32)
    for k in range(STEPS):
        beta = norms[k][0:1, 0:1] if k < STEPS - 1 else norm
        coefs = jnp.where((row == 0) & (col == k), alphas[k][0:1, 0:1], coefs)
        coefs = jnp.where((row == 1) & (col == k), beta, coefs)
    coef_ref[...] = coefs


def permuted(size):
    return size <= 4 and size & (size - 1) == 0


def share(array, axis):
    size = lax.axis_size(axis)
    if not permuted(size):
        return [swap(jnp.broadcast_to(array[None], (size,) + array.shape), axis).reshape(-1, array.shape[1])]
    return [array] + [lax.ppermute(array, axis, [(d, d ^ s) for d in range(size)]) for s in range(1, size)]


def addends(array, axis):
    size = lax.axis_size(axis)
    if size != 8:
        return [swap(jnp.broadcast_to(array[None], (size,) + array.shape), axis).reshape(-1, array.shape[1])]
    other = lax.ppermute(array, axis, [(d, d ^ 1) for d in range(size)])
    both = call(add_kernel, jax.ShapeDtypeStruct(array.shape, F32), [VMEM] * 2, array, other)
    return [both] + [lax.ppermute(both, axis, [(d, d ^ s) for d in range(size)]) for s in (2, 4, 6)]


def swap(array, axis):
    return lax.all_to_all(array, axis, split_axis=0, concat_axis=0, tiled=True)


def body(start, lat_mats, footprints, blk_sub, blk_off, counts, rinv):
    per_dev, held, lat_rows = start.shape
    nc = lax.axis_size("cell")
    no = lax.axis_size("obs")
    lon_cols = held * nc
    band = lat_rows // nc
    groups = band // CR
    nb, ob, _ = footprints.shape
    subs = counts.shape[0]
    modes = -(-held // 16) * 16
    mine = nc * nb
    periods = per_dev * no
    dims = (nc, nb, modes, groups, band)
    shape = functools.partial(jax.ShapeDtypeStruct, dtype=F32)

    high, low = lon_table(lon_cols, nc, modes)
    if modes != held:
        start = jnp.pad(start, ((0, 0), (0, modes - held), (0, 0)))
        lat_mats = jnp.pad(lat_mats, ((0, modes - held), (0, 0), (0, 0)))
    own = lax.axis_index("obs").astype(jnp.int32).reshape(1)
    cell = lax.axis_index("cell").astype(jnp.int32).reshape(1)

    start = start.reshape(per_dev * modes, lat_rows)
    near = share(start, "obs")
    foot_rows = nb * CR * modes
    hats, weights = call(
        functools.partial(transform_kernel, dims),
        (jax.ShapeDtypeStruct((nc, foot_rows + 16, ob), BF16), shape((subs, ob))),
        [SMEM] + [ANY] * 7,
        cell, jnp.asarray(high), jnp.asarray(low), footprints, blk_off, blk_sub, counts, rinv.reshape(subs, ob),
        scratch=[
            pltpu.VMEM(high.shape, BF16),
            pltpu.VMEM(low.shape, BF16),
            pltpu.VMEM(footprints.shape, BF16),
            pltpu.SMEM((nb,), jnp.int32),
            pltpu.SMEM((nb,), jnp.int32),
            pltpu.SMEM((subs,), jnp.int32),
            pltpu.VMEM((subs, ob), F32),
            pltpu.SemaphoreType.DMA((7,)),
        ],
        limit=60,
    )
    came = swap(hats, "cell")
    lat, start, _ = lax.optimization_barrier((lat_mats, start, weights))
    lat, start = call(
        fetch_kernel,
        (shape((lat_rows, modes, lat_rows)), shape(start.shape)),
        [ANY] * 2,
        lat, start,
        scratch=[pltpu.SemaphoreType.DMA((modes + 1,))],
        limit=50,
        cost=pl.CostEstimate(flops=0, transcendentals=0, bytes_accessed=8 * (lat.size + start.size)),
    )
    if permuted(no):
        near[0] = start

    field_shape = shape((periods, modes, lat_rows))
    small = shape((ROWS, 128))
    own_shape = shape((per_dev, modes, lat_rows))
    sims, field, foot, ids = call(
        functools.partial(first_kernel, dims, no),
        (
            shape((subs + ROWS, ob)),
            field_shape,
            jax.ShapeDtypeStruct((nc, foot_rows, ob), BF16),
            jax.ShapeDtypeStruct((nc, 128), jnp.int32),
        ),
        [SMEM] + [VMEM] * (2 + len(near)),
        own, lat, came, *near,
        scratch=[pltpu.SMEM((nc, 128), jnp.int32), pltpu.SemaphoreType.DMA],
    )
    ways = min(no, WAYS)
    rows, alphas, norms = [], [], []
    vector = None
    for step in range(STEPS):
        first, last = step == 0, step == STEPS - 1
        parts = addends(sims, "cell")
        coefs, norm = call(
            functools.partial(adjoint_kernel, dims, first),
            (shape((mine + subs + (ROWS if first else 0), 128)), small),
            [SMEM] + [VMEM] * (2 + len(parts)),
            ids, weights, foot, *parts,
            scratch=[pltpu.VMEM((subs, ob), F32)],
        )
        coefs = share(coefs, "obs")
        if first:
            every = call(
                functools.partial(every_kernel, dims, no, mine + subs),
                jax.ShapeDtypeStruct((2 * no, 128), jnp.int32),
                [VMEM] * len(coefs),
                *coefs,
            )
        before = [] if first else [vector]
        sims, row, field, *vector, alpha = call(
            functools.partial(image_kernel, dims, no, first, last),
            (
                shape((ROWS if last else subs + ROWS, 128)),
                own_shape,
                own_shape if last else field_shape,
                *([] if last else [field_shape]),
                small,
            ),
            [SMEM] * 3 + [VMEM] * (4 + len(before) + len(coefs)),
            own, ids, every, lat, foot, norm, field, *before, *coefs,
            scratch=[pltpu.VMEM(field_shape.shape, F32)] * last
            + [pltpu.VMEM((no, mine, 128), F32)]
            + [pltpu.VMEM(field_shape.shape, F32)] * ways
            + [pltpu.VMEM((CR * modes, CHUNK * 128), F32)] * ways,
            limit=16,
        )
        vector = None if last else vector[0]
        rows.append(row)
        alphas.append(alpha)
        norms.append(norm)
    factor = math.sqrt(periods * lon_cols * lat_rows)
    parts = addends(sims, "cell")
    krylov, coeffs = call(
        functools.partial(finish_kernel, factor, len(parts)),
        (shape((STEPS + 1, per_dev, modes, lat_rows)), shape((2, STEPS))),
        [VMEM] * (len(parts) + STEPS + 1 + STEPS + STEPS - 1),
        *parts, *rows, field, *alphas, *norms[1:],
    )
    return krylov[:, :, :held], coeffs


def solution(mesh):
    placed = (
        P("obs", "cell", None),
        P("cell", None, None),
        P(("obs", "cell"), None, None),
        P(("obs", "cell")),
        P(("obs", "cell")),
        P("obs"),
        P("obs"),
    )
    return jax.shard_map(
        body,
        mesh=mesh,
        in_specs=placed,
        out_specs=(P(None, "obs", "cell", None), P()),
        check_vma=False,
    )
```

```python
import functools
import math

import jax
import jax.numpy as jnp
import ml_dtypes
import numpy as np
from jax import lax
from jax.experimental import pallas as pl
from jax.experimental.pallas import tpu as pltpu
from jax.sharding import PartitionSpec as P

CR = 2
WAYS = 2
CHUNK = 16
TERMS = 3
STEPS = 3
ROWS = 8
VMEM = pl.BlockSpec(memory_space=pltpu.VMEM)
ANY = pl.BlockSpec(memory_space=pl.ANY)
SMEM = pl.BlockSpec(memory_space=pltpu.SMEM)
F32 = jnp.float32
BF16 = jnp.bfloat16


def lon_table(order, parts, padded):
    index = np.arange(order)
    half = order // 2
    freq = np.where(index <= half, index, index - half)[:, None]
    phase = (freq * index[None, :] % order) * (2.0 * math.pi / order)
    factor = np.where((index == 0) | (index == half), math.sqrt(1.0 / order), math.sqrt(2.0 / order))
    table = np.where(index[:, None] <= half, np.cos(phase), np.sin(phase)) * factor[:, None]
    table = table.reshape(parts, order // parts, order)
    table = np.pad(table, ((0, 0), (0, padded - order // parts), (0, 0))).reshape(parts * padded, order)
    high = table.astype(np.float32).astype(ml_dtypes.bfloat16)
    low = (table - high.astype(np.float64)).astype(np.float32).astype(ml_dtypes.bfloat16)
    return high, low


def call(kernel, outs, specs, *args, scratch=(), limit=8, cost=None):
    return pl.pallas_call(
        kernel,
        out_shape=outs,
        in_specs=specs,
        out_specs=jax.tree.map(lambda _: VMEM, outs),
        scratch_shapes=scratch,
        cost_estimate=cost,
        compiler_params=pltpu.CompilerParams(vmem_limit_bytes=limit * 1024 * 1024),
    )(*args)


def tree_sum(parts):
    parts = list(parts)
    while len(parts) > 1:
        parts = [sum(parts[at:at + 2][1:], parts[at]) for at in range(0, len(parts), 2)]
    return parts[0]


def transform_kernel(dims, cell_ref, high_any, low_any, foot_any, off_any, sub_any, count_any, rinv_any, *refs):
    nc, nb, modes, groups, band = dims
    out_ref, weight_ref, high_ref, low_ref, foot_ref, off_ref, sub_ref, count_ref, rinv_ref, sems = refs
    copies = [
        pltpu.make_async_copy(source, target, sems.at[at])
        for at, (source, target) in enumerate(
            [
                (foot_any, foot_ref),
                (high_any, high_ref),
                (low_any, low_ref),
                (off_any, off_ref),
                (sub_any, sub_ref),
                (count_any, count_ref),
                (rinv_any, rinv_ref),
            ]
        )
    ]
    for copy in copies:
        copy.start()
    for copy in copies:
        copy.wait()
    ob = foot_ref.shape[1]
    lon = high_ref.shape[1]
    contract = (((1,), (1,)), ((), ()))
    for r in range(CR):
        foot = foot_ref[:, :, r * lon:(r + 1) * lon].reshape(nb * ob, lon)
        hat = lax.dot_general(high_ref[...], foot, contract, preferred_element_type=F32)
        hat += lax.dot_general(low_ref[...], foot, contract, preferred_element_type=F32)
        hat = hat.astype(BF16)
        for b in range(nb):
            at = (b * CR + r) * modes
            for c in range(nc):
                out_ref[c, at:at + modes, :] = hat[c * modes:(c + 1) * modes, b * ob:(b + 1) * ob]
    lane = lax.broadcasted_iota(jnp.int32, (16, ob), 1)
    ids = jnp.zeros((16, ob), F32)
    for b in range(nb):
        off = off_ref[b]
        values = (off // groups, cell_ref[0] * (band // CR) + off % groups, sub_ref[b])
        for at, value in enumerate(values):
            ids = jnp.where(lane == at * nb + b, value.astype(F32), ids)
    ids = ids.astype(BF16)
    for c in range(nc):
        out_ref[c, nb * CR * modes:, :] = ids
    row = lax.broadcasted_iota(jnp.int32, weight_ref.shape, 0)
    limit = jnp.zeros(weight_ref.shape, jnp.int32)
    for s in range(weight_ref.shape[0]):
        limit = jnp.where(row == s, count_ref[s], limit)
    lane = lax.broadcasted_iota(jnp.int32, weight_ref.shape, 1)
    weight_ref[...] = jnp.where(lane < limit, rinv_ref[...], 0.0)


def fetch_kernel(lat_any, start_any, lat_ref, start_ref, pick_ref, sems):
    modes = lat_any.shape[0]
    copies = [pltpu.make_async_copy(lat_any.at[m], lat_ref.at[:, m, :], sems.at[m]) for m in range(modes)]
    copies.append(pltpu.make_async_copy(start_any, start_ref, sems.at[modes]))
    for copy in copies:
        copy.start()
    line = lax.broadcasted_iota(jnp.int32, pick_ref.shape, 0)
    lane = lax.broadcasted_iota(jnp.int32, pick_ref.shape, 1)
    pick_ref[...] = jnp.where(line % CHUNK == lane // 128, 1.0, 0.0).astype(BF16)
    for copy in copies:
        copy.wait()


def fold(ref):
    periods, modes, _ = ref.shape
    total = jnp.zeros((ROWS, ref.shape[2]), F32)
    for p in range(periods):
        for at in range(0, modes, ROWS):
            part = ref[p, at:at + ROWS, :]
            total += part * part
    return total


def forward(dims, field_ref, lat_ref, foot_ref, ids_ref, sim_ref):
    nc, nb, modes, groups, band = dims
    subs = sim_ref.shape[0] - ROWS
    sim_ref[...] = jnp.zeros_like(sim_ref)
    for j in range(nc):
        for b in range(nb):
            period = ids_ref[j, b]
            row = ids_ref[j, nb + b] * CR
            sub = ids_ref[j, 2 * nb + b]
            total = None
            for r in range(CR):
                column = jnp.sum(lat_ref[row + r] * field_ref[period], axis=1, keepdims=True)
                at = (b * CR + r) * modes
                term = foot_ref[j, at:at + modes, :].astype(F32) * column
                total = term if total is None else total + term
            sim_ref[pl.ds(sub, 1), :] += jnp.sum(total, axis=0, keepdims=True)
    sim_ref[subs:, :] = fold(field_ref)


def pieces(refs, size, rows):
    found = []
    for ref in refs:
        found += [ref.at[at:at + rows] for at in range(0, ref.shape[0], rows)]
    assert len(found) == size
    return found


def added(refs, rows):
    return tree_sum(ref[...] for ref in pieces(refs, sum(ref.shape[0] for ref in refs) // rows, rows))


def add_kernel(one_ref, other_ref, out_ref):
    out_ref[...] = one_ref[...] + other_ref[...]


def first_kernel(dims, no, own_ref, lat_ref, came_ref, *refs):
    nc, nb, modes, _, _ = dims
    near_refs, refs = refs[:-8], refs[-8:]
    out_ref, field_ref, foot_ref, all_ref, choose_ref, tail_ref, ids_ref, sem = refs
    rows = nb * CR * modes
    for j in range(nc):
        all_ref[j:j + 1, :] = came_ref[j, rows:rows + 16, :].astype(F32)[0:1].astype(jnp.int32)
    copy = pltpu.make_async_copy(all_ref, ids_ref, sem)
    copy.start()
    for j in range(nc):
        foot_ref[j] = came_ref[j, :rows, :]
    per_dev = field_ref.shape[0] // no
    for s, near_ref in enumerate(pieces(near_refs, no, per_dev * modes)):
        for l in range(per_dev):
            field_ref[((own_ref[0] ^ s) if permuted(no) else s) * per_dev + l] = near_ref[l * modes:(l + 1) * modes, :]
    copy.wait()
    line = lax.broadcasted_iota(jnp.int32, choose_ref.shape, 0)
    lane = lax.broadcasted_iota(jnp.int32, choose_ref.shape, 1)
    tail_line = lax.broadcasted_iota(jnp.int32, tail_ref.shape, 0)
    tail_lane = lax.broadcasted_iota(jnp.int32, tail_ref.shape, 1)
    subs = jnp.zeros(choose_ref.shape, jnp.int32)
    tail = jnp.zeros(tail_ref.shape, jnp.int32)
    for j in range(nc):
        for b in range(nb):
            subs = jnp.where(line == j * nb + b, ids_ref[j, 2 * nb + b], subs)
            value = jnp.where(tail_line == 0, ids_ref[j, b], ids_ref[j, nb + b])
            tail = jnp.where(tail_lane == j * nb + b, value, tail)
    choose_ref[...] = jnp.where(lane % (choose_ref.shape[1] // TERMS) == subs, 1.0, 0.0).astype(BF16)
    tail_ref[...] = tail.astype(F32)
    forward(dims, field_ref, lat_ref, foot_ref, ids_ref, out_ref)


def split(values):
    terms = []
    for _ in range(TERMS):
        terms.append(values.astype(BF16).astype(F32))
        values = values - terms[-1]
    return jnp.concatenate(terms, axis=0).astype(BF16)


def adjoint_kernel(dims, tails, choose_ref, weight_ref, foot_ref, *refs):
    nc, nb, modes, groups, band = dims
    tail_refs, refs = refs[:tails], refs[tails:]
    sim_refs, refs = refs[:-3], refs[-3:]
    out_ref, norm_ref, chosen_ref = refs
    subs = weight_ref.shape[0]
    mine = nc * nb
    total = added(sim_refs, subs + ROWS)
    norm = jnp.sqrt(jnp.sum(total[subs:], keepdims=True))
    norm_ref[...] = jnp.broadcast_to(norm, norm_ref.shape)
    scale = 1.0 / norm
    sim = total[:subs]
    weighted = sim * weight_ref[...]
    chosen_ref[...] = jnp.dot(choose_ref[...], split(weighted), preferred_element_type=F32)
    lane = lax.broadcasted_iota(jnp.int32, (modes, 128), 1)
    parts = [jnp.zeros((modes, 128), F32) for _ in range(CR)]
    for j in range(nc):
        for b in range(nb):
            at_t = j * nb + b
            chosen = chosen_ref[at_t:at_t + 1, :]
            for r in range(CR):
                at = (b * CR + r) * modes
                column = jnp.sum(foot_ref[j, at:at + modes, :].astype(F32) * chosen, axis=1, keepdims=True)
                parts[r] = jnp.where(lane == at_t, column, parts[r])
    rest = 128 - CR * modes
    if rest:
        parts.append(jnp.zeros((rest, 128), F32))
    rows = jnp.concatenate(parts, axis=0).T
    out_ref[:mine, :] = rows[:mine] * scale
    out_ref[mine:mine + subs, :] = (sim * scale) * (weighted * scale)
    for tail_ref in tail_refs:
        out_ref[mine + subs:, :] = tail_ref[...]


def every_kernel(dims, no, at, *refs):
    refs, out_ref = refs[:-1], refs[-1]
    rows = sum(ref.shape[0] for ref in refs) // no
    for s, ref in enumerate(pieces(refs, no, rows)):
        out_ref[2 * s:2 * s + 2, :] = ref[at:at + ROWS, :][0:2].astype(jnp.int32)


def image_kernel(dims, no, first, last, own_ref, ids_ref, all_ref, lat_ref, foot_ref, pick_ref, norm_ref, field_ref, *refs):
    nc, nb, modes, groups, band = dims
    if not first:
        prior_ref, refs = refs[0], refs[1:]
    ways = min(no, WAYS)
    kept = 6 + 2 * ways
    coef_refs, refs = refs[:-kept], refs[-kept:]
    wide_refs, refs = refs[-ways:], refs[:-ways]
    sum_refs, refs = refs[-ways:], refs[:-ways]
    if last:
        out_ref, row_ref, mine_ref, alpha_ref, next_ref, held_ref = refs
    else:
        out_ref, row_ref, next_ref, vector_ref, alpha_ref, held_ref = refs
    mine = nc * nb
    periods = field_ref.shape[0]
    per_dev = row_ref.shape[0]
    subs = ROWS
    rows = sum(ref.shape[0] for ref in coef_refs) // no
    coef_refs = pieces(coef_refs, no, rows)
    for s in range(no):
        held_ref[s] = coef_refs[s][:mine, :]
    for sum_ref in sum_refs:
        sum_ref[...] = jnp.zeros_like(sum_ref)

    def group(at, carry):
        found = [at * ways + i for i in range(ways)]
        if permuted(no):
            found = [own_ref[0] ^ at_i for at_i in found]
        for chunk in range(0, mine, CHUNK):
            for at_i, wide_ref in zip(found, wide_refs):
                left = split(held_ref[at_i, chunk:chunk + CHUNK, :])
                wide = lax.dot_general(left, pick_ref[...], (((0,), (0,)), ((), ())), preferred_element_type=F32)
                wide_ref[...] = wide[:CR * modes]
            for at in range(CHUNK):
                for at_i, wide_ref, sum_ref in zip(found, wide_refs, sum_refs):
                    period = all_ref[2 * at_i, chunk + at]
                    row = all_ref[2 * at_i + 1, chunk + at] * CR
                    total = sum_ref[period]
                    for r in range(CR):
                        coef = wide_ref[r * modes:(r + 1) * modes, at * 128:(at + 1) * 128]
                        total += coef * lat_ref[row + r]
                    sum_ref[period] = total
        return carry

    if no <= 4:
        for at in range(no // ways):
            group(at, 0)
    else:
        lax.fori_loop(0, no // ways, group, 0)
    gain = jnp.sum(tree_sum(ref[mine:mine + subs, :] for ref in coef_refs), keepdims=True)
    alpha_ref[...] = jnp.broadcast_to(1.0 + gain, alpha_ref.shape)
    norm = norm_ref[0:1, :]
    scale = 1.0 / norm
    for p in range(periods):
        vector = field_ref[p] * scale
        if not last:
            vector_ref[p] = vector
        rest = tree_sum(sum_ref[p] for sum_ref in sum_refs) - vector * gain
        if not first:
            rest -= prior_ref[p] * norm
        next_ref[p] = rest
    for l in range(per_dev):
        row_ref[l] = field_ref[own_ref[0] * per_dev + l] * scale
    if last:
        out_ref[...] = fold(next_ref)
        for l in range(per_dev):
            mine_ref[l] = next_ref[own_ref[0] * per_dev + l]
    else:
        forward(dims, next_ref, lat_ref, foot_ref, ids_ref, out_ref)


def finish_kernel(factor, sums, *refs):
    sum_refs, refs = refs[:sums], refs[sums:]
    row_refs, refs = refs[:STEPS], refs[STEPS:]
    mine_ref, refs = refs[0], refs[1:]
    alphas, refs = refs[:STEPS], refs[STEPS:]
    norms, refs = refs[:STEPS - 1], refs[STEPS - 1:]
    out_ref, coef_ref = refs
    norm = jnp.sqrt(jnp.sum(added(sum_refs, ROWS), keepdims=True))
    for k in range(STEPS):
        out_ref[k] = row_refs[k][...] * factor
    out_ref[STEPS] = mine_ref[...] * (factor / norm)
    row = lax.broadcasted_iota(jnp.int32, coef_ref.shape, 0)
    col = lax.broadcasted_iota(jnp.int32, coef_ref.shape, 1)
    coefs = jnp.zeros(coef_ref.shape, F32)
    for k in range(STEPS):
        beta = norms[k][0:1, 0:1] if k < STEPS - 1 else norm
        coefs = jnp.where((row == 0) & (col == k), alphas[k][0:1, 0:1], coefs)
        coefs = jnp.where((row == 1) & (col == k), beta, coefs)
    coef_ref[...] = coefs


def permuted(size):
    return size <= 4 and size & (size - 1) == 0


def share(array, axis):
    size = lax.axis_size(axis)
    if not permuted(size):
        return [swap(jnp.broadcast_to(array[None], (size,) + array.shape), axis).reshape(-1, array.shape[1])]
    return [array] + [lax.ppermute(array, axis, [(d, d ^ s) for d in range(size)]) for s in range(1, size)]


def addends(array, axis):
    size = lax.axis_size(axis)
    if size != 8:
        return [swap(jnp.broadcast_to(array[None], (size,) + array.shape), axis).reshape(-1, array.shape[1])]
    other = lax.ppermute(array, axis, [(d, d ^ 1) for d in range(size)])
    both = call(add_kernel, jax.ShapeDtypeStruct(array.shape, F32), [VMEM] * 2, array, other)
    return [both] + [lax.ppermute(both, axis, [(d, d ^ s) for d in range(size)]) for s in (2, 4, 6)]


def swap(array, axis):
    return lax.all_to_all(array, axis, split_axis=0, concat_axis=0, tiled=True)


def body(start, lat_mats, footprints, blk_sub, blk_off, counts, rinv):
    per_dev, held, lat_rows = start.shape
    nc = lax.axis_size("cell")
    no = lax.axis_size("obs")
    lon_cols = held * nc
    band = lat_rows // nc
    groups = band // CR
    nb, ob, _ = footprints.shape
    subs = counts.shape[0]
    modes = -(-held // 16) * 16
    mine = nc * nb
    periods = per_dev * no
    dims = (nc, nb, modes, groups, band)
    shape = functools.partial(jax.ShapeDtypeStruct, dtype=F32)

    high, low = lon_table(lon_cols, nc, modes)
    if modes != held:
        start = jnp.pad(start, ((0, 0), (0, modes - held), (0, 0)))
        lat_mats = jnp.pad(lat_mats, ((0, modes - held), (0, 0), (0, 0)))
    own = lax.axis_index("obs").astype(jnp.int32).reshape(1)
    cell = lax.axis_index("cell").astype(jnp.int32).reshape(1)

    start = start.reshape(per_dev * modes, lat_rows)
    near = share(start, "obs")
    foot_rows = nb * CR * modes
    hats, weights = call(
        functools.partial(transform_kernel, dims),
        (jax.ShapeDtypeStruct((nc, foot_rows + 16, ob), BF16), shape((subs, ob))),
        [SMEM] + [ANY] * 7,
        cell, jnp.asarray(high), jnp.asarray(low), footprints, blk_off, blk_sub, counts, rinv.reshape(subs, ob),
        scratch=[
            pltpu.VMEM(high.shape, BF16),
            pltpu.VMEM(low.shape, BF16),
            pltpu.VMEM(footprints.shape, BF16),
            pltpu.SMEM((nb,), jnp.int32),
            pltpu.SMEM((nb,), jnp.int32),
            pltpu.SMEM((subs,), jnp.int32),
            pltpu.VMEM((subs, ob), F32),
            pltpu.SemaphoreType.DMA((7,)),
        ],
        limit=60,
    )
    came = swap(hats, "cell")
    lat, start, _ = lax.optimization_barrier((lat_mats, start, weights))
    lat, start, pick = call(
        fetch_kernel,
        (
            shape((lat_rows, modes, lat_rows)),
            shape(start.shape),
            jax.ShapeDtypeStruct((TERMS * CHUNK, CHUNK * 128), BF16),
        ),
        [ANY] * 2,
        lat, start,
        scratch=[pltpu.SemaphoreType.DMA((modes + 1,))],
        limit=50,
        cost=pl.CostEstimate(flops=0, transcendentals=0, bytes_accessed=8 * (lat.size + start.size)),
    )
    if permuted(no):
        near[0] = start

    field_shape = shape((periods, modes, lat_rows))
    small = shape((ROWS, 128))
    own_shape = shape((per_dev, modes, lat_rows))
    sims, field, foot, ids, choose, tail = call(
        functools.partial(first_kernel, dims, no),
        (
            shape((subs + ROWS, ob)),
            field_shape,
            jax.ShapeDtypeStruct((nc, foot_rows, ob), BF16),
            jax.ShapeDtypeStruct((nc, 128), jnp.int32),
            jax.ShapeDtypeStruct((mine, TERMS * subs), BF16),
            shape((ROWS, 128)),
        ),
        [SMEM] + [VMEM] * (2 + len(near)),
        own, lat, came, *near,
        scratch=[pltpu.SMEM((nc, 128), jnp.int32), pltpu.SemaphoreType.DMA],
    )
    ways = min(no, WAYS)
    rows, alphas, norms = [], [], []
    vector = None
    for step in range(STEPS):
        first, last = step == 0, step == STEPS - 1
        parts = addends(sims, "cell")
        tails = [tail] if first else []
        coefs, norm = call(
            functools.partial(adjoint_kernel, dims, len(tails)),
            (shape((mine + subs + (ROWS if first else 0), 128)), small),
            [VMEM] * (3 + len(tails) + len(parts)),
            choose, weights, foot, *tails, *parts,
            scratch=[pltpu.VMEM((mine, ob), F32)],
        )
        coefs = share(coefs, "obs")
        if first:
            every = call(
                functools.partial(every_kernel, dims, no, mine + subs),
                jax.ShapeDtypeStruct((2 * no, 128), jnp.int32),
                [VMEM] * len(coefs),
                *coefs,
            )
        before = [] if first else [vector]
        sims, row, field, *vector, alpha = call(
            functools.partial(image_kernel, dims, no, first, last),
            (
                shape((ROWS if last else subs + ROWS, 128)),
                own_shape,
                own_shape if last else field_shape,
                *([] if last else [field_shape]),
                small,
            ),
            [SMEM] * 3 + [VMEM] * (5 + len(before) + len(coefs)),
            own, ids, every, lat, foot, pick, norm, field, *before, *coefs,
            scratch=[pltpu.VMEM(field_shape.shape, F32)] * last
            + [pltpu.VMEM((no, mine, 128), F32)]
            + [pltpu.VMEM(field_shape.shape, F32)] * ways
            + [pltpu.VMEM((CR * modes, CHUNK * 128), F32)] * ways,
            limit=16,
        )
        vector = None if last else vector[0]
        rows.append(row)
        alphas.append(alpha)
        norms.append(norm)
    factor = math.sqrt(periods * lon_cols * lat_rows)
    parts = addends(sims, "cell")
    krylov, coeffs = call(
        functools.partial(finish_kernel, factor, len(parts)),
        (shape((STEPS + 1, per_dev, modes, lat_rows)), shape((2, STEPS))),
        [VMEM] * (len(parts) + STEPS + 1 + STEPS + STEPS - 1),
        *parts, *rows, field, *alphas, *norms[1:],
    )
    return krylov[:, :, :held], coeffs


def solution(mesh):
    placed = (
        P("obs", "cell", None),
        P("cell", None, None),
        P(("obs", "cell"), None, None),
        P(("obs", "cell")),
        P(("obs", "cell")),
        P("obs"),
        P("obs"),
    )
    return jax.shard_map(
        body,
        mesh=mesh,
        in_specs=placed,
        out_specs=(P(None, "obs", "cell", None), P()),
        check_vma=False,
    )
```

```python
import functools
import math

import jax
import jax.numpy as jnp
import ml_dtypes
import numpy as np
from jax import lax
from jax.experimental import pallas as pl
from jax.experimental.pallas import tpu as pltpu
from jax.sharding import PartitionSpec as P

CR = 2
WAYS = 2
CHUNK = 16
TERMS = 3
STEPS = 3
ROWS = 8
VMEM = pl.BlockSpec(memory_space=pltpu.VMEM)
ANY = pl.BlockSpec(memory_space=pl.ANY)
F32 = jnp.float32
BF16 = jnp.bfloat16


def lon_table(order, parts, padded):
    index = np.arange(order)
    half = order // 2
    freq = np.where(index <= half, index, index - half)[:, None]
    phase = (freq * index[None, :] % order) * (2.0 * math.pi / order)
    factor = np.where((index == 0) | (index == half), math.sqrt(1.0 / order), math.sqrt(2.0 / order))
    table = np.where(index[:, None] <= half, np.cos(phase), np.sin(phase)) * factor[:, None]
    table = table.reshape(parts, order // parts, order)
    table = np.pad(table, ((0, 0), (0, padded - order // parts), (0, 0))).reshape(parts * padded, order)
    high = table.astype(np.float32).astype(ml_dtypes.bfloat16)
    low = (table - high.astype(np.float64)).astype(np.float32).astype(ml_dtypes.bfloat16)
    return high, low


def call(kernel, outs, specs, *args, scratch=(), limit=8, cost=None):
    return pl.pallas_call(
        kernel,
        out_shape=outs,
        in_specs=specs,
        out_specs=jax.tree.map(lambda _: VMEM, outs),
        scratch_shapes=scratch,
        cost_estimate=cost,
        compiler_params=pltpu.CompilerParams(vmem_limit_bytes=limit * 1024 * 1024),
    )(*args)


def tree_sum(parts):
    parts = list(parts)
    while len(parts) > 1:
        parts = [sum(parts[at:at + 2][1:], parts[at]) for at in range(0, len(parts), 2)]
    return parts[0]


def transform_kernel(dims, place_any, high_any, low_any, foot_any, off_any, sub_any, count_any, rinv_any, *refs):
    nc, nb, modes, groups, band = dims
    out_ref, weight_ref, high_ref, low_ref, foot_ref, off_ref, sub_ref, count_ref, rinv_ref, place_ref, sems = refs
    copies = [
        pltpu.make_async_copy(source, target, sems.at[at])
        for at, (source, target) in enumerate(
            [
                (foot_any, foot_ref),
                (high_any, high_ref),
                (low_any, low_ref),
                (off_any, off_ref),
                (sub_any, sub_ref),
                (count_any, count_ref),
                (rinv_any, rinv_ref),
                (place_any, place_ref),
            ]
        )
    ]
    for copy in copies:
        copy.start()
    for copy in copies:
        copy.wait()
    cell = place_ref[0] % nc
    obs = place_ref[0] // nc
    ob = foot_ref.shape[1]
    lon = high_ref.shape[1]
    contract = (((1,), (1,)), ((), ()))
    for r in range(CR):
        foot = foot_ref[:, :, r * lon:(r + 1) * lon].reshape(nb * ob, lon)
        hat = lax.dot_general(high_ref[...], foot, contract, preferred_element_type=F32)
        hat += lax.dot_general(low_ref[...], foot, contract, preferred_element_type=F32)
        hat = hat.astype(BF16)
        for b in range(nb):
            at = (b * CR + r) * modes
            for c in range(nc):
                out_ref[c, at:at + modes, :] = hat[c * modes:(c + 1) * modes, b * ob:(b + 1) * ob]
    lane = lax.broadcasted_iota(jnp.int32, (16, ob), 1)
    ids = jnp.zeros((16, ob), F32)
    for b in range(nb):
        off = off_ref[b]
        values = (off // groups, cell * (band // CR) + off % groups, sub_ref[b])
        for at, value in enumerate(values):
            ids = jnp.where(lane == at * nb + b, value.astype(F32), ids)
    ids = jnp.where(lane == 3 * nb, obs.astype(F32), ids).astype(BF16)
    for c in range(nc):
        out_ref[c, nb * CR * modes:, :] = ids
    row = lax.broadcasted_iota(jnp.int32, weight_ref.shape, 0)
    limit = jnp.zeros(weight_ref.shape, jnp.int32)
    for s in range(weight_ref.shape[0]):
        limit = jnp.where(row == s, count_ref[s], limit)
    lane = lax.broadcasted_iota(jnp.int32, weight_ref.shape, 1)
    weight_ref[...] = jnp.where(lane < limit, rinv_ref[...], 0.0)


def fetch_kernel(lat_any, start_any, lat_ref, start_ref, pick_ref, sems):
    modes = lat_any.shape[0]
    copies = [pltpu.make_async_copy(lat_any.at[m], lat_ref.at[:, m, :], sems.at[m]) for m in range(modes)]
    copies.append(pltpu.make_async_copy(start_any, start_ref, sems.at[modes]))
    for copy in copies:
        copy.start()
    line = lax.broadcasted_iota(jnp.int32, pick_ref.shape, 0)
    lane = lax.broadcasted_iota(jnp.int32, pick_ref.shape, 1)
    pick_ref[...] = jnp.where(line % CHUNK == lane // 128, 1.0, 0.0).astype(BF16)
    for copy in copies:
        copy.wait()


def fold(ref):
    periods, modes, _ = ref.shape
    total = jnp.zeros((ROWS, ref.shape[2]), F32)
    for p in range(periods):
        for at in range(0, modes, ROWS):
            part = ref[p, at:at + ROWS, :]
            total += part * part
    return total


def forward(dims, field_ref, lat_ref, foot_ref, ids_ref, sim_ref):
    nc, nb, modes, groups, band = dims
    subs = sim_ref.shape[0] - ROWS
    sim_ref[...] = jnp.zeros_like(sim_ref)
    for j in range(nc):
        for b in range(nb):
            period = ids_ref[j, b]
            row = ids_ref[j, nb + b] * CR
            sub = ids_ref[j, 2 * nb + b]
            total = None
            for r in range(CR):
                column = jnp.sum(lat_ref[row + r] * field_ref[period], axis=1, keepdims=True)
                at = (b * CR + r) * modes
                term = foot_ref[j, at:at + modes, :].astype(F32) * column
                total = term if total is None else total + term
            sim_ref[pl.ds(sub, 1), :] += jnp.sum(total, axis=0, keepdims=True)
    sim_ref[subs:, :] = fold(field_ref)


def pieces(refs, size, rows):
    found = []
    for ref in refs:
        found += [ref.at[at:at + rows] for at in range(0, ref.shape[0], rows)]
    assert len(found) == size
    return found


def added(refs, rows):
    return tree_sum(ref[...] for ref in pieces(refs, sum(ref.shape[0] for ref in refs) // rows, rows))


def add_kernel(one_ref, other_ref, out_ref):
    out_ref[...] = one_ref[...] + other_ref[...]


def first_kernel(dims, no, lat_ref, came_ref, *refs):
    nc, nb, modes, _, _ = dims
    near_refs, refs = refs[:-8], refs[-8:]
    out_ref, field_ref, foot_ref, all_ref, choose_ref, tail_ref, ids_ref, sem = refs
    rows = nb * CR * modes
    for j in range(nc):
        all_ref[j:j + 1, :] = came_ref[j, rows:rows + 16, :].astype(F32)[0:1].astype(jnp.int32)
    copy = pltpu.make_async_copy(all_ref, ids_ref, sem)
    copy.start()
    for j in range(nc):
        foot_ref[j] = came_ref[j, :rows, :]
    per_dev = field_ref.shape[0] // no
    copy.wait()
    own = ids_ref[0, 3 * nb]
    for s, near_ref in enumerate(pieces(near_refs, no, per_dev * modes)):
        for l in range(per_dev):
            field_ref[((own ^ s) if permuted(no) else s) * per_dev + l] = near_ref[l * modes:(l + 1) * modes, :]
    line = lax.broadcasted_iota(jnp.int32, choose_ref.shape, 0)
    lane = lax.broadcasted_iota(jnp.int32, choose_ref.shape, 1)
    tail_line = lax.broadcasted_iota(jnp.int32, tail_ref.shape, 0)
    tail_lane = lax.broadcasted_iota(jnp.int32, tail_ref.shape, 1)
    subs = jnp.zeros(choose_ref.shape, jnp.int32)
    tail = jnp.zeros(tail_ref.shape, jnp.int32)
    for j in range(nc):
        for b in range(nb):
            subs = jnp.where(line == j * nb + b, ids_ref[j, 2 * nb + b], subs)
            value = jnp.where(tail_line == 0, ids_ref[j, b], ids_ref[j, nb + b])
            tail = jnp.where(tail_lane == j * nb + b, value, tail)
    choose_ref[...] = jnp.where(lane % (choose_ref.shape[1] // TERMS) == subs, 1.0, 0.0).astype(BF16)
    tail_ref[...] = tail.astype(F32)
    forward(dims, field_ref, lat_ref, foot_ref, ids_ref, out_ref)


def split(values):
    terms = []
    for _ in range(TERMS):
        terms.append(values.astype(BF16).astype(F32))
        values = values - terms[-1]
    return jnp.concatenate(terms, axis=0).astype(BF16)


def adjoint_kernel(dims, tails, choose_ref, weight_ref, foot_ref, *refs):
    nc, nb, modes, groups, band = dims
    tail_refs, refs = refs[:tails], refs[tails:]
    sim_refs, refs = refs[:-3], refs[-3:]
    out_ref, norm_ref, chosen_ref = refs
    subs = weight_ref.shape[0]
    mine = nc * nb
    total = added(sim_refs, subs + ROWS)
    norm = jnp.sqrt(jnp.sum(total[subs:], keepdims=True))
    norm_ref[...] = jnp.broadcast_to(norm, norm_ref.shape)
    scale = 1.0 / norm
    sim = total[:subs]
    weighted = sim * weight_ref[...]
    chosen_ref[...] = jnp.dot(choose_ref[...], split(weighted), preferred_element_type=F32)
    lane = lax.broadcasted_iota(jnp.int32, (modes, 128), 1)
    parts = [jnp.zeros((modes, 128), F32) for _ in range(CR)]
    for j in range(nc):
        for b in range(nb):
            at_t = j * nb + b
            chosen = chosen_ref[at_t:at_t + 1, :]
            for r in range(CR):
                at = (b * CR + r) * modes
                column = jnp.sum(foot_ref[j, at:at + modes, :].astype(F32) * chosen, axis=1, keepdims=True)
                parts[r] = jnp.where(lane == at_t, column, parts[r])
    rest = 128 - CR * modes
    if rest:
        parts.append(jnp.zeros((rest, 128), F32))
    rows = jnp.concatenate(parts, axis=0).T
    out_ref[:mine, :] = rows[:mine] * scale
    out_ref[mine:mine + subs, :] = (sim * scale) * (weighted * scale)
    for tail_ref in tail_refs:
        out_ref[mine + subs:, :] = tail_ref[...]


def every_kernel(dims, no, at, *refs):
    refs, out_ref = refs[:-1], refs[-1]
    rows = sum(ref.shape[0] for ref in refs) // no
    for s, ref in enumerate(pieces(refs, no, rows)):
        out_ref[2 * s:2 * s + 2, :] = ref[at:at + ROWS, :][0:2].astype(jnp.int32)


def widen(rows, pick_ref):
    return lax.dot_general(split(rows), pick_ref[...], (((0,), (0,)), ((), ())), preferred_element_type=F32)


def image_kernel(dims, no, first, last, ids_in, all_in, lat_ref, foot_ref, pick_ref, norm_ref, field_ref, *refs):
    nc, nb, modes, groups, band = dims
    if not first:
        prior_ref, refs = refs[0], refs[1:]
    ways = min(no, WAYS)
    ids_ref, all_ref, sems = refs[-3:]
    refs = refs[:-3]
    copies = [
        pltpu.make_async_copy(ids_in, ids_ref, sems.at[0]),
        pltpu.make_async_copy(all_in, all_ref, sems.at[1]),
    ]
    for copy in copies:
        copy.start()
    kept = 7 + ways
    coef_refs, refs = refs[:-kept], refs[-kept:]
    wide_ref, refs = refs[-1], refs[:-1]
    sum_refs, refs = refs[-ways:], refs[:-ways]
    if last:
        out_ref, row_ref, mine_ref, alpha_ref, next_ref, held_ref = refs
    else:
        out_ref, row_ref, next_ref, vector_ref, alpha_ref, held_ref = refs
    mine = nc * nb
    chunks = mine // CHUNK
    periods = field_ref.shape[0]
    per_dev = row_ref.shape[0]
    subs = ROWS
    rows = sum(ref.shape[0] for ref in coef_refs) // no
    coef_refs = pieces(coef_refs, no, rows)
    ahead = no <= 4
    for s in range(no):
        if ahead:
            for q in range(chunks):
                wide_ref[s * chunks + q] = widen(coef_refs[s][q * CHUNK:(q + 1) * CHUNK, :], pick_ref)[:CR * modes]
        else:
            held_ref[s] = coef_refs[s][:mine, :]
    for sum_ref in sum_refs:
        sum_ref[...] = jnp.zeros_like(sum_ref)
    gain = jnp.sum(tree_sum(ref[mine:mine + subs, :] for ref in coef_refs), keepdims=True)
    alpha_ref[...] = jnp.broadcast_to(1.0 + gain, alpha_ref.shape)
    norm = norm_ref[0:1, :]
    scale = 1.0 / norm
    for copy in copies:
        copy.wait()
    own = ids_ref[0, 3 * nb]

    def group(at, carry):
        found = [at * ways + i for i in range(ways)]
        if permuted(no):
            found = [own ^ at_i for at_i in found]
        for q in range(chunks):
            slots = [at_i * chunks + q for at_i in found] if ahead else range(ways)
            if not ahead:
                for at_i, slot in zip(found, slots):
                    wide_ref[slot] = widen(held_ref[at_i, q * CHUNK:(q + 1) * CHUNK, :], pick_ref)[:CR * modes]
            for at in range(CHUNK):
                for at_i, slot, sum_ref in zip(found, slots, sum_refs):
                    period = all_ref[2 * at_i, q * CHUNK + at]
                    row = all_ref[2 * at_i + 1, q * CHUNK + at] * CR
                    total = sum_ref[period]
                    for r in range(CR):
                        coef = wide_ref[slot, r * modes:(r + 1) * modes, at * 128:(at + 1) * 128]
                        total += coef * lat_ref[row + r]
                    sum_ref[period] = total
        return carry

    if no <= 4:
        for at in range(no // ways):
            group(at, 0)
    else:
        lax.fori_loop(0, no // ways, group, 0)
    for p in range(periods):
        vector = field_ref[p] * scale
        if not last:
            vector_ref[p] = vector
        rest = tree_sum(sum_ref[p] for sum_ref in sum_refs) - vector * gain
        if not first:
            rest -= prior_ref[p] * norm
        next_ref[p] = rest
    for l in range(per_dev):
        row_ref[l] = field_ref[own * per_dev + l] * scale
    if last:
        out_ref[...] = fold(next_ref)
        for l in range(per_dev):
            mine_ref[l] = next_ref[own * per_dev + l]
    else:
        forward(dims, next_ref, lat_ref, foot_ref, ids_ref, out_ref)


def finish_kernel(factor, sums, *refs):
    sum_refs, refs = refs[:sums], refs[sums:]
    row_refs, refs = refs[:STEPS], refs[STEPS:]
    mine_ref, refs = refs[0], refs[1:]
    alphas, refs = refs[:STEPS], refs[STEPS:]
    norms, refs = refs[:STEPS - 1], refs[STEPS - 1:]
    out_ref, coef_ref = refs
    norm = jnp.sqrt(jnp.sum(added(sum_refs, ROWS), keepdims=True))
    for k in range(STEPS):
        out_ref[k] = row_refs[k][...] * factor
    out_ref[STEPS] = mine_ref[...] * (factor / norm)
    row = lax.broadcasted_iota(jnp.int32, coef_ref.shape, 0)
    col = lax.broadcasted_iota(jnp.int32, coef_ref.shape, 1)
    coefs = jnp.zeros(coef_ref.shape, F32)
    for k in range(STEPS):
        beta = norms[k][0:1, 0:1] if k < STEPS - 1 else norm
        coefs = jnp.where((row == 0) & (col == k), alphas[k][0:1, 0:1], coefs)
        coefs = jnp.where((row == 1) & (col == k), beta, coefs)
    coef_ref[...] = coefs


def permuted(size):
    return size <= 4 and size & (size - 1) == 0


def share(array, axis):
    size = lax.axis_size(axis)
    if not permuted(size):
        return [swap(jnp.broadcast_to(array[None], (size,) + array.shape), axis).reshape(-1, array.shape[1])]
    return [array] + [lax.ppermute(array, axis, [(d, d ^ s) for d in range(size)]) for s in range(1, size)]


def addends(array, axis):
    size = lax.axis_size(axis)
    if size != 8:
        return [swap(jnp.broadcast_to(array[None], (size,) + array.shape), axis).reshape(-1, array.shape[1])]
    other = lax.ppermute(array, axis, [(d, d ^ 1) for d in range(size)])
    both = call(add_kernel, jax.ShapeDtypeStruct(array.shape, F32), [VMEM] * 2, array, other)
    return [both] + [lax.ppermute(both, axis, [(d, d ^ s) for d in range(size)]) for s in (2, 4, 6)]


def swap(array, axis):
    return lax.all_to_all(array, axis, split_axis=0, concat_axis=0, tiled=True)


def body(start, lat_mats, footprints, blk_sub, blk_off, counts, rinv):
    per_dev, held, lat_rows = start.shape
    nc = lax.axis_size("cell")
    no = lax.axis_size("obs")
    lon_cols = held * nc
    band = lat_rows // nc
    groups = band // CR
    nb, ob, _ = footprints.shape
    subs = counts.shape[0]
    modes = -(-held // 16) * 16
    mine = nc * nb
    periods = per_dev * no
    dims = (nc, nb, modes, groups, band)
    shape = functools.partial(jax.ShapeDtypeStruct, dtype=F32)

    high, low = lon_table(lon_cols, nc, modes)
    if modes != held:
        start = jnp.pad(start, ((0, 0), (0, modes - held), (0, 0)))
        lat_mats = jnp.pad(lat_mats, ((0, modes - held), (0, 0), (0, 0)))
    place = lax.axis_index(("obs", "cell")).astype(jnp.int32).reshape(1)

    start = start.reshape(per_dev * modes, lat_rows)
    near = share(start, "obs")
    foot_rows = nb * CR * modes
    hats, weights = call(
        functools.partial(transform_kernel, dims),
        (jax.ShapeDtypeStruct((nc, foot_rows + 16, ob), BF16), shape((subs, ob))),
        [ANY] * 8,
        place, jnp.asarray(high), jnp.asarray(low), footprints, blk_off, blk_sub, counts, rinv.reshape(subs, ob),
        scratch=[
            pltpu.VMEM(high.shape, BF16),
            pltpu.VMEM(low.shape, BF16),
            pltpu.VMEM(footprints.shape, BF16),
            pltpu.SMEM((nb,), jnp.int32),
            pltpu.SMEM((nb,), jnp.int32),
            pltpu.SMEM((subs,), jnp.int32),
            pltpu.VMEM((subs, ob), F32),
            pltpu.SMEM((1,), jnp.int32),
            pltpu.SemaphoreType.DMA((8,)),
        ],
        limit=60,
    )
    came = swap(hats, "cell")
    lat, start, _ = lax.optimization_barrier((lat_mats, start, weights))
    lat, start, pick = call(
        fetch_kernel,
        (
            shape((lat_rows, modes, lat_rows)),
            shape(start.shape),
            jax.ShapeDtypeStruct((TERMS * CHUNK, CHUNK * 128), BF16),
        ),
        [ANY] * 2,
        lat, start,
        scratch=[pltpu.SemaphoreType.DMA((modes + 1,))],
        limit=50,
        cost=pl.CostEstimate(flops=0, transcendentals=0, bytes_accessed=8 * (lat.size + start.size)),
    )
    if permuted(no):
        near[0] = start

    field_shape = shape((periods, modes, lat_rows))
    small = shape((ROWS, 128))
    own_shape = shape((per_dev, modes, lat_rows))
    sims, field, foot, ids, choose, tail = call(
        functools.partial(first_kernel, dims, no),
        (
            shape((subs + ROWS, ob)),
            field_shape,
            jax.ShapeDtypeStruct((nc, foot_rows, ob), BF16),
            jax.ShapeDtypeStruct((nc, 128), jnp.int32),
            jax.ShapeDtypeStruct((mine, TERMS * subs), BF16),
            shape((ROWS, 128)),
        ),
        [VMEM] * (2 + len(near)),
        lat, came, *near,
        scratch=[pltpu.SMEM((nc, 128), jnp.int32), pltpu.SemaphoreType.DMA],
    )
    ways = min(no, WAYS)
    rows, alphas, norms = [], [], []
    vector = None
    for step in range(STEPS):
        first, last = step == 0, step == STEPS - 1
        parts = addends(sims, "cell")
        tails = [tail] if first else []
        coefs, norm = call(
            functools.partial(adjoint_kernel, dims, len(tails)),
            (shape((mine + subs + (ROWS if first else 0), 128)), small),
            [VMEM] * (3 + len(tails) + len(parts)),
            choose, weights, foot, *tails, *parts,
            scratch=[pltpu.VMEM((mine, ob), F32)],
        )
        coefs = share(coefs, "obs")
        if first:
            every = call(
                functools.partial(every_kernel, dims, no, mine + subs),
                jax.ShapeDtypeStruct((2 * no, 128), jnp.int32),
                [VMEM] * len(coefs),
                *coefs,
            )
        before = [] if first else [vector]
        sims, row, field, *vector, alpha = call(
            functools.partial(image_kernel, dims, no, first, last),
            (
                shape((ROWS if last else subs + ROWS, 128)),
                own_shape,
                own_shape if last else field_shape,
                *([] if last else [field_shape]),
                small,
            ),
            [VMEM] * (7 + len(before) + len(coefs)),
            ids, every, lat, foot, pick, norm, field, *before, *coefs,
            scratch=[pltpu.VMEM(field_shape.shape, F32)] * last
            + [pltpu.VMEM((no, mine, 128), F32)]
            + [pltpu.VMEM(field_shape.shape, F32)] * ways
            + [pltpu.VMEM((no * mine // CHUNK if no <= 4 else ways, CR * modes, CHUNK * 128), F32)]
            + [pltpu.SMEM((nc, 128), jnp.int32), pltpu.SMEM((2 * no, 128), jnp.int32)]
            + [pltpu.SemaphoreType.DMA((2,))],
            limit=16,
        )
        vector = None if last else vector[0]
        rows.append(row)
        alphas.append(alpha)
        norms.append(norm)
    factor = math.sqrt(periods * lon_cols * lat_rows)
    parts = addends(sims, "cell")
    krylov, coeffs = call(
        functools.partial(finish_kernel, factor, len(parts)),
        (shape((STEPS + 1, per_dev, modes, lat_rows)), shape((2, STEPS))),
        [VMEM] * (len(parts) + STEPS + 1 + STEPS + STEPS - 1),
        *parts, *rows, field, *alphas, *norms[1:],
    )
    return krylov[:, :, :held], coeffs


def solution(mesh):
    placed = (
        P("obs", "cell", None),
        P("cell", None, None),
        P(("obs", "cell"), None, None),
        P(("obs", "cell")),
        P(("obs", "cell")),
        P("obs"),
        P("obs"),
    )
    return jax.shard_map(
        body,
        mesh=mesh,
        in_specs=placed,
        out_specs=(P(None, "obs", "cell", None), P()),
        check_vma=False,
    )
```

```python
import functools
import math

import jax
import jax.numpy as jnp
import ml_dtypes
import numpy as np
from jax import lax
from jax.experimental import pallas as pl
from jax.experimental.pallas import tpu as pltpu
from jax.sharding import PartitionSpec as P

CR = 2
WAYS = 2
CHUNK = 16
TERMS = 3
STEPS = 3
ROWS = 8
VMEM = pl.BlockSpec(memory_space=pltpu.VMEM)
SMEM = pl.BlockSpec(memory_space=pltpu.SMEM)
ANY = pl.BlockSpec(memory_space=pl.ANY)
F32 = jnp.float32
BF16 = jnp.bfloat16


def lon_table(order, parts, padded):
    index = np.arange(order)
    half = order // 2
    freq = np.where(index <= half, index, index - half)[:, None]
    phase = (freq * index[None, :] % order) * (2.0 * math.pi / order)
    factor = np.where((index == 0) | (index == half), math.sqrt(1.0 / order), math.sqrt(2.0 / order))
    table = np.where(index[:, None] <= half, np.cos(phase), np.sin(phase)) * factor[:, None]
    table = table.reshape(parts, order // parts, order)
    table = np.pad(table, ((0, 0), (0, padded - order // parts), (0, 0))).reshape(parts * padded, order)
    high = table.astype(np.float32).astype(ml_dtypes.bfloat16)
    low = (table - high.astype(np.float64)).astype(np.float32).astype(ml_dtypes.bfloat16)
    return high, low


def call(kernel, outs, specs, *args, scratch=(), limit=8, cost=None):
    return pl.pallas_call(
        kernel,
        out_shape=outs,
        in_specs=specs,
        out_specs=jax.tree.map(lambda _: VMEM, outs),
        scratch_shapes=scratch,
        cost_estimate=cost,
        compiler_params=pltpu.CompilerParams(vmem_limit_bytes=limit * 1024 * 1024),
    )(*args)


def tree_sum(parts):
    parts = list(parts)
    while len(parts) > 1:
        parts = [sum(parts[at:at + 2][1:], parts[at]) for at in range(0, len(parts), 2)]
    return parts[0]


def transform_kernel(dims, place_any, high_any, low_any, foot_any, off_any, sub_any, count_any, rinv_any, *refs):
    nc, nb, modes, groups, band = dims
    out_ref, weight_ref, high_ref, low_ref, foot_ref, off_ref, sub_ref, count_ref, rinv_ref, place_ref, sems = refs
    copies = [
        pltpu.make_async_copy(source, target, sems.at[at])
        for at, (source, target) in enumerate(
            [
                (foot_any, foot_ref),
                (high_any, high_ref),
                (low_any, low_ref),
                (off_any, off_ref),
                (sub_any, sub_ref),
                (count_any, count_ref),
                (rinv_any, rinv_ref),
                (place_any, place_ref),
            ]
        )
    ]
    for copy in copies:
        copy.start()
    for copy in copies:
        copy.wait()
    cell = place_ref[0] % nc
    obs = place_ref[0] // nc
    ob = foot_ref.shape[1]
    lon = high_ref.shape[1]
    contract = (((1,), (1,)), ((), ()))
    for r in range(CR):
        foot = foot_ref[:, :, r * lon:(r + 1) * lon].reshape(nb * ob, lon)
        hat = lax.dot_general(high_ref[...], foot, contract, preferred_element_type=F32)
        hat += lax.dot_general(low_ref[...], foot, contract, preferred_element_type=F32)
        hat = hat.astype(BF16)
        for b in range(nb):
            at = (b * CR + r) * modes
            for c in range(nc):
                out_ref[c, at:at + modes, :] = hat[c * modes:(c + 1) * modes, b * ob:(b + 1) * ob]
    lane = lax.broadcasted_iota(jnp.int32, (16, ob), 1)
    ids = jnp.zeros((16, ob), F32)
    for b in range(nb):
        off = off_ref[b]
        values = (off // groups, cell * (band // CR) + off % groups, sub_ref[b])
        for at, value in enumerate(values):
            ids = jnp.where(lane == at * nb + b, value.astype(F32), ids)
    ids = jnp.where(lane == 3 * nb, obs.astype(F32), ids).astype(BF16)
    for c in range(nc):
        out_ref[c, nb * CR * modes:, :] = ids
    row = lax.broadcasted_iota(jnp.int32, weight_ref.shape, 0)
    limit = jnp.zeros(weight_ref.shape, jnp.int32)
    for s in range(weight_ref.shape[0]):
        limit = jnp.where(row == s, count_ref[s], limit)
    lane = lax.broadcasted_iota(jnp.int32, weight_ref.shape, 1)
    weight_ref[...] = jnp.where(lane < limit, rinv_ref[...], 0.0)


def fetch_kernel(lat_any, start_any, lat_ref, start_ref, pick_ref, sems):
    modes = lat_any.shape[0]
    copies = [pltpu.make_async_copy(lat_any.at[m], lat_ref.at[:, m, :], sems.at[m]) for m in range(modes)]
    copies.append(pltpu.make_async_copy(start_any, start_ref, sems.at[modes]))
    for copy in copies:
        copy.start()
    line = lax.broadcasted_iota(jnp.int32, pick_ref.shape, 0)
    lane = lax.broadcasted_iota(jnp.int32, pick_ref.shape, 1)
    pick_ref[...] = jnp.where(line % CHUNK == lane // 128, 1.0, 0.0).astype(BF16)
    for copy in copies:
        copy.wait()


def fold(ref):
    periods, modes, _ = ref.shape
    total = jnp.zeros((ROWS, ref.shape[2]), F32)
    for p in range(periods):
        for at in range(0, modes, ROWS):
            part = ref[p, at:at + ROWS, :]
            total += part * part
    return total


def split(values):
    terms = []
    for _ in range(TERMS):
        terms.append(values.astype(BF16).astype(F32))
        values = values - terms[-1]
    return jnp.concatenate(terms, axis=0).astype(BF16)


def forward(dims, field_ref, lat_ref, foot_ref, ids_ref, place_ref, prod_ref, sim_ref):
    nc, nb, modes, groups, band = dims
    subs = sim_ref.shape[0] - ROWS
    for j in range(nc):
        for b in range(nb):
            period = ids_ref[j, b]
            row = ids_ref[j, nb + b] * CR
            total = None
            for r in range(CR):
                column = jnp.sum(lat_ref[row + r] * field_ref[period], axis=1, keepdims=True)
                at = (b * CR + r) * modes
                term = foot_ref[j, at:at + modes, :].astype(F32) * column
                total = term if total is None else total + term
            prod_ref[j * nb + b:j * nb + b + 1, :] = jnp.sum(total, axis=0, keepdims=True)
    sim_ref[:subs, :] = jnp.dot(place_ref[...], split(prod_ref[...]), preferred_element_type=F32)
    sim_ref[subs:, :] = fold(field_ref)


def pieces(refs, size, rows):
    found = []
    for ref in refs:
        found += [ref.at[at:at + rows] for at in range(0, ref.shape[0], rows)]
    assert len(found) == size
    return found


def added(refs, rows):
    return tree_sum(ref[...] for ref in pieces(refs, sum(ref.shape[0] for ref in refs) // rows, rows))


def add_kernel(one_ref, other_ref, out_ref):
    out_ref[...] = one_ref[...] + other_ref[...]


def first_kernel(dims, no, lat_ref, came_ref, *refs):
    nc, nb, modes, _, _ = dims
    near_refs, refs = refs[:-10], refs[-10:]
    out_ref, field_ref, foot_ref, all_ref, choose_ref, place_ref, tail_ref, ids_ref, prod_ref, sem = refs
    rows = nb * CR * modes
    for j in range(nc):
        all_ref[j:j + 1, :] = came_ref[j, rows:rows + 16, :].astype(F32)[0:1].astype(jnp.int32)
    copy = pltpu.make_async_copy(all_ref, ids_ref, sem)
    copy.start()
    for j in range(nc):
        foot_ref[j] = came_ref[j, :rows, :]
    per_dev = field_ref.shape[0] // no
    copy.wait()
    own = ids_ref[0, 3 * nb]
    for s, near_ref in enumerate(pieces(near_refs, no, per_dev * modes)):
        for l in range(per_dev):
            field_ref[((own ^ s) if permuted(no) else s) * per_dev + l] = near_ref[l * modes:(l + 1) * modes, :]
    line = lax.broadcasted_iota(jnp.int32, choose_ref.shape, 0)
    lane = lax.broadcasted_iota(jnp.int32, choose_ref.shape, 1)
    tail_line = lax.broadcasted_iota(jnp.int32, tail_ref.shape, 0)
    tail_lane = lax.broadcasted_iota(jnp.int32, tail_ref.shape, 1)
    place_line = lax.broadcasted_iota(jnp.int32, place_ref.shape, 0)
    place_lane = lax.broadcasted_iota(jnp.int32, place_ref.shape, 1) % (nc * nb)
    subs = jnp.zeros(choose_ref.shape, jnp.int32)
    place = jnp.zeros(place_ref.shape, jnp.int32)
    tail = jnp.zeros(tail_ref.shape, jnp.int32)
    for j in range(nc):
        for b in range(nb):
            subs = jnp.where(line == j * nb + b, ids_ref[j, 2 * nb + b], subs)
            place = jnp.where(place_lane == j * nb + b, ids_ref[j, 2 * nb + b], place)
            value = jnp.where(tail_line == 0, ids_ref[j, b], ids_ref[j, nb + b])
            tail = jnp.where(tail_lane == j * nb + b, value, tail)
    choose_ref[...] = jnp.where(lane % (choose_ref.shape[1] // TERMS) == subs, 1.0, 0.0).astype(BF16)
    place_ref[...] = jnp.where(place_line == place, 1.0, 0.0).astype(BF16)
    tail_ref[...] = tail.astype(F32)
    forward(dims, field_ref, lat_ref, foot_ref, ids_ref, place_ref, prod_ref, out_ref)


def adjoint_kernel(dims, tails, choose_ref, weight_ref, foot_ref, *refs):
    nc, nb, modes, groups, band = dims
    tail_refs, refs = refs[:tails], refs[tails:]
    sim_refs, refs = refs[:-3], refs[-3:]
    out_ref, norm_ref, chosen_ref = refs
    subs = weight_ref.shape[0]
    mine = nc * nb
    total = added(sim_refs, subs + ROWS)
    norm = jnp.sqrt(jnp.sum(total[subs:], keepdims=True))
    norm_ref[...] = jnp.broadcast_to(norm, norm_ref.shape)
    scale = 1.0 / norm
    sim = total[:subs]
    weighted = sim * weight_ref[...]
    chosen_ref[...] = jnp.dot(choose_ref[...], split(weighted), preferred_element_type=F32)
    lane = lax.broadcasted_iota(jnp.int32, (modes, 128), 1)
    parts = [jnp.zeros((modes, 128), F32) for _ in range(CR)]
    for j in range(nc):
        for b in range(nb):
            at_t = j * nb + b
            chosen = chosen_ref[at_t:at_t + 1, :]
            for r in range(CR):
                at = (b * CR + r) * modes
                column = jnp.sum(foot_ref[j, at:at + modes, :].astype(F32) * chosen, axis=1, keepdims=True)
                parts[r] = jnp.where(lane == at_t, column, parts[r])
    rest = 128 - CR * modes
    if rest:
        parts.append(jnp.zeros((rest, 128), F32))
    rows = jnp.concatenate(parts, axis=0).T
    out_ref[:mine, :] = rows[:mine] * scale
    out_ref[mine:mine + subs, :] = (sim * scale) * (weighted * scale)
    for tail_ref in tail_refs:
        out_ref[mine + subs:, :] = tail_ref[...]


def every_kernel(dims, no, at, *refs):
    refs, out_ref = refs[:-1], refs[-1]
    rows = sum(ref.shape[0] for ref in refs) // no
    for s, ref in enumerate(pieces(refs, no, rows)):
        out_ref[2 * s:2 * s + 2, :] = ref[at:at + ROWS, :][0:2].astype(jnp.int32)


def widen(rows, pick_ref):
    return lax.dot_general(split(rows), pick_ref[...], (((0,), (0,)), ((), ())), preferred_element_type=F32)


def image_kernel(dims, no, first, last, ids_ref, all_ref, lat_ref, foot_ref, pick_ref, place_ref, norm_ref, field_ref, *refs):
    nc, nb, modes, groups, band = dims
    if not first:
        prior_ref, refs = refs[0], refs[1:]
    ways = min(no, WAYS)
    kept = 7 + 2 * ways
    coef_refs, refs = refs[:-kept], refs[-kept:]
    wide_refs, refs = refs[-ways:], refs[:-ways]
    sum_refs, refs = refs[-ways:], refs[:-ways]
    if last:
        out_ref, row_ref, mine_ref, alpha_ref, next_ref, prod_ref, held_ref = refs
    else:
        out_ref, row_ref, next_ref, vector_ref, alpha_ref, prod_ref, held_ref = refs
    mine = nc * nb
    periods = field_ref.shape[0]
    per_dev = row_ref.shape[0]
    subs = ROWS
    rows = sum(ref.shape[0] for ref in coef_refs) // no
    coef_refs = pieces(coef_refs, no, rows)
    for s in range(no):
        held_ref[s] = coef_refs[s][:mine, :]
    for sum_ref in sum_refs:
        sum_ref[...] = jnp.zeros_like(sum_ref)
    gain = jnp.sum(tree_sum(ref[mine:mine + subs, :] for ref in coef_refs), keepdims=True)
    alpha_ref[...] = jnp.broadcast_to(1.0 + gain, alpha_ref.shape)
    norm = norm_ref[0:1, :]
    scale = 1.0 / norm
    own = ids_ref[0, 3 * nb]

    def group(at, carry):
        found = [at * ways + i for i in range(ways)]
        if permuted(no):
            found = [own ^ at_i for at_i in found]
        for chunk in range(0, mine, CHUNK):
            helds = [held_ref[at_i, chunk:chunk + CHUNK, :] for at_i in found]
            for held, wide_ref in zip(helds, wide_refs):
                wide_ref[...] = widen(held[:, :modes], pick_ref)
            columns = [held.T for held in helds]
            for at_t in range(CHUNK):
                for at_i, wide_ref, column, sum_ref in zip(found, wide_refs, columns, sum_refs):
                    period = all_ref[2 * at_i, chunk + at_t]
                    row = all_ref[2 * at_i + 1, chunk + at_t] * CR
                    total = sum_ref[period] + wide_ref[:, at_t * 128:(at_t + 1) * 128] * lat_ref[row]
                    for r in range(1, CR):
                        total += column[r * modes:(r + 1) * modes, at_t:at_t + 1] * lat_ref[row + r]
                    sum_ref[period] = total
        return carry

    if no <= 4:
        for at in range(no // ways):
            group(at, 0)
    else:
        lax.fori_loop(0, no // ways, group, 0)
    for p in range(periods):
        vector = field_ref[p] * scale
        if not last:
            vector_ref[p] = vector
        rest = tree_sum(sum_ref[p] for sum_ref in sum_refs) - vector * gain
        if not first:
            rest -= prior_ref[p] * norm
        next_ref[p] = rest
    for l in range(per_dev):
        row_ref[l] = field_ref[own * per_dev + l] * scale
    if last:
        out_ref[...] = fold(next_ref)
        for l in range(per_dev):
            mine_ref[l] = next_ref[own * per_dev + l]
    else:
        forward(dims, next_ref, lat_ref, foot_ref, ids_ref, place_ref, prod_ref, out_ref)


def finish_kernel(factor, sums, *refs):
    sum_refs, refs = refs[:sums], refs[sums:]
    row_refs, refs = refs[:STEPS], refs[STEPS:]
    mine_ref, refs = refs[0], refs[1:]
    alphas, refs = refs[:STEPS], refs[STEPS:]
    norms, refs = refs[:STEPS - 1], refs[STEPS - 1:]
    out_ref, coef_ref = refs
    norm = jnp.sqrt(jnp.sum(added(sum_refs, ROWS), keepdims=True))
    for k in range(STEPS):
        out_ref[k] = row_refs[k][...] * factor
    out_ref[STEPS] = mine_ref[...] * (factor / norm)
    row = lax.broadcasted_iota(jnp.int32, coef_ref.shape, 0)
    col = lax.broadcasted_iota(jnp.int32, coef_ref.shape, 1)
    coefs = jnp.zeros(coef_ref.shape, F32)
    for k in range(STEPS):
        beta = norms[k][0:1, 0:1] if k < STEPS - 1 else norm
        coefs = jnp.where((row == 0) & (col == k), alphas[k][0:1, 0:1], coefs)
        coefs = jnp.where((row == 1) & (col == k), beta, coefs)
    coef_ref[...] = coefs


def permuted(size):
    return size <= 4 and size & (size - 1) == 0


def share(array, axis):
    size = lax.axis_size(axis)
    if not permuted(size):
        return [swap(jnp.broadcast_to(array[None], (size,) + array.shape), axis).reshape(-1, array.shape[1])]
    return [array] + [lax.ppermute(array, axis, [(d, d ^ s) for d in range(size)]) for s in range(1, size)]


def addends(array, axis):
    size = lax.axis_size(axis)
    if size != 8:
        return [swap(jnp.broadcast_to(array[None], (size,) + array.shape), axis).reshape(-1, array.shape[1])]
    other = lax.ppermute(array, axis, [(d, d ^ 1) for d in range(size)])
    both = call(add_kernel, jax.ShapeDtypeStruct(array.shape, F32), [VMEM] * 2, array, other)
    return [both] + [lax.ppermute(both, axis, [(d, d ^ s) for d in range(size)]) for s in (2, 4, 6)]


def swap(array, axis):
    return lax.all_to_all(array, axis, split_axis=0, concat_axis=0, tiled=True)


def body(start, lat_mats, footprints, blk_sub, blk_off, counts, rinv):
    per_dev, held, lat_rows = start.shape
    nc = lax.axis_size("cell")
    no = lax.axis_size("obs")
    lon_cols = held * nc
    band = lat_rows // nc
    groups = band // CR
    nb, ob, _ = footprints.shape
    subs = counts.shape[0]
    modes = -(-held // 16) * 16
    mine = nc * nb
    periods = per_dev * no
    dims = (nc, nb, modes, groups, band)
    shape = functools.partial(jax.ShapeDtypeStruct, dtype=F32)

    high, low = lon_table(lon_cols, nc, modes)
    if modes != held:
        start = jnp.pad(start, ((0, 0), (0, modes - held), (0, 0)))
        lat_mats = jnp.pad(lat_mats, ((0, modes - held), (0, 0), (0, 0)))
    place = lax.axis_index(("obs", "cell")).astype(jnp.int32).reshape(1)

    start = start.reshape(per_dev * modes, lat_rows)
    near = share(start, "obs")
    foot_rows = nb * CR * modes
    hats, weights = call(
        functools.partial(transform_kernel, dims),
        (jax.ShapeDtypeStruct((nc, foot_rows + 16, ob), BF16), shape((subs, ob))),
        [ANY] * 8,
        place, jnp.asarray(high), jnp.asarray(low), footprints, blk_off, blk_sub, counts, rinv.reshape(subs, ob),
        scratch=[
            pltpu.VMEM(high.shape, BF16),
            pltpu.VMEM(low.shape, BF16),
            pltpu.VMEM(footprints.shape, BF16),
            pltpu.SMEM((nb,), jnp.int32),
            pltpu.SMEM((nb,), jnp.int32),
            pltpu.SMEM((subs,), jnp.int32),
            pltpu.VMEM((subs, ob), F32),
            pltpu.SMEM((1,), jnp.int32),
            pltpu.SemaphoreType.DMA((8,)),
        ],
        limit=60,
    )
    came = swap(hats, "cell")
    lat, start, _ = lax.optimization_barrier((lat_mats, start, weights))
    lat, start, pick = call(
        fetch_kernel,
        (
            shape((lat_rows, modes, lat_rows)),
            shape(start.shape),
            jax.ShapeDtypeStruct((TERMS * CHUNK, CHUNK * 128), BF16),
        ),
        [ANY] * 2,
        lat, start,
        scratch=[pltpu.SemaphoreType.DMA((modes + 1,))],
        limit=50,
        cost=pl.CostEstimate(flops=0, transcendentals=0, bytes_accessed=8 * (lat.size + start.size)),
    )
    if permuted(no):
        near[0] = start

    field_shape = shape((periods, modes, lat_rows))
    small = shape((ROWS, 128))
    own_shape = shape((per_dev, modes, lat_rows))
    sims, field, foot, ids, choose, spots, tail = call(
        functools.partial(first_kernel, dims, no),
        (
            shape((subs + ROWS, ob)),
            field_shape,
            jax.ShapeDtypeStruct((nc, foot_rows, ob), BF16),
            jax.ShapeDtypeStruct((nc, 128), jnp.int32),
            jax.ShapeDtypeStruct((mine, TERMS * subs), BF16),
            jax.ShapeDtypeStruct((subs, TERMS * mine), BF16),
            shape((ROWS, 128)),
        ),
        [VMEM] * (2 + len(near)),
        lat, came, *near,
        scratch=[pltpu.SMEM((nc, 128), jnp.int32), pltpu.VMEM((mine, ob), F32), pltpu.SemaphoreType.DMA],
    )
    ways = min(no, WAYS)
    rows, alphas, norms = [], [], []
    vector = None
    for step in range(STEPS):
        first, last = step == 0, step == STEPS - 1
        parts = addends(sims, "cell")
        tails = [tail] if first else []
        coefs, norm = call(
            functools.partial(adjoint_kernel, dims, len(tails)),
            (shape((mine + subs + (ROWS if first else 0), 128)), small),
            [VMEM] * (3 + len(tails) + len(parts)),
            choose, weights, foot, *tails, *parts,
            scratch=[pltpu.VMEM((mine, ob), F32)],
        )
        coefs = share(coefs, "obs")
        if first:
            every = call(
                functools.partial(every_kernel, dims, no, mine + subs),
                jax.ShapeDtypeStruct((2 * no, 128), jnp.int32),
                [VMEM] * len(coefs),
                *coefs,
            )
        before = [] if first else [vector]
        sims, row, field, *vector, alpha = call(
            functools.partial(image_kernel, dims, no, first, last),
            (
                shape((ROWS if last else subs + ROWS, 128)),
                own_shape,
                own_shape if last else field_shape,
                *([] if last else [field_shape]),
                small,
            ),
            [SMEM] * 2 + [VMEM] * (6 + len(before) + len(coefs)),
            ids, every, lat, foot, pick, spots, norm, field, *before, *coefs,
            scratch=[pltpu.VMEM(field_shape.shape, F32)] * last
            + [pltpu.VMEM((mine, ob), F32)]
            + [pltpu.VMEM((no, mine, 128), F32)]
            + [pltpu.VMEM(field_shape.shape, F32)] * ways
            + [pltpu.VMEM((modes, CHUNK * 128), F32)] * ways,
            limit=16,
        )
        vector = None if last else vector[0]
        rows.append(row)
        alphas.append(alpha)
        norms.append(norm)
    factor = math.sqrt(periods * lon_cols * lat_rows)
    parts = addends(sims, "cell")
    krylov, coeffs = call(
        functools.partial(finish_kernel, factor, len(parts)),
        (shape((STEPS + 1, per_dev, modes, lat_rows)), shape((2, STEPS))),
        [VMEM] * (len(parts) + STEPS + 1 + STEPS + STEPS - 1),
        *parts, *rows, field, *alphas, *norms[1:],
    )
    return krylov[:, :, :held], coeffs


def solution(mesh):
    placed = (
        P("obs", "cell", None),
        P("cell", None, None),
        P(("obs", "cell"), None, None),
        P(("obs", "cell")),
        P(("obs", "cell")),
        P("obs"),
        P("obs"),
    )
    return jax.shard_map(
        body,
        mesh=mesh,
        in_specs=placed,
        out_specs=(P(None, "obs", "cell", None), P()),
        check_vma=False,
    )
```

```python
import functools
import math

import jax
import jax.numpy as jnp
import ml_dtypes
import numpy as np
from jax import lax
from jax.experimental import pallas as pl
from jax.experimental.pallas import tpu as pltpu
from jax.sharding import PartitionSpec as P

CR = 2
WAYS = 4
CHUNK = 16
TERMS = 3
STEPS = 3
ROWS = 8
VMEM = pl.BlockSpec(memory_space=pltpu.VMEM)
SMEM = pl.BlockSpec(memory_space=pltpu.SMEM)
ANY = pl.BlockSpec(memory_space=pl.ANY)
F32 = jnp.float32
BF16 = jnp.bfloat16


def lon_table(order, parts, padded):
    index = np.arange(order)
    half = order // 2
    freq = np.where(index <= half, index, index - half)[:, None]
    phase = (freq * index[None, :] % order) * (2.0 * math.pi / order)
    factor = np.where((index == 0) | (index == half), math.sqrt(1.0 / order), math.sqrt(2.0 / order))
    table = np.where(index[:, None] <= half, np.cos(phase), np.sin(phase)) * factor[:, None]
    table = table.reshape(parts, order // parts, order)
    table = np.pad(table, ((0, 0), (0, padded - order // parts), (0, 0))).reshape(parts * padded, order)
    high = table.astype(np.float32).astype(ml_dtypes.bfloat16)
    low = (table - high.astype(np.float64)).astype(np.float32).astype(ml_dtypes.bfloat16)
    return high, low


def call(kernel, outs, specs, *args, scratch=(), limit=8, cost=None):
    return pl.pallas_call(
        kernel,
        out_shape=outs,
        in_specs=specs,
        out_specs=jax.tree.map(lambda _: VMEM, outs),
        scratch_shapes=scratch,
        cost_estimate=cost,
        compiler_params=pltpu.CompilerParams(vmem_limit_bytes=limit * 1024 * 1024),
    )(*args)


def tree_sum(parts):
    parts = list(parts)
    while len(parts) > 1:
        parts = [sum(parts[at:at + 2][1:], parts[at]) for at in range(0, len(parts), 2)]
    return parts[0]


def transform_kernel(dims, place_any, high_any, low_any, foot_any, off_any, sub_any, count_any, rinv_any, *refs):
    nc, nb, modes, groups, band = dims
    out_ref, weight_ref, high_ref, low_ref, foot_ref, off_ref, sub_ref, count_ref, rinv_ref, place_ref, sems = refs
    copies = [
        pltpu.make_async_copy(source, target, sems.at[at])
        for at, (source, target) in enumerate(
            [
                (foot_any, foot_ref),
                (high_any, high_ref),
                (low_any, low_ref),
                (off_any, off_ref),
                (sub_any, sub_ref),
                (count_any, count_ref),
                (rinv_any, rinv_ref),
                (place_any, place_ref),
            ]
        )
    ]
    for copy in copies:
        copy.start()
    for copy in copies:
        copy.wait()
    cell = place_ref[0] % nc
    obs = place_ref[0] // nc
    ob = foot_ref.shape[1]
    lon = high_ref.shape[1]
    contract = (((1,), (1,)), ((), ()))
    for r in range(CR):
        foot = foot_ref[:, :, r * lon:(r + 1) * lon].reshape(nb * ob, lon)
        hat = lax.dot_general(high_ref[...], foot, contract, preferred_element_type=F32)
        hat += lax.dot_general(low_ref[...], foot, contract, preferred_element_type=F32)
        hat = hat.astype(BF16)
        for b in range(nb):
            at = (b * CR + r) * modes
            for c in range(nc):
                out_ref[c, at:at + modes, :] = hat[c * modes:(c + 1) * modes, b * ob:(b + 1) * ob]
    lane = lax.broadcasted_iota(jnp.int32, (16, ob), 1)
    ids = jnp.zeros((16, ob), F32)
    for b in range(nb):
        off = off_ref[b]
        values = (off // groups, cell * (band // CR) + off % groups, sub_ref[b])
        for at, value in enumerate(values):
            ids = jnp.where(lane == at * nb + b, value.astype(F32), ids)
    ids = jnp.where(lane == 3 * nb, obs.astype(F32), ids).astype(BF16)
    for c in range(nc):
        out_ref[c, nb * CR * modes:, :] = ids
    row = lax.broadcasted_iota(jnp.int32, weight_ref.shape, 0)
    limit = jnp.zeros(weight_ref.shape, jnp.int32)
    for s in range(weight_ref.shape[0]):
        limit = jnp.where(row == s, count_ref[s], limit)
    lane = lax.broadcasted_iota(jnp.int32, weight_ref.shape, 1)
    weight_ref[...] = jnp.where(lane < limit, rinv_ref[...], 0.0)


def fetch_kernel(lat_any, start_any, lat_ref, start_ref, pick_ref, sems):
    modes = lat_any.shape[0]
    copies = [pltpu.make_async_copy(lat_any.at[m], lat_ref.at[:, m, :], sems.at[m]) for m in range(modes)]
    copies.append(pltpu.make_async_copy(start_any, start_ref, sems.at[modes]))
    for copy in copies:
        copy.start()
    line = lax.broadcasted_iota(jnp.int32, pick_ref.shape, 0)
    lane = lax.broadcasted_iota(jnp.int32, pick_ref.shape, 1)
    pick_ref[...] = jnp.where(line % CHUNK == lane // 128, 1.0, 0.0).astype(BF16)
    for copy in copies:
        copy.wait()


def fold(ref):
    periods, modes, _ = ref.shape
    total = jnp.zeros((ROWS, ref.shape[2]), F32)
    for p in range(periods):
        for at in range(0, modes, ROWS):
            part = ref[p, at:at + ROWS, :]
            total += part * part
    return total


def forward(dims, field_ref, lat_ref, foot_ref, ids_ref, sim_ref):
    nc, nb, modes, groups, band = dims
    subs = sim_ref.shape[0] - ROWS
    sim_ref[...] = jnp.zeros_like(sim_ref)
    for j in range(nc):
        for b in range(nb):
            period = ids_ref[j, b]
            row = ids_ref[j, nb + b] * CR
            sub = ids_ref[j, 2 * nb + b]
            total = None
            for r in range(CR):
                column = jnp.sum(lat_ref[row + r] * field_ref[period], axis=1, keepdims=True)
                at = (b * CR + r) * modes
                term = foot_ref[j, at:at + modes, :].astype(F32) * column
                total = term if total is None else total + term
            sim_ref[pl.ds(sub, 1), :] += jnp.sum(total, axis=0, keepdims=True)
    sim_ref[subs:, :] = fold(field_ref)


def pieces(refs, size, rows):
    found = []
    for ref in refs:
        found += [ref.at[at:at + rows] for at in range(0, ref.shape[0], rows)]
    assert len(found) == size
    return found


def added(refs, rows):
    return tree_sum(ref[...] for ref in pieces(refs, sum(ref.shape[0] for ref in refs) // rows, rows))


def add_kernel(one_ref, other_ref, out_ref):
    out_ref[...] = one_ref[...] + other_ref[...]


def first_kernel(dims, no, lat_ref, came_ref, *refs):
    nc, nb, modes, _, _ = dims
    near_refs, refs = refs[:-8], refs[-8:]
    out_ref, field_ref, foot_ref, all_ref, choose_ref, tail_ref, ids_ref, sem = refs
    rows = nb * CR * modes
    for j in range(nc):
        all_ref[j:j + 1, :] = came_ref[j, rows:rows + 16, :].astype(F32)[0:1].astype(jnp.int32)
    copy = pltpu.make_async_copy(all_ref, ids_ref, sem)
    copy.start()
    for j in range(nc):
        foot_ref[j] = came_ref[j, :rows, :]
    per_dev = field_ref.shape[0] // no
    copy.wait()
    own = ids_ref[0, 3 * nb]
    for s, near_ref in enumerate(pieces(near_refs, no, per_dev * modes)):
        for l in range(per_dev):
            field_ref[((own ^ s) if permuted(no) else s) * per_dev + l] = near_ref[l * modes:(l + 1) * modes, :]
    line = lax.broadcasted_iota(jnp.int32, choose_ref.shape, 0)
    lane = lax.broadcasted_iota(jnp.int32, choose_ref.shape, 1)
    tail_line = lax.broadcasted_iota(jnp.int32, tail_ref.shape, 0)
    tail_lane = lax.broadcasted_iota(jnp.int32, tail_ref.shape, 1)
    subs = jnp.zeros(choose_ref.shape, jnp.int32)
    tail = jnp.zeros(tail_ref.shape, jnp.int32)
    for j in range(nc):
        for b in range(nb):
            subs = jnp.where(line == j * nb + b, ids_ref[j, 2 * nb + b], subs)
            value = jnp.where(tail_line == 0, ids_ref[j, b], ids_ref[j, nb + b])
            tail = jnp.where(tail_lane == j * nb + b, value, tail)
    choose_ref[...] = jnp.where(lane % (choose_ref.shape[1] // TERMS) == subs, 1.0, 0.0).astype(BF16)
    tail_ref[...] = tail.astype(F32)
    forward(dims, field_ref, lat_ref, foot_ref, ids_ref, out_ref)


def split(values):
    terms = []
    for _ in range(TERMS):
        terms.append(values.astype(BF16).astype(F32))
        values = values - terms[-1]
    return jnp.concatenate(terms, axis=0).astype(BF16)


def adjoint_kernel(dims, tails, choose_ref, weight_ref, foot_ref, *refs):
    nc, nb, modes, groups, band = dims
    tail_refs, refs = refs[:tails], refs[tails:]
    sim_refs, refs = refs[:-3], refs[-3:]
    out_ref, norm_ref, chosen_ref = refs
    subs = weight_ref.shape[0]
    mine = nc * nb
    total = added(sim_refs, subs + ROWS)
    norm = jnp.sqrt(jnp.sum(total[subs:], keepdims=True))
    norm_ref[...] = jnp.broadcast_to(norm, norm_ref.shape)
    scale = 1.0 / norm
    sim = total[:subs]
    weighted = sim * weight_ref[...]
    chosen_ref[...] = jnp.dot(choose_ref[...], split(weighted), preferred_element_type=F32)
    lane = lax.broadcasted_iota(jnp.int32, (modes, 128), 1)
    parts = [jnp.zeros((modes, 128), F32) for _ in range(CR)]
    for j in range(nc):
        for b in range(nb):
            at_t = j * nb + b
            chosen = chosen_ref[at_t:at_t + 1, :]
            for r in range(CR):
                at = (b * CR + r) * modes
                column = jnp.sum(foot_ref[j, at:at + modes, :].astype(F32) * chosen, axis=1, keepdims=True)
                parts[r] = jnp.where(lane == at_t, column, parts[r])
    rest = 128 - CR * modes
    if rest:
        parts.append(jnp.zeros((rest, 128), F32))
    rows = jnp.concatenate(parts, axis=0).T
    out_ref[:mine, :] = rows[:mine] * scale
    out_ref[mine:mine + subs, :] = (sim * scale) * (weighted * scale)
    for tail_ref in tail_refs:
        out_ref[mine + subs:, :] = tail_ref[...]


def every_kernel(dims, no, at, *refs):
    refs, out_ref = refs[:-1], refs[-1]
    rows = sum(ref.shape[0] for ref in refs) // no
    for s, ref in enumerate(pieces(refs, no, rows)):
        out_ref[2 * s:2 * s + 2, :] = ref[at:at + ROWS, :][0:2].astype(jnp.int32)


def image_kernel(dims, no, first, last, ids_ref, all_ref, lat_ref, foot_ref, pick_ref, norm_ref, field_ref, *refs):
    nc, nb, modes, groups, band = dims
    if not first:
        prior_ref, refs = refs[0], refs[1:]
    ways = min(no, WAYS)
    kept = 6 + ways
    coef_refs, refs = refs[:-kept], refs[-kept:]
    sum_refs, refs = refs[-ways:], refs[:-ways]
    if last:
        out_ref, row_ref, mine_ref, alpha_ref, next_ref, held_ref = refs
    else:
        out_ref, row_ref, next_ref, vector_ref, alpha_ref, held_ref = refs
    mine = nc * nb
    periods = field_ref.shape[0]
    per_dev = row_ref.shape[0]
    subs = ROWS
    rows = sum(ref.shape[0] for ref in coef_refs) // no
    coef_refs = pieces(coef_refs, no, rows)
    for s in range(no):
        held_ref[s] = coef_refs[s][:mine, :]
    for sum_ref in sum_refs:
        sum_ref[...] = jnp.zeros_like(sum_ref)
    gain = jnp.sum(tree_sum(ref[mine:mine + subs, :] for ref in coef_refs), keepdims=True)
    alpha_ref[...] = jnp.broadcast_to(1.0 + gain, alpha_ref.shape)
    norm = norm_ref[0:1, :]
    scale = 1.0 / norm
    own = ids_ref[0, 3 * nb]

    def group(at, carry):
        found = [at * ways + i for i in range(ways)]
        for chunk in range(0, mine, CHUNK):
            left = [split(held_ref[s, chunk:chunk + CHUNK, :]) for s in found]
            left = jnp.concatenate(left, axis=1)
            for pair in range(0, CHUNK, 2):
                wide = lax.dot_general(
                    left,
                    pick_ref[:, pair * 128:(pair + 2) * 128],
                    (((0,), (0,)), ((), ())),
                    preferred_element_type=F32,
                )
                for at_t in range(2):
                    for i, s in enumerate(found):
                        period = all_ref[2 * s, chunk + pair + at_t]
                        row = all_ref[2 * s + 1, chunk + pair + at_t] * CR
                        total = sum_refs[i][period]
                        for r in range(CR):
                            start = i * 128 + r * modes
                            coef = wide[start:start + modes, at_t * 128:(at_t + 1) * 128]
                            total += coef * lat_ref[row + r]
                        sum_refs[i][period] = total
        return carry

    if no <= 4:
        for at in range(no // ways):
            group(at, 0)
    else:
        lax.fori_loop(0, no // ways, group, 0)
    for p in range(periods):
        vector = field_ref[p] * scale
        if not last:
            vector_ref[p] = vector
        rest = tree_sum(sum_ref[p] for sum_ref in sum_refs) - vector * gain
        if not first:
            rest -= prior_ref[p] * norm
        next_ref[p] = rest
    for l in range(per_dev):
        row_ref[l] = field_ref[own * per_dev + l] * scale
    if last:
        out_ref[...] = fold(next_ref)
        for l in range(per_dev):
            mine_ref[l] = next_ref[own * per_dev + l]
    else:
        forward(dims, next_ref, lat_ref, foot_ref, ids_ref, out_ref)


def finish_kernel(factor, sums, *refs):
    sum_refs, refs = refs[:sums], refs[sums:]
    row_refs, refs = refs[:STEPS], refs[STEPS:]
    mine_ref, refs = refs[0], refs[1:]
    alphas, refs = refs[:STEPS], refs[STEPS:]
    norms, refs = refs[:STEPS - 1], refs[STEPS - 1:]
    out_ref, coef_ref = refs
    norm = jnp.sqrt(jnp.sum(added(sum_refs, ROWS), keepdims=True))
    for k in range(STEPS):
        out_ref[k] = row_refs[k][...] * factor
    out_ref[STEPS] = mine_ref[...] * (factor / norm)
    row = lax.broadcasted_iota(jnp.int32, coef_ref.shape, 0)
    col = lax.broadcasted_iota(jnp.int32, coef_ref.shape, 1)
    coefs = jnp.zeros(coef_ref.shape, F32)
    for k in range(STEPS):
        beta = norms[k][0:1, 0:1] if k < STEPS - 1 else norm
        coefs = jnp.where((row == 0) & (col == k), alphas[k][0:1, 0:1], coefs)
        coefs = jnp.where((row == 1) & (col == k), beta, coefs)
    coef_ref[...] = coefs


def permuted(size):
    return size <= 4 and size & (size - 1) == 0


def share(array, axis):
    size = lax.axis_size(axis)
    if not permuted(size):
        return [swap(jnp.broadcast_to(array[None], (size,) + array.shape), axis).reshape(-1, array.shape[1])]
    return [array] + [lax.ppermute(array, axis, [(d, d ^ s) for d in range(size)]) for s in range(1, size)]


def addends(array, axis):
    size = lax.axis_size(axis)
    if size != 8:
        return [swap(jnp.broadcast_to(array[None], (size,) + array.shape), axis).reshape(-1, array.shape[1])]
    other = lax.ppermute(array, axis, [(d, d ^ 1) for d in range(size)])
    both = call(add_kernel, jax.ShapeDtypeStruct(array.shape, F32), [VMEM] * 2, array, other)
    return [both] + [lax.ppermute(both, axis, [(d, d ^ s) for d in range(size)]) for s in (2, 4, 6)]


def swap(array, axis):
    return lax.all_to_all(array, axis, split_axis=0, concat_axis=0, tiled=True)


def body(start, lat_mats, footprints, blk_sub, blk_off, counts, rinv):
    per_dev, held, lat_rows = start.shape
    nc = lax.axis_size("cell")
    no = lax.axis_size("obs")
    lon_cols = held * nc
    band = lat_rows // nc
    groups = band // CR
    nb, ob, _ = footprints.shape
    subs = counts.shape[0]
    modes = -(-held // 16) * 16
    mine = nc * nb
    periods = per_dev * no
    dims = (nc, nb, modes, groups, band)
    shape = functools.partial(jax.ShapeDtypeStruct, dtype=F32)

    high, low = lon_table(lon_cols, nc, modes)
    if modes != held:
        start = jnp.pad(start, ((0, 0), (0, modes - held), (0, 0)))
        lat_mats = jnp.pad(lat_mats, ((0, modes - held), (0, 0), (0, 0)))
    place = lax.axis_index(("obs", "cell")).astype(jnp.int32).reshape(1)

    start = start.reshape(per_dev * modes, lat_rows)
    near = share(start, "obs")
    foot_rows = nb * CR * modes
    hats, weights = call(
        functools.partial(transform_kernel, dims),
        (jax.ShapeDtypeStruct((nc, foot_rows + 16, ob), BF16), shape((subs, ob))),
        [ANY] * 8,
        place, jnp.asarray(high), jnp.asarray(low), footprints, blk_off, blk_sub, counts, rinv.reshape(subs, ob),
        scratch=[
            pltpu.VMEM(high.shape, BF16),
            pltpu.VMEM(low.shape, BF16),
            pltpu.VMEM(footprints.shape, BF16),
            pltpu.SMEM((nb,), jnp.int32),
            pltpu.SMEM((nb,), jnp.int32),
            pltpu.SMEM((subs,), jnp.int32),
            pltpu.VMEM((subs, ob), F32),
            pltpu.SMEM((1,), jnp.int32),
            pltpu.SemaphoreType.DMA((8,)),
        ],
        limit=60,
    )
    came = swap(hats, "cell")
    lat, start, _ = lax.optimization_barrier((lat_mats, start, weights))
    lat, start, pick = call(
        fetch_kernel,
        (
            shape((lat_rows, modes, lat_rows)),
            shape(start.shape),
            jax.ShapeDtypeStruct((TERMS * CHUNK, CHUNK * 128), BF16),
        ),
        [ANY] * 2,
        lat, start,
        scratch=[pltpu.SemaphoreType.DMA((modes + 1,))],
        limit=50,
        cost=pl.CostEstimate(flops=0, transcendentals=0, bytes_accessed=8 * (lat.size + start.size)),
    )
    if permuted(no):
        near[0] = start

    field_shape = shape((periods, modes, lat_rows))
    small = shape((ROWS, 128))
    own_shape = shape((per_dev, modes, lat_rows))
    sims, field, foot, ids, choose, tail = call(
        functools.partial(first_kernel, dims, no),
        (
            shape((subs + ROWS, ob)),
            field_shape,
            jax.ShapeDtypeStruct((nc, foot_rows, ob), BF16),
            jax.ShapeDtypeStruct((nc, 128), jnp.int32),
            jax.ShapeDtypeStruct((mine, TERMS * subs), BF16),
            shape((ROWS, 128)),
        ),
        [VMEM] * (2 + len(near)),
        lat, came, *near,
        scratch=[pltpu.SMEM((nc, 128), jnp.int32), pltpu.SemaphoreType.DMA],
    )
    ways = min(no, WAYS)
    rows, alphas, norms = [], [], []
    vector = None
    for step in range(STEPS):
        first, last = step == 0, step == STEPS - 1
        parts = addends(sims, "cell")
        tails = [tail] if first else []
        coefs, norm = call(
            functools.partial(adjoint_kernel, dims, len(tails)),
            (shape((mine + subs + (ROWS if first else 0), 128)), small),
            [VMEM] * (3 + len(tails) + len(parts)),
            choose, weights, foot, *tails, *parts,
            scratch=[pltpu.VMEM((mine, ob), F32)],
        )
        coefs = share(coefs, "obs")
        if first:
            every = call(
                functools.partial(every_kernel, dims, no, mine + subs),
                jax.ShapeDtypeStruct((2 * no, 128), jnp.int32),
                [VMEM] * len(coefs),
                *coefs,
            )
        before = [] if first else [vector]
        sims, row, field, *vector, alpha = call(
            functools.partial(image_kernel, dims, no, first, last),
            (
                shape((ROWS if last else subs + ROWS, 128)),
                own_shape,
                own_shape if last else field_shape,
                *([] if last else [field_shape]),
                small,
            ),
            [SMEM] * 2 + [VMEM] * (5 + len(before) + len(coefs)),
            ids, every, lat, foot, pick, norm, field, *before, *coefs,
            scratch=[pltpu.VMEM(field_shape.shape, F32)] * last
            + [pltpu.VMEM((no, mine, 128), F32)]
            + [pltpu.VMEM(field_shape.shape, F32)] * ways,
            limit=16,
        )
        vector = None if last else vector[0]
        rows.append(row)
        alphas.append(alpha)
        norms.append(norm)
    factor = math.sqrt(periods * lon_cols * lat_rows)
    parts = addends(sims, "cell")
    krylov, coeffs = call(
        functools.partial(finish_kernel, factor, len(parts)),
        (shape((STEPS + 1, per_dev, modes, lat_rows)), shape((2, STEPS))),
        [VMEM] * (len(parts) + STEPS + 1 + STEPS + STEPS - 1),
        *parts, *rows, field, *alphas, *norms[1:],
    )
    return krylov[:, :, :held], coeffs


def solution(mesh):
    placed = (
        P("obs", "cell", None),
        P("cell", None, None),
        P(("obs", "cell"), None, None),
        P(("obs", "cell")),
        P(("obs", "cell")),
        P("obs"),
        P("obs"),
    )
    return jax.shard_map(
        body,
        mesh=mesh,
        in_specs=placed,
        out_specs=(P(None, "obs", "cell", None), P()),
        check_vma=False,
    )
```

```python
import functools
import math

import jax
import jax.numpy as jnp
import ml_dtypes
import numpy as np
from jax import lax
from jax.experimental import pallas as pl
from jax.experimental.pallas import tpu as pltpu
from jax.sharding import PartitionSpec as P

CR = 2
WAYS = 4
PARTS = 4
CHUNK = 16
TERMS = 3
STEPS = 3
ROWS = 8
VMEM = pl.BlockSpec(memory_space=pltpu.VMEM)
SMEM = pl.BlockSpec(memory_space=pltpu.SMEM)
ANY = pl.BlockSpec(memory_space=pl.ANY)
F32 = jnp.float32
BF16 = jnp.bfloat16


def lon_table(order, parts, padded):
    index = np.arange(order)
    half = order // 2
    freq = np.where(index <= half, index, index - half)[:, None]
    phase = (freq * index[None, :] % order) * (2.0 * math.pi / order)
    factor = np.where((index == 0) | (index == half), math.sqrt(1.0 / order), math.sqrt(2.0 / order))
    table = np.where(index[:, None] <= half, np.cos(phase), np.sin(phase)) * factor[:, None]
    table = table.reshape(parts, order // parts, order)
    table = np.pad(table, ((0, 0), (0, padded - order // parts), (0, 0))).reshape(parts * padded, order)
    high = table.astype(np.float32).astype(ml_dtypes.bfloat16)
    low = (table - high.astype(np.float64)).astype(np.float32).astype(ml_dtypes.bfloat16)
    return high, low


def call(kernel, outs, specs, *args, scratch=(), limit=8, cost=None):
    return pl.pallas_call(
        kernel,
        out_shape=outs,
        in_specs=specs,
        out_specs=jax.tree.map(lambda _: VMEM, outs),
        scratch_shapes=scratch,
        cost_estimate=cost,
        compiler_params=pltpu.CompilerParams(vmem_limit_bytes=limit * 1024 * 1024),
    )(*args)


def tree_sum(parts):
    parts = list(parts)
    while len(parts) > 1:
        parts = [sum(parts[at:at + 2][1:], parts[at]) for at in range(0, len(parts), 2)]
    return parts[0]


def transform_kernel(dims, place_any, high_any, low_any, foot_any, off_any, sub_any, count_any, rinv_any, *refs):
    nc, nb, modes, groups, band = dims
    out_ref, weight_ref, high_ref, low_ref, foot_ref, off_ref, sub_ref, count_ref, rinv_ref, place_ref, sems = refs
    copies = [
        pltpu.make_async_copy(source, target, sems.at[at])
        for at, (source, target) in enumerate(
            [
                (foot_any, foot_ref),
                (high_any, high_ref),
                (low_any, low_ref),
                (off_any, off_ref),
                (sub_any, sub_ref),
                (count_any, count_ref),
                (rinv_any, rinv_ref),
                (place_any, place_ref),
            ]
        )
    ]
    for copy in copies:
        copy.start()
    for copy in copies:
        copy.wait()
    cell = place_ref[0] % nc
    obs = place_ref[0] // nc
    ob = foot_ref.shape[1]
    lon = high_ref.shape[1]
    contract = (((1,), (1,)), ((), ()))
    for r in range(CR):
        foot = foot_ref[:, :, r * lon:(r + 1) * lon].reshape(nb * ob, lon)
        hat = lax.dot_general(high_ref[...], foot, contract, preferred_element_type=F32)
        hat += lax.dot_general(low_ref[...], foot, contract, preferred_element_type=F32)
        hat = hat.astype(BF16)
        for b in range(nb):
            at = (b * CR + r) * modes
            for c in range(nc):
                out_ref[c, at:at + modes, :] = hat[c * modes:(c + 1) * modes, b * ob:(b + 1) * ob]
    lane = lax.broadcasted_iota(jnp.int32, (16, ob), 1)
    ids = jnp.zeros((16, ob), F32)
    for b in range(nb):
        off = off_ref[b]
        values = (off // groups, cell * (band // CR) + off % groups, sub_ref[b])
        for at, value in enumerate(values):
            ids = jnp.where(lane == at * nb + b, value.astype(F32), ids)
    ids = jnp.where(lane == 3 * nb, obs.astype(F32), ids).astype(BF16)
    for c in range(nc):
        out_ref[c, nb * CR * modes:, :] = ids
    row = lax.broadcasted_iota(jnp.int32, weight_ref.shape, 0)
    limit = jnp.zeros(weight_ref.shape, jnp.int32)
    for s in range(weight_ref.shape[0]):
        limit = jnp.where(row == s, count_ref[s], limit)
    lane = lax.broadcasted_iota(jnp.int32, weight_ref.shape, 1)
    weight_ref[...] = jnp.where(lane < limit, rinv_ref[...], 0.0)


def fetch_kernel(lat_any, start_any, lat_ref, start_ref, pick_ref, sems):
    modes = lat_any.shape[0]
    copies = [pltpu.make_async_copy(lat_any.at[m], lat_ref.at[:, m, :], sems.at[m]) for m in range(modes)]
    copies.append(pltpu.make_async_copy(start_any, start_ref, sems.at[modes]))
    for copy in copies:
        copy.start()
    line = lax.broadcasted_iota(jnp.int32, pick_ref.shape, 0)
    lane = lax.broadcasted_iota(jnp.int32, pick_ref.shape, 1)
    pick_ref[...] = jnp.where(line % CHUNK == lane // 128, 1.0, 0.0).astype(BF16)
    for copy in copies:
        copy.wait()


def fold(ref):
    periods, modes, _ = ref.shape
    total = jnp.zeros((ROWS, ref.shape[2]), F32)
    for p in range(periods):
        for at in range(0, modes, ROWS):
            part = ref[p, at:at + ROWS, :]
            total += part * part
    return total


def forward(dims, field_ref, lat_ref, foot_ref, ids_ref, part_refs, sim_ref):
    nc, nb, modes, groups, band = dims
    subs = sim_ref.shape[0] - ROWS
    for part_ref in part_refs:
        part_ref[...] = jnp.zeros_like(part_ref)
    found = []
    for j in range(nc):
        for b in range(nb):
            period = ids_ref[j, b]
            row = ids_ref[j, nb + b] * CR
            sub = ids_ref[j, 2 * nb + b]
            total = None
            for r in range(CR):
                column = jnp.sum(lat_ref[row + r] * field_ref[period], axis=1, keepdims=True)
                at = (b * CR + r) * modes
                term = foot_ref[j, at:at + modes, :].astype(F32) * column
                total = term if total is None else total + term
            found.append((sub, jnp.sum(total, axis=0, keepdims=True)))
    sim_ref[subs:, :] = fold(field_ref)
    for at in range(0, len(found), len(part_refs)):
        here = list(zip(part_refs, found[at:at + len(part_refs)]))
        sums = [part_ref[pl.ds(sub, 1), :] + line for part_ref, (sub, line) in here]
        for (part_ref, (sub, _)), line in zip(here, sums):
            part_ref[pl.ds(sub, 1), :] = line
    sim_ref[:subs, :] = tree_sum(part_ref[...] for part_ref in part_refs)


def pieces(refs, size, rows):
    found = []
    for ref in refs:
        found += [ref.at[at:at + rows] for at in range(0, ref.shape[0], rows)]
    assert len(found) == size
    return found


def added(refs, rows):
    return tree_sum(ref[...] for ref in pieces(refs, sum(ref.shape[0] for ref in refs) // rows, rows))


def add_kernel(one_ref, other_ref, out_ref):
    out_ref[...] = one_ref[...] + other_ref[...]


def first_kernel(dims, no, lat_ref, came_ref, *refs):
    nc, nb, modes, _, _ = dims
    refs, part_refs = refs[:-PARTS], refs[-PARTS:]
    near_refs, refs = refs[:-8], refs[-8:]
    out_ref, field_ref, foot_ref, all_ref, choose_ref, tail_ref, ids_ref, sem = refs
    rows = nb * CR * modes
    for j in range(nc):
        all_ref[j:j + 1, :] = came_ref[j, rows:rows + 16, :].astype(F32)[0:1].astype(jnp.int32)
    copy = pltpu.make_async_copy(all_ref, ids_ref, sem)
    copy.start()
    for j in range(nc):
        foot_ref[j] = came_ref[j, :rows, :]
    per_dev = field_ref.shape[0] // no
    copy.wait()
    own = ids_ref[0, 3 * nb]
    for s, near_ref in enumerate(pieces(near_refs, no, per_dev * modes)):
        for l in range(per_dev):
            field_ref[((own ^ s) if permuted(no) else s) * per_dev + l] = near_ref[l * modes:(l + 1) * modes, :]
    line = lax.broadcasted_iota(jnp.int32, choose_ref.shape, 0)
    lane = lax.broadcasted_iota(jnp.int32, choose_ref.shape, 1)
    tail_line = lax.broadcasted_iota(jnp.int32, tail_ref.shape, 0)
    tail_lane = lax.broadcasted_iota(jnp.int32, tail_ref.shape, 1)
    subs = jnp.zeros(choose_ref.shape, jnp.int32)
    tail = jnp.zeros(tail_ref.shape, jnp.int32)
    for j in range(nc):
        for b in range(nb):
            subs = jnp.where(line == j * nb + b, ids_ref[j, 2 * nb + b], subs)
            value = jnp.where(tail_line == 0, ids_ref[j, b], ids_ref[j, nb + b])
            tail = jnp.where(tail_lane == j * nb + b, value, tail)
    choose_ref[...] = jnp.where(lane % (choose_ref.shape[1] // TERMS) == subs, 1.0, 0.0).astype(BF16)
    tail_ref[...] = tail.astype(F32)
    forward(dims, field_ref, lat_ref, foot_ref, ids_ref, part_refs, out_ref)


def split(values):
    terms = []
    for _ in range(TERMS):
        terms.append(values.astype(BF16).astype(F32))
        values = values - terms[-1]
    return jnp.concatenate(terms, axis=0).astype(BF16)


def adjoint_kernel(dims, tails, choose_ref, weight_ref, foot_ref, *refs):
    nc, nb, modes, groups, band = dims
    tail_refs, refs = refs[:tails], refs[tails:]
    sim_refs, refs = refs[:-3], refs[-3:]
    out_ref, norm_ref, chosen_ref = refs
    subs = weight_ref.shape[0]
    mine = nc * nb
    total = added(sim_refs, subs + ROWS)
    norm = jnp.sqrt(jnp.sum(total[subs:], keepdims=True))
    norm_ref[...] = jnp.broadcast_to(norm, norm_ref.shape)
    scale = 1.0 / norm
    sim = total[:subs]
    weighted = sim * weight_ref[...]
    chosen_ref[...] = jnp.dot(choose_ref[...], split(weighted), preferred_element_type=F32)
    lane = lax.broadcasted_iota(jnp.int32, (modes, 128), 1)
    parts = [jnp.zeros((modes, 128), F32) for _ in range(CR)]
    for j in range(nc):
        for b in range(nb):
            at_t = j * nb + b
            chosen = chosen_ref[at_t:at_t + 1, :]
            for r in range(CR):
                at = (b * CR + r) * modes
                column = jnp.sum(foot_ref[j, at:at + modes, :].astype(F32) * chosen, axis=1, keepdims=True)
                parts[r] = jnp.where(lane == at_t, column, parts[r])
    rest = 128 - CR * modes
    if rest:
        parts.append(jnp.zeros((rest, 128), F32))
    rows = jnp.concatenate(parts, axis=0).T
    out_ref[:mine, :] = rows[:mine] * scale
    out_ref[mine:mine + subs, :] = (sim * scale) * (weighted * scale)
    for tail_ref in tail_refs:
        out_ref[mine + subs:, :] = tail_ref[...]


def every_kernel(dims, no, at, *refs):
    refs, out_ref = refs[:-1], refs[-1]
    rows = sum(ref.shape[0] for ref in refs) // no
    for s, ref in enumerate(pieces(refs, no, rows)):
        out_ref[2 * s:2 * s + 2, :] = ref[at:at + ROWS, :][0:2].astype(jnp.int32)


def image_kernel(dims, no, first, last, ids_ref, all_ref, lat_ref, foot_ref, pick_ref, norm_ref, field_ref, *refs):
    nc, nb, modes, groups, band = dims
    if not first:
        prior_ref, refs = refs[0], refs[1:]
    ways = min(no, WAYS)
    refs, part_refs = refs[:-PARTS], refs[-PARTS:]
    kept = 6 + ways
    coef_refs, refs = refs[:-kept], refs[-kept:]
    sum_refs, refs = refs[-ways:], refs[:-ways]
    if last:
        out_ref, row_ref, mine_ref, alpha_ref, next_ref, held_ref = refs
    else:
        out_ref, row_ref, next_ref, vector_ref, alpha_ref, held_ref = refs
    mine = nc * nb
    periods = field_ref.shape[0]
    per_dev = row_ref.shape[0]
    subs = ROWS
    rows = sum(ref.shape[0] for ref in coef_refs) // no
    coef_refs = pieces(coef_refs, no, rows)
    for s in range(no):
        held_ref[s] = coef_refs[s][:mine, :]
    for sum_ref in sum_refs:
        sum_ref[...] = jnp.zeros_like(sum_ref)
    gain = jnp.sum(tree_sum(ref[mine:mine + subs, :] for ref in coef_refs), keepdims=True)
    alpha_ref[...] = jnp.broadcast_to(1.0 + gain, alpha_ref.shape)
    norm = norm_ref[0:1, :]
    scale = 1.0 / norm
    own = ids_ref[0, 3 * nb]

    def group(at, carry):
        found = [at * ways + i for i in range(ways)]
        for chunk in range(0, mine, CHUNK):
            left = [split(held_ref[s, chunk:chunk + CHUNK, :]) for s in found]
            left = jnp.concatenate(left, axis=1)
            for pair in range(0, CHUNK, 2):
                wide = lax.dot_general(
                    left,
                    pick_ref[:, pair * 128:(pair + 2) * 128],
                    (((0,), (0,)), ((), ())),
                    preferred_element_type=F32,
                )
                for at_t in range(2):
                    at_block = chunk + pair + at_t
                    totals = []
                    for i, s in enumerate(found):
                        row = all_ref[2 * s + 1, at_block] * CR
                        total = sum_refs[i][all_ref[2 * s, at_block]]
                        for r in range(CR):
                            start = i * 128 + r * modes
                            coef = wide[start:start + modes, at_t * 128:(at_t + 1) * 128]
                            total += coef * lat_ref[row + r]
                        totals.append(total)
                    for i, s in enumerate(found):
                        sum_refs[i][all_ref[2 * s, at_block]] = totals[i]
        return carry

    if no <= 4:
        for at in range(no // ways):
            group(at, 0)
    else:
        lax.fori_loop(0, no // ways, group, 0)
    for p in range(periods):
        vector = field_ref[p] * scale
        if not last:
            vector_ref[p] = vector
        rest = tree_sum(sum_ref[p] for sum_ref in sum_refs) - vector * gain
        if not first:
            rest -= prior_ref[p] * norm
        next_ref[p] = rest
    for l in range(per_dev):
        row_ref[l] = field_ref[own * per_dev + l] * scale
    if last:
        out_ref[...] = fold(next_ref)
        for l in range(per_dev):
            mine_ref[l] = next_ref[own * per_dev + l]
    else:
        forward(dims, next_ref, lat_ref, foot_ref, ids_ref, part_refs, out_ref)


def finish_kernel(factor, sums, *refs):
    sum_refs, refs = refs[:sums], refs[sums:]
    row_refs, refs = refs[:STEPS], refs[STEPS:]
    mine_ref, refs = refs[0], refs[1:]
    alphas, refs = refs[:STEPS], refs[STEPS:]
    norms, refs = refs[:STEPS - 1], refs[STEPS - 1:]
    out_ref, coef_ref = refs
    norm = jnp.sqrt(jnp.sum(added(sum_refs, ROWS), keepdims=True))
    for k in range(STEPS):
        out_ref[k] = row_refs[k][...] * factor
    out_ref[STEPS] = mine_ref[...] * (factor / norm)
    row = lax.broadcasted_iota(jnp.int32, coef_ref.shape, 0)
    col = lax.broadcasted_iota(jnp.int32, coef_ref.shape, 1)
    coefs = jnp.zeros(coef_ref.shape, F32)
    for k in range(STEPS):
        beta = norms[k][0:1, 0:1] if k < STEPS - 1 else norm
        coefs = jnp.where((row == 0) & (col == k), alphas[k][0:1, 0:1], coefs)
        coefs = jnp.where((row == 1) & (col == k), beta, coefs)
    coef_ref[...] = coefs


def permuted(size):
    return size <= 4 and size & (size - 1) == 0


def share(array, axis):
    size = lax.axis_size(axis)
    if not permuted(size):
        return [swap(jnp.broadcast_to(array[None], (size,) + array.shape), axis).reshape(-1, array.shape[1])]
    return [array] + [lax.ppermute(array, axis, [(d, d ^ s) for d in range(size)]) for s in range(1, size)]


def addends(array, axis):
    size = lax.axis_size(axis)
    if size != 8:
        return [swap(jnp.broadcast_to(array[None], (size,) + array.shape), axis).reshape(-1, array.shape[1])]
    other = lax.ppermute(array, axis, [(d, d ^ 1) for d in range(size)])
    both = call(add_kernel, jax.ShapeDtypeStruct(array.shape, F32), [VMEM] * 2, array, other)
    return [both] + [lax.ppermute(both, axis, [(d, d ^ s) for d in range(size)]) for s in (2, 4, 6)]


def swap(array, axis):
    return lax.all_to_all(array, axis, split_axis=0, concat_axis=0, tiled=True)


def body(start, lat_mats, footprints, blk_sub, blk_off, counts, rinv):
    per_dev, held, lat_rows = start.shape
    nc = lax.axis_size("cell")
    no = lax.axis_size("obs")
    lon_cols = held * nc
    band = lat_rows // nc
    groups = band // CR
    nb, ob, _ = footprints.shape
    subs = counts.shape[0]
    modes = -(-held // 16) * 16
    mine = nc * nb
    periods = per_dev * no
    dims = (nc, nb, modes, groups, band)
    shape = functools.partial(jax.ShapeDtypeStruct, dtype=F32)

    high, low = lon_table(lon_cols, nc, modes)
    if modes != held:
        start = jnp.pad(start, ((0, 0), (0, modes - held), (0, 0)))
        lat_mats = jnp.pad(lat_mats, ((0, modes - held), (0, 0), (0, 0)))
    place = lax.axis_index(("obs", "cell")).astype(jnp.int32).reshape(1)

    start = start.reshape(per_dev * modes, lat_rows)
    near = share(start, "obs")
    foot_rows = nb * CR * modes
    hats, weights = call(
        functools.partial(transform_kernel, dims),
        (jax.ShapeDtypeStruct((nc, foot_rows + 16, ob), BF16), shape((subs, ob))),
        [ANY] * 8,
        place, jnp.asarray(high), jnp.asarray(low), footprints, blk_off, blk_sub, counts, rinv.reshape(subs, ob),
        scratch=[
            pltpu.VMEM(high.shape, BF16),
            pltpu.VMEM(low.shape, BF16),
            pltpu.VMEM(footprints.shape, BF16),
            pltpu.SMEM((nb,), jnp.int32),
            pltpu.SMEM((nb,), jnp.int32),
            pltpu.SMEM((subs,), jnp.int32),
            pltpu.VMEM((subs, ob), F32),
            pltpu.SMEM((1,), jnp.int32),
            pltpu.SemaphoreType.DMA((8,)),
        ],
        limit=60,
    )
    came = swap(hats, "cell")
    lat, start, _ = lax.optimization_barrier((lat_mats, start, weights))
    lat, start, pick = call(
        fetch_kernel,
        (
            shape((lat_rows, modes, lat_rows)),
            shape(start.shape),
            jax.ShapeDtypeStruct((TERMS * CHUNK, CHUNK * 128), BF16),
        ),
        [ANY] * 2,
        lat, start,
        scratch=[pltpu.SemaphoreType.DMA((modes + 1,))],
        limit=50,
        cost=pl.CostEstimate(flops=0, transcendentals=0, bytes_accessed=8 * (lat.size + start.size)),
    )
    if permuted(no):
        near[0] = start

    field_shape = shape((periods, modes, lat_rows))
    small = shape((ROWS, 128))
    own_shape = shape((per_dev, modes, lat_rows))
    sims, field, foot, ids, choose, tail = call(
        functools.partial(first_kernel, dims, no),
        (
            shape((subs + ROWS, ob)),
            field_shape,
            jax.ShapeDtypeStruct((nc, foot_rows, ob), BF16),
            jax.ShapeDtypeStruct((nc, 128), jnp.int32),
            jax.ShapeDtypeStruct((mine, TERMS * subs), BF16),
            shape((ROWS, 128)),
        ),
        [VMEM] * (2 + len(near)),
        lat, came, *near,
        scratch=[pltpu.SMEM((nc, 128), jnp.int32), pltpu.SemaphoreType.DMA] + [pltpu.VMEM((subs, ob), F32)] * PARTS,
    )
    ways = min(no, WAYS)
    rows, alphas, norms = [], [], []
    vector = None
    for step in range(STEPS):
        first, last = step == 0, step == STEPS - 1
        parts = addends(sims, "cell")
        tails = [tail] if first else []
        coefs, norm = call(
            functools.partial(adjoint_kernel, dims, len(tails)),
            (shape((mine + subs + (ROWS if first else 0), 128)), small),
            [VMEM] * (3 + len(tails) + len(parts)),
            choose, weights, foot, *tails, *parts,
            scratch=[pltpu.VMEM((mine, ob), F32)],
        )
        coefs = share(coefs, "obs")
        if first:
            every = call(
                functools.partial(every_kernel, dims, no, mine + subs),
                jax.ShapeDtypeStruct((2 * no, 128), jnp.int32),
                [VMEM] * len(coefs),
                *coefs,
            )
        before = [] if first else [vector]
        sims, row, field, *vector, alpha = call(
            functools.partial(image_kernel, dims, no, first, last),
            (
                shape((ROWS if last else subs + ROWS, 128)),
                own_shape,
                own_shape if last else field_shape,
                *([] if last else [field_shape]),
                small,
            ),
            [SMEM] * 2 + [VMEM] * (5 + len(before) + len(coefs)),
            ids, every, lat, foot, pick, norm, field, *before, *coefs,
            scratch=[pltpu.VMEM(field_shape.shape, F32)] * last
            + [pltpu.VMEM((no, mine, 128), F32)]
            + [pltpu.VMEM(field_shape.shape, F32)] * ways
            + [pltpu.VMEM((subs, ob), F32)] * PARTS,
            limit=16,
        )
        vector = None if last else vector[0]
        rows.append(row)
        alphas.append(alpha)
        norms.append(norm)
    factor = math.sqrt(periods * lon_cols * lat_rows)
    parts = addends(sims, "cell")
    krylov, coeffs = call(
        functools.partial(finish_kernel, factor, len(parts)),
        (shape((STEPS + 1, per_dev, modes, lat_rows)), shape((2, STEPS))),
        [VMEM] * (len(parts) + STEPS + 1 + STEPS + STEPS - 1),
        *parts, *rows, field, *alphas, *norms[1:],
    )
    return krylov[:, :, :held], coeffs


def solution(mesh):
    placed = (
        P("obs", "cell", None),
        P("cell", None, None),
        P(("obs", "cell"), None, None),
        P(("obs", "cell")),
        P(("obs", "cell")),
        P("obs"),
        P("obs"),
    )
    return jax.shard_map(
        body,
        mesh=mesh,
        in_specs=placed,
        out_specs=(P(None, "obs", "cell", None), P()),
        check_vma=False,
    )
```

```python
import functools
import math

import jax
import jax.numpy as jnp
import ml_dtypes
import numpy as np
from jax import lax
from jax.experimental import pallas as pl
from jax.experimental.pallas import tpu as pltpu
from jax.sharding import PartitionSpec as P

CR = 2
WAYS = 4
PARTS = 4
CHUNK = 16
TERMS = 3
STEPS = 3
ROWS = 8
VMEM = pl.BlockSpec(memory_space=pltpu.VMEM)
SMEM = pl.BlockSpec(memory_space=pltpu.SMEM)
ANY = pl.BlockSpec(memory_space=pl.ANY)
F32 = jnp.float32
BF16 = jnp.bfloat16


def lon_table(order, parts, padded):
    index = np.arange(order)
    half = order // 2
    freq = np.where(index <= half, index, index - half)[:, None]
    phase = (freq * index[None, :] % order) * (2.0 * math.pi / order)
    factor = np.where((index == 0) | (index == half), math.sqrt(1.0 / order), math.sqrt(2.0 / order))
    table = np.where(index[:, None] <= half, np.cos(phase), np.sin(phase)) * factor[:, None]
    table = table.reshape(parts, order // parts, order)
    table = np.pad(table, ((0, 0), (0, padded - order // parts), (0, 0))).reshape(parts * padded, order)
    high = table.astype(np.float32).astype(ml_dtypes.bfloat16)
    low = (table - high.astype(np.float64)).astype(np.float32).astype(ml_dtypes.bfloat16)
    return high, low


def call(kernel, outs, specs, *args, scratch=(), limit=8, cost=None, out_specs=None):
    return pl.pallas_call(
        kernel,
        out_shape=outs,
        in_specs=specs,
        out_specs=out_specs or jax.tree.map(lambda _: VMEM, outs),
        scratch_shapes=scratch,
        cost_estimate=cost,
        compiler_params=pltpu.CompilerParams(vmem_limit_bytes=limit * 1024 * 1024),
    )(*args)


def tree_sum(parts):
    parts = list(parts)
    while len(parts) > 1:
        parts = [sum(parts[at:at + 2][1:], parts[at]) for at in range(0, len(parts), 2)]
    return parts[0]


def transform_kernel(dims, place_any, high_any, low_any, foot_any, off_any, sub_any, count_any, rinv_any, start_any, *refs):
    nc, nb, modes, groups, band = dims
    out_any, weight_ref, start_ref, *refs, sems, out_sems = refs
    high_ref, low_ref, foot_ref, off_ref, sub_ref, count_ref, rinv_ref, place_ref, out_ref = refs
    copies = [
        pltpu.make_async_copy(source, target, sems.at[at])
        for at, (source, target) in enumerate(
            [
                (foot_any, foot_ref),
                (high_any, high_ref),
                (low_any, low_ref),
                (off_any, off_ref),
                (sub_any, sub_ref),
                (count_any, count_ref),
                (rinv_any, rinv_ref),
                (place_any, place_ref),
                (start_any, start_ref),
            ]
        )
    ]
    for copy in copies:
        copy.start()
    for copy in copies:
        copy.wait()
    cell = place_ref[0] % nc
    obs = place_ref[0] // nc
    ob = foot_ref.shape[1]
    lon = high_ref.shape[1]
    contract = (((1,), (1,)), ((), ()))
    sent = []

    def send(at, rows):
        sent.append(
            pltpu.make_async_copy(
                out_ref.at[:, at:at + rows, :], out_any.at[:, at:at + rows, :], out_sems.at[len(sent)]
            )
        )
        sent[-1].start()

    for r in range(CR):
        foot = foot_ref[:, :, r * lon:(r + 1) * lon].reshape(nb * ob, lon)
        hat = lax.dot_general(high_ref[...], foot, contract, preferred_element_type=F32)
        hat += lax.dot_general(low_ref[...], foot, contract, preferred_element_type=F32)
        hat = hat.astype(BF16)
        for b in range(nb):
            at = (b * CR + r) * modes
            for c in range(nc):
                out_ref[c, at:at + modes, :] = hat[c * modes:(c + 1) * modes, b * ob:(b + 1) * ob]
            send(at, modes)
    lane = lax.broadcasted_iota(jnp.int32, (16, ob), 1)
    ids = jnp.zeros((16, ob), F32)
    for b in range(nb):
        off = off_ref[b]
        values = (off // groups, cell * (band // CR) + off % groups, sub_ref[b])
        for at, value in enumerate(values):
            ids = jnp.where(lane == at * nb + b, value.astype(F32), ids)
    ids = jnp.where(lane == 3 * nb, obs.astype(F32), ids).astype(BF16)
    for c in range(nc):
        out_ref[c, nb * CR * modes:, :] = ids
    send(nb * CR * modes, 16)
    row = lax.broadcasted_iota(jnp.int32, weight_ref.shape, 0)
    limit = jnp.zeros(weight_ref.shape, jnp.int32)
    for s in range(weight_ref.shape[0]):
        limit = jnp.where(row == s, count_ref[s], limit)
    lane = lax.broadcasted_iota(jnp.int32, weight_ref.shape, 1)
    weight_ref[...] = jnp.where(lane < limit, rinv_ref[...], 0.0)
    for copy in sent:
        copy.wait()


def fetch_kernel(lat_any, lat_ref, pick_ref, sems):
    modes = lat_any.shape[0]
    copies = [pltpu.make_async_copy(lat_any.at[m], lat_ref.at[:, m, :], sems.at[m]) for m in range(modes)]
    for copy in copies:
        copy.start()
    line = lax.broadcasted_iota(jnp.int32, pick_ref.shape, 0)
    lane = lax.broadcasted_iota(jnp.int32, pick_ref.shape, 1)
    pick_ref[...] = jnp.where(line % CHUNK == lane // 128, 1.0, 0.0).astype(BF16)
    for copy in copies:
        copy.wait()


def fold(ref):
    periods, modes, _ = ref.shape
    total = jnp.zeros((ROWS, ref.shape[2]), F32)
    for p in range(periods):
        for at in range(0, modes, ROWS):
            part = ref[p, at:at + ROWS, :]
            total += part * part
    return total


def forward(dims, field_ref, lat_ref, foot_ref, ids_ref, part_refs, sim_ref):
    nc, nb, modes, groups, band = dims
    subs = sim_ref.shape[0] - ROWS
    for part_ref in part_refs:
        part_ref[...] = jnp.zeros_like(part_ref)
    found = []
    for j in range(nc):
        for b in range(nb):
            period = ids_ref[j, b]
            row = ids_ref[j, nb + b] * CR
            sub = ids_ref[j, 2 * nb + b]
            total = None
            for r in range(CR):
                column = jnp.sum(lat_ref[row + r] * field_ref[period], axis=1, keepdims=True)
                at = (b * CR + r) * modes
                term = foot_ref[j, at:at + modes, :].astype(F32) * column
                total = term if total is None else total + term
            found.append((sub, jnp.sum(total, axis=0, keepdims=True)))
    sim_ref[subs:, :] = fold(field_ref)
    for at in range(0, len(found), len(part_refs)):
        here = list(zip(part_refs, found[at:at + len(part_refs)]))
        sums = [part_ref[pl.ds(sub, 1), :] + line for part_ref, (sub, line) in here]
        for (part_ref, (sub, _)), line in zip(here, sums):
            part_ref[pl.ds(sub, 1), :] = line
    sim_ref[:subs, :] = tree_sum(part_ref[...] for part_ref in part_refs)


def pieces(refs, size, rows):
    found = []
    for ref in refs:
        found += [ref.at[at:at + rows] for at in range(0, ref.shape[0], rows)]
    assert len(found) == size
    return found


def added(refs, rows):
    return tree_sum(ref[...] for ref in pieces(refs, sum(ref.shape[0] for ref in refs) // rows, rows))


def add_kernel(one_ref, other_ref, out_ref):
    out_ref[...] = one_ref[...] + other_ref[...]


def first_kernel(dims, no, lat_ref, came_ref, *refs):
    nc, nb, modes, _, _ = dims
    refs, part_refs = refs[:-PARTS], refs[-PARTS:]
    near_refs, refs = refs[:-8], refs[-8:]
    out_ref, field_ref, foot_ref, all_ref, choose_ref, tail_ref, ids_ref, sem = refs
    rows = nb * CR * modes
    for j in range(nc):
        all_ref[j:j + 1, :] = came_ref[j, rows:rows + 16, :].astype(F32)[0:1].astype(jnp.int32)
    copy = pltpu.make_async_copy(all_ref, ids_ref, sem)
    copy.start()
    for j in range(nc):
        foot_ref[j] = came_ref[j, :rows, :]
    per_dev = field_ref.shape[0] // no
    copy.wait()
    own = ids_ref[0, 3 * nb]
    for s, near_ref in enumerate(pieces(near_refs, no, per_dev * modes)):
        for l in range(per_dev):
            field_ref[((own ^ s) if permuted(no) else s) * per_dev + l] = near_ref[l * modes:(l + 1) * modes, :]
    line = lax.broadcasted_iota(jnp.int32, choose_ref.shape, 0)
    lane = lax.broadcasted_iota(jnp.int32, choose_ref.shape, 1)
    tail_line = lax.broadcasted_iota(jnp.int32, tail_ref.shape, 0)
    tail_lane = lax.broadcasted_iota(jnp.int32, tail_ref.shape, 1)
    subs = jnp.zeros(choose_ref.shape, jnp.int32)
    tail = jnp.zeros(tail_ref.shape, jnp.int32)
    for j in range(nc):
        for b in range(nb):
            subs = jnp.where(line == j * nb + b, ids_ref[j, 2 * nb + b], subs)
            value = jnp.where(tail_line == 0, ids_ref[j, b], ids_ref[j, nb + b])
            tail = jnp.where(tail_lane == j * nb + b, value, tail)
    choose_ref[...] = jnp.where(lane % (choose_ref.shape[1] // TERMS) == subs, 1.0, 0.0).astype(BF16)
    tail_ref[...] = tail.astype(F32)
    forward(dims, field_ref, lat_ref, foot_ref, ids_ref, part_refs, out_ref)


def split(values):
    terms = []
    for _ in range(TERMS):
        terms.append(values.astype(BF16).astype(F32))
        values = values - terms[-1]
    return jnp.concatenate(terms, axis=0).astype(BF16)


def adjoint_kernel(dims, tails, choose_ref, weight_ref, foot_ref, *refs):
    nc, nb, modes, groups, band = dims
    tail_refs, refs = refs[:tails], refs[tails:]
    sim_refs, refs = refs[:-3], refs[-3:]
    out_ref, norm_ref, chosen_ref = refs
    subs = weight_ref.shape[0]
    mine = nc * nb
    total = added(sim_refs, subs + ROWS)
    norm = jnp.sqrt(jnp.sum(total[subs:], keepdims=True))
    norm_ref[...] = jnp.broadcast_to(norm, norm_ref.shape)
    scale = 1.0 / norm
    sim = total[:subs]
    weighted = sim * weight_ref[...]
    chosen_ref[...] = jnp.dot(choose_ref[...], split(weighted), preferred_element_type=F32)
    lane = lax.broadcasted_iota(jnp.int32, (modes, 128), 1)
    parts = [jnp.zeros((modes, 128), F32) for _ in range(CR)]
    for j in range(nc):
        for b in range(nb):
            at_t = j * nb + b
            chosen = chosen_ref[at_t:at_t + 1, :]
            for r in range(CR):
                at = (b * CR + r) * modes
                column = jnp.sum(foot_ref[j, at:at + modes, :].astype(F32) * chosen, axis=1, keepdims=True)
                parts[r] = jnp.where(lane == at_t, column, parts[r])
    rest = 128 - CR * modes
    if rest:
        parts.append(jnp.zeros((rest, 128), F32))
    rows = jnp.concatenate(parts, axis=0).T
    out_ref[:mine, :] = rows[:mine] * scale
    out_ref[mine:mine + subs, :] = (sim * scale) * (weighted * scale)
    for tail_ref in tail_refs:
        out_ref[mine + subs:, :] = tail_ref[...]


def every_kernel(dims, no, at, *refs):
    refs, out_ref = refs[:-1], refs[-1]
    rows = sum(ref.shape[0] for ref in refs) // no
    for s, ref in enumerate(pieces(refs, no, rows)):
        out_ref[2 * s:2 * s + 2, :] = ref[at:at + ROWS, :][0:2].astype(jnp.int32)


def image_kernel(dims, no, first, last, ids_ref, all_ref, lat_ref, foot_ref, pick_ref, norm_ref, field_ref, *refs):
    nc, nb, modes, groups, band = dims
    if not first:
        prior_ref, refs = refs[0], refs[1:]
    ways = min(no, WAYS)
    refs, part_refs = refs[:-PARTS], refs[-PARTS:]
    kept = 6 + ways
    coef_refs, refs = refs[:-kept], refs[-kept:]
    sum_refs, refs = refs[-ways:], refs[:-ways]
    if last:
        out_ref, row_ref, mine_ref, alpha_ref, next_ref, held_ref = refs
    else:
        out_ref, row_ref, next_ref, vector_ref, alpha_ref, held_ref = refs
    mine = nc * nb
    periods = field_ref.shape[0]
    per_dev = row_ref.shape[0]
    subs = ROWS
    rows = sum(ref.shape[0] for ref in coef_refs) // no
    coef_refs = pieces(coef_refs, no, rows)
    for s in range(no):
        held_ref[s] = coef_refs[s][:mine, :]
    for sum_ref in sum_refs:
        sum_ref[...] = jnp.zeros_like(sum_ref)
    gain = jnp.sum(tree_sum(ref[mine:mine + subs, :] for ref in coef_refs), keepdims=True)
    alpha_ref[...] = jnp.broadcast_to(1.0 + gain, alpha_ref.shape)
    norm = norm_ref[0:1, :]
    scale = 1.0 / norm
    own = ids_ref[0, 3 * nb]

    def group(at, carry):
        found = [at * ways + i for i in range(ways)]
        for chunk in range(0, mine, CHUNK):
            left = [split(held_ref[s, chunk:chunk + CHUNK, :]) for s in found]
            left = jnp.concatenate(left, axis=1)
            for pair in range(0, CHUNK, 2):
                wide = lax.dot_general(
                    left,
                    pick_ref[:, pair * 128:(pair + 2) * 128],
                    (((0,), (0,)), ((), ())),
                    preferred_element_type=F32,
                )
                for at_t in range(2):
                    at_block = chunk + pair + at_t
                    totals = []
                    for i, s in enumerate(found):
                        row = all_ref[2 * s + 1, at_block] * CR
                        total = sum_refs[i][all_ref[2 * s, at_block]]
                        for r in range(CR):
                            start = i * 128 + r * modes
                            coef = wide[start:start + modes, at_t * 128:(at_t + 1) * 128]
                            total += coef * lat_ref[row + r]
                        totals.append(total)
                    for i, s in enumerate(found):
                        sum_refs[i][all_ref[2 * s, at_block]] = totals[i]
        return carry

    if no <= 4:
        for at in range(no // ways):
            group(at, 0)
    else:
        lax.fori_loop(0, no // ways, group, 0)
    for p in range(periods):
        vector = field_ref[p] * scale
        if not last:
            vector_ref[p] = vector
        rest = tree_sum(sum_ref[p] for sum_ref in sum_refs) - vector * gain
        if not first:
            rest -= prior_ref[p] * norm
        next_ref[p] = rest
    for l in range(per_dev):
        row_ref[l] = field_ref[own * per_dev + l] * scale
    if last:
        out_ref[...] = fold(next_ref)
        for l in range(per_dev):
            mine_ref[l] = next_ref[own * per_dev + l]
    else:
        forward(dims, next_ref, lat_ref, foot_ref, ids_ref, part_refs, out_ref)


def finish_kernel(factor, sums, *refs):
    sum_refs, refs = refs[:sums], refs[sums:]
    row_refs, refs = refs[:STEPS], refs[STEPS:]
    mine_ref, refs = refs[0], refs[1:]
    alphas, refs = refs[:STEPS], refs[STEPS:]
    norms, refs = refs[:STEPS - 1], refs[STEPS - 1:]
    out_ref, coef_ref = refs
    norm = jnp.sqrt(jnp.sum(added(sum_refs, ROWS), keepdims=True))
    for k in range(STEPS):
        out_ref[k] = row_refs[k][...] * factor
    out_ref[STEPS] = mine_ref[...] * (factor / norm)
    row = lax.broadcasted_iota(jnp.int32, coef_ref.shape, 0)
    col = lax.broadcasted_iota(jnp.int32, coef_ref.shape, 1)
    coefs = jnp.zeros(coef_ref.shape, F32)
    for k in range(STEPS):
        beta = norms[k][0:1, 0:1] if k < STEPS - 1 else norm
        coefs = jnp.where((row == 0) & (col == k), alphas[k][0:1, 0:1], coefs)
        coefs = jnp.where((row == 1) & (col == k), beta, coefs)
    coef_ref[...] = coefs


def permuted(size):
    return size <= 4 and size & (size - 1) == 0


def share(array, axis):
    size = lax.axis_size(axis)
    if not permuted(size):
        return [swap(jnp.broadcast_to(array[None], (size,) + array.shape), axis).reshape(-1, array.shape[1])]
    return [array] + [lax.ppermute(array, axis, [(d, d ^ s) for d in range(size)]) for s in range(1, size)]


def addends(array, axis):
    size = lax.axis_size(axis)
    if size != 8:
        return [swap(jnp.broadcast_to(array[None], (size,) + array.shape), axis).reshape(-1, array.shape[1])]
    other = lax.ppermute(array, axis, [(d, d ^ 1) for d in range(size)])
    both = call(add_kernel, jax.ShapeDtypeStruct(array.shape, F32), [VMEM] * 2, array, other)
    return [both] + [lax.ppermute(both, axis, [(d, d ^ s) for d in range(size)]) for s in (2, 4, 6)]


def swap(array, axis):
    return lax.all_to_all(array, axis, split_axis=0, concat_axis=0, tiled=True)


def body(start, lat_mats, footprints, blk_sub, blk_off, counts, rinv):
    per_dev, held, lat_rows = start.shape
    nc = lax.axis_size("cell")
    no = lax.axis_size("obs")
    lon_cols = held * nc
    band = lat_rows // nc
    groups = band // CR
    nb, ob, _ = footprints.shape
    subs = counts.shape[0]
    modes = -(-held // 16) * 16
    mine = nc * nb
    periods = per_dev * no
    dims = (nc, nb, modes, groups, band)
    shape = functools.partial(jax.ShapeDtypeStruct, dtype=F32)

    high, low = lon_table(lon_cols, nc, modes)
    if modes != held:
        start = jnp.pad(start, ((0, 0), (0, modes - held), (0, 0)))
        lat_mats = jnp.pad(lat_mats, ((0, modes - held), (0, 0), (0, 0)))
    place = lax.axis_index(("obs", "cell")).astype(jnp.int32).reshape(1)

    start = start.reshape(per_dev * modes, lat_rows)
    near = share(start, "obs")
    foot_rows = nb * CR * modes
    hats, weights, start = call(
        functools.partial(transform_kernel, dims),
        (jax.ShapeDtypeStruct((nc, foot_rows + 16, ob), BF16), shape((subs, ob)), shape(start.shape)),
        [ANY] * 9,
        place, jnp.asarray(high), jnp.asarray(low), footprints, blk_off, blk_sub, counts, rinv.reshape(subs, ob), start,
        out_specs=(ANY, VMEM, VMEM),
        scratch=[
            pltpu.VMEM(high.shape, BF16),
            pltpu.VMEM(low.shape, BF16),
            pltpu.VMEM(footprints.shape, BF16),
            pltpu.SMEM((nb,), jnp.int32),
            pltpu.SMEM((nb,), jnp.int32),
            pltpu.SMEM((subs,), jnp.int32),
            pltpu.VMEM((subs, ob), F32),
            pltpu.SMEM((1,), jnp.int32),
            pltpu.VMEM((nc, foot_rows + 16, ob), BF16),
            pltpu.SemaphoreType.DMA((9,)),
            pltpu.SemaphoreType.DMA((nb * CR + 1,)),
        ],
        limit=60,
    )
    came = swap(hats, "cell")
    lat, _ = lax.optimization_barrier((lat_mats, weights))
    lat, pick = call(
        fetch_kernel,
        (
            shape((lat_rows, modes, lat_rows)),
            jax.ShapeDtypeStruct((TERMS * CHUNK, CHUNK * 128), BF16),
        ),
        [ANY],
        lat,
        scratch=[pltpu.SemaphoreType.DMA((modes,))],
        limit=50,
        cost=pl.CostEstimate(flops=0, transcendentals=0, bytes_accessed=8 * lat.size),
    )
    if permuted(no):
        near[0] = start

    field_shape = shape((periods, modes, lat_rows))
    small = shape((ROWS, 128))
    own_shape = shape((per_dev, modes, lat_rows))
    sims, field, foot, ids, choose, tail = call(
        functools.partial(first_kernel, dims, no),
        (
            shape((subs + ROWS, ob)),
            field_shape,
            jax.ShapeDtypeStruct((nc, foot_rows, ob), BF16),
            jax.ShapeDtypeStruct((nc, 128), jnp.int32),
            jax.ShapeDtypeStruct((mine, TERMS * subs), BF16),
            shape((ROWS, 128)),
        ),
        [VMEM] * (2 + len(near)),
        lat, came, *near,
        scratch=[pltpu.SMEM((nc, 128), jnp.int32), pltpu.SemaphoreType.DMA] + [pltpu.VMEM((subs, ob), F32)] * PARTS,
    )
    ways = min(no, WAYS)
    rows, alphas, norms = [], [], []
    vector = None
    for step in range(STEPS):
        first, last = step == 0, step == STEPS - 1
        parts = addends(sims, "cell")
        tails = [tail] if first else []
        coefs, norm = call(
            functools.partial(adjoint_kernel, dims, len(tails)),
            (shape((mine + subs + (ROWS if first else 0), 128)), small),
            [VMEM] * (3 + len(tails) + len(parts)),
            choose, weights, foot, *tails, *parts,
            scratch=[pltpu.VMEM((mine, ob), F32)],
        )
        coefs = share(coefs, "obs")
        if first:
            every = call(
                functools.partial(every_kernel, dims, no, mine + subs),
                jax.ShapeDtypeStruct((2 * no, 128), jnp.int32),
                [VMEM] * len(coefs),
                *coefs,
            )
        before = [] if first else [vector]
        sims, row, field, *vector, alpha = call(
            functools.partial(image_kernel, dims, no, first, last),
            (
                shape((ROWS if last else subs + ROWS, 128)),
                own_shape,
                own_shape if last else field_shape,
                *([] if last else [field_shape]),
                small,
            ),
            [SMEM] * 2 + [VMEM] * (5 + len(before) + len(coefs)),
            ids, every, lat, foot, pick, norm, field, *before, *coefs,
            scratch=[pltpu.VMEM(field_shape.shape, F32)] * last
            + [pltpu.VMEM((no, mine, 128), F32)]
            + [pltpu.VMEM(field_shape.shape, F32)] * ways
            + [pltpu.VMEM((subs, ob), F32)] * PARTS,
            limit=16,
        )
        vector = None if last else vector[0]
        rows.append(row)
        alphas.append(alpha)
        norms.append(norm)
    factor = math.sqrt(periods * lon_cols * lat_rows)
    parts = addends(sims, "cell")
    krylov, coeffs = call(
        functools.partial(finish_kernel, factor, len(parts)),
        (shape((STEPS + 1, per_dev, modes, lat_rows)), shape((2, STEPS))),
        [VMEM] * (len(parts) + STEPS + 1 + STEPS + STEPS - 1),
        *parts, *rows, field, *alphas, *norms[1:],
    )
    return krylov[:, :, :held], coeffs


def solution(mesh):
    placed = (
        P("obs", "cell", None),
        P("cell", None, None),
        P(("obs", "cell"), None, None),
        P(("obs", "cell")),
        P(("obs", "cell")),
        P("obs"),
        P("obs"),
    )
    return jax.shard_map(
        body,
        mesh=mesh,
        in_specs=placed,
        out_specs=(P(None, "obs", "cell", None), P()),
        check_vma=False,
    )
```

```python
import functools
import math

import jax
import jax.numpy as jnp
import ml_dtypes
import numpy as np
from jax import lax
from jax.experimental import pallas as pl
from jax.experimental.pallas import tpu as pltpu
from jax.sharding import PartitionSpec as P

CR = 2
WAYS = 4
PARTS = 4
CHUNK = 16
TERMS = 3
STEPS = 3
ROWS = 8
VMEM = pl.BlockSpec(memory_space=pltpu.VMEM)
SMEM = pl.BlockSpec(memory_space=pltpu.SMEM)
ANY = pl.BlockSpec(memory_space=pl.ANY)
F32 = jnp.float32
BF16 = jnp.bfloat16


def lon_table(order, parts, padded):
    index = np.arange(order)
    half = order // 2
    freq = np.where(index <= half, index, index - half)[:, None]
    phase = (freq * index[None, :] % order) * (2.0 * math.pi / order)
    factor = np.where((index == 0) | (index == half), math.sqrt(1.0 / order), math.sqrt(2.0 / order))
    table = np.where(index[:, None] <= half, np.cos(phase), np.sin(phase)) * factor[:, None]
    table = table.reshape(parts, order // parts, order)
    table = np.pad(table, ((0, 0), (0, padded - order // parts), (0, 0))).reshape(parts * padded, order)
    high = table.astype(np.float32).astype(ml_dtypes.bfloat16)
    low = (table - high.astype(np.float64)).astype(np.float32).astype(ml_dtypes.bfloat16)
    return high, low


def call(kernel, outs, specs, *args, scratch=(), limit=8, cost=None):
    return pl.pallas_call(
        kernel,
        out_shape=outs,
        in_specs=specs,
        out_specs=jax.tree.map(lambda _: VMEM, outs),
        scratch_shapes=scratch,
        cost_estimate=cost,
        compiler_params=pltpu.CompilerParams(vmem_limit_bytes=limit * 1024 * 1024),
    )(*args)


def tree_sum(parts):
    parts = list(parts)
    while len(parts) > 1:
        parts = [sum(parts[at:at + 2][1:], parts[at]) for at in range(0, len(parts), 2)]
    return parts[0]


def transform_kernel(dims, place_any, high_any, low_any, foot_any, off_any, sub_any, count_any, rinv_any, *refs):
    nc, nb, modes, groups, band = dims
    out_ref, weight_ref, high_ref, low_ref, foot_ref, off_ref, sub_ref, count_ref, rinv_ref, place_ref, sems = refs
    copies = [
        pltpu.make_async_copy(source, target, sems.at[at])
        for at, (source, target) in enumerate(
            [
                (foot_any, foot_ref),
                (high_any, high_ref),
                (low_any, low_ref),
                (off_any, off_ref),
                (sub_any, sub_ref),
                (count_any, count_ref),
                (rinv_any, rinv_ref),
                (place_any, place_ref),
            ]
        )
    ]
    for copy in copies:
        copy.start()
    ob = foot_ref.shape[1]
    lon = high_ref.shape[1]
    contract = (((1,), (1,)), ((), ()))
    copies[0].wait()
    copies[1].wait()
    feet = [foot_ref[:, :, r * lon:(r + 1) * lon].reshape(nb * ob, lon) for r in range(CR)]
    hats = [lax.dot_general(high_ref[...], foot, contract, preferred_element_type=F32) for foot in feet]
    copies[2].wait()
    for r in range(CR):
        hat = hats[r] + lax.dot_general(low_ref[...], feet[r], contract, preferred_element_type=F32)
        hat = hat.astype(BF16)
        for b in range(nb):
            at = (b * CR + r) * modes
            for c in range(nc):
                out_ref[c, at:at + modes, :] = hat[c * modes:(c + 1) * modes, b * ob:(b + 1) * ob]
    for copy in copies[3:]:
        copy.wait()
    cell = place_ref[0] % nc
    obs = place_ref[0] // nc
    lane = lax.broadcasted_iota(jnp.int32, (16, ob), 1)
    ids = jnp.zeros((16, ob), F32)
    for b in range(nb):
        off = off_ref[b]
        values = (off // groups, cell * (band // CR) + off % groups, sub_ref[b])
        for at, value in enumerate(values):
            ids = jnp.where(lane == at * nb + b, value.astype(F32), ids)
    ids = jnp.where(lane == 3 * nb, obs.astype(F32), ids).astype(BF16)
    for c in range(nc):
        out_ref[c, nb * CR * modes:, :] = ids
    row = lax.broadcasted_iota(jnp.int32, weight_ref.shape, 0)
    limit = jnp.zeros(weight_ref.shape, jnp.int32)
    for s in range(weight_ref.shape[0]):
        limit = jnp.where(row == s, count_ref[s], limit)
    lane = lax.broadcasted_iota(jnp.int32, weight_ref.shape, 1)
    weight_ref[...] = jnp.where(lane < limit, rinv_ref[...], 0.0)


def fetch_kernel(lat_any, start_any, lat_ref, start_ref, pick_ref, sems):
    modes = lat_any.shape[0]
    copies = [pltpu.make_async_copy(lat_any.at[m], lat_ref.at[:, m, :], sems.at[m]) for m in range(modes)]
    copies.append(pltpu.make_async_copy(start_any, start_ref, sems.at[modes]))
    for copy in copies:
        copy.start()
    line = lax.broadcasted_iota(jnp.int32, pick_ref.shape, 0)
    lane = lax.broadcasted_iota(jnp.int32, pick_ref.shape, 1)
    pick_ref[...] = jnp.where(line % CHUNK == lane // 128, 1.0, 0.0).astype(BF16)
    for copy in copies:
        copy.wait()


def fold(ref):
    periods, modes, _ = ref.shape
    total = jnp.zeros((ROWS, ref.shape[2]), F32)
    for p in range(periods):
        for at in range(0, modes, ROWS):
            part = ref[p, at:at + ROWS, :]
            total += part * part
    return total


def forward(dims, field_ref, lat_ref, foot_ref, ids_ref, part_refs, sim_ref):
    nc, nb, modes, groups, band = dims
    subs = sim_ref.shape[0] - ROWS
    for part_ref in part_refs:
        part_ref[...] = jnp.zeros_like(part_ref)
    found = []
    for j in range(nc):
        for b in range(nb):
            period = ids_ref[j, b]
            row = ids_ref[j, nb + b] * CR
            sub = ids_ref[j, 2 * nb + b]
            total = None
            for r in range(CR):
                column = jnp.sum(lat_ref[row + r] * field_ref[period], axis=1, keepdims=True)
                at = (b * CR + r) * modes
                term = foot_ref[j, at:at + modes, :].astype(F32) * column
                total = term if total is None else total + term
            found.append((sub, jnp.sum(total, axis=0, keepdims=True)))
    sim_ref[subs:, :] = fold(field_ref)
    for at in range(0, len(found), len(part_refs)):
        here = list(zip(part_refs, found[at:at + len(part_refs)]))
        sums = [part_ref[pl.ds(sub, 1), :] + line for part_ref, (sub, line) in here]
        for (part_ref, (sub, _)), line in zip(here, sums):
            part_ref[pl.ds(sub, 1), :] = line
    sim_ref[:subs, :] = tree_sum(part_ref[...] for part_ref in part_refs)


def pieces(refs, size, rows):
    found = []
    for ref in refs:
        found += [ref.at[at:at + rows] for at in range(0, ref.shape[0], rows)]
    assert len(found) == size
    return found


def added(refs, rows):
    return tree_sum(ref[...] for ref in pieces(refs, sum(ref.shape[0] for ref in refs) // rows, rows))


def add_kernel(one_ref, other_ref, out_ref):
    out_ref[...] = one_ref[...] + other_ref[...]


def first_kernel(dims, no, lat_ref, came_ref, *refs):
    nc, nb, modes, _, _ = dims
    refs, part_refs = refs[:-PARTS], refs[-PARTS:]
    near_refs, refs = refs[:-8], refs[-8:]
    out_ref, field_ref, foot_ref, all_ref, choose_ref, tail_ref, ids_ref, sem = refs
    rows = nb * CR * modes
    for j in range(nc):
        all_ref[j:j + 1, :] = came_ref[j, rows:rows + 16, :].astype(F32)[0:1].astype(jnp.int32)
    copy = pltpu.make_async_copy(all_ref, ids_ref, sem)
    copy.start()
    for j in range(nc):
        foot_ref[j] = came_ref[j, :rows, :]
    per_dev = field_ref.shape[0] // no
    copy.wait()
    own = ids_ref[0, 3 * nb]
    for s, near_ref in enumerate(pieces(near_refs, no, per_dev * modes)):
        for l in range(per_dev):
            field_ref[((own ^ s) if permuted(no) else s) * per_dev + l] = near_ref[l * modes:(l + 1) * modes, :]
    line = lax.broadcasted_iota(jnp.int32, choose_ref.shape, 0)
    lane = lax.broadcasted_iota(jnp.int32, choose_ref.shape, 1)
    tail_line = lax.broadcasted_iota(jnp.int32, tail_ref.shape, 0)
    tail_lane = lax.broadcasted_iota(jnp.int32, tail_ref.shape, 1)
    subs = jnp.zeros(choose_ref.shape, jnp.int32)
    tail = jnp.zeros(tail_ref.shape, jnp.int32)
    for j in range(nc):
        for b in range(nb):
            subs = jnp.where(line == j * nb + b, ids_ref[j, 2 * nb + b], subs)
            value = jnp.where(tail_line == 0, ids_ref[j, b], ids_ref[j, nb + b])
            tail = jnp.where(tail_lane == j * nb + b, value, tail)
    choose_ref[...] = jnp.where(lane % (choose_ref.shape[1] // TERMS) == subs, 1.0, 0.0).astype(BF16)
    tail_ref[...] = tail.astype(F32)
    forward(dims, field_ref, lat_ref, foot_ref, ids_ref, part_refs, out_ref)


def split(values):
    terms = []
    for _ in range(TERMS):
        terms.append(values.astype(BF16).astype(F32))
        values = values - terms[-1]
    return jnp.concatenate(terms, axis=0).astype(BF16)


def adjoint_kernel(dims, tails, choose_ref, weight_ref, foot_ref, *refs):
    nc, nb, modes, groups, band = dims
    tail_refs, refs = refs[:tails], refs[tails:]
    sim_refs, refs = refs[:-3], refs[-3:]
    out_ref, norm_ref, chosen_ref = refs
    subs = weight_ref.shape[0]
    mine = nc * nb
    total = added(sim_refs, subs + ROWS)
    norm = jnp.sqrt(jnp.sum(total[subs:], keepdims=True))
    norm_ref[...] = jnp.broadcast_to(norm, norm_ref.shape)
    scale = 1.0 / norm
    sim = total[:subs]
    weighted = sim * weight_ref[...]
    chosen_ref[...] = jnp.dot(choose_ref[...], split(weighted), preferred_element_type=F32)
    lane = lax.broadcasted_iota(jnp.int32, (modes, 128), 1)
    parts = [jnp.zeros((modes, 128), F32) for _ in range(CR)]
    for j in range(nc):
        for b in range(nb):
            at_t = j * nb + b
            chosen = chosen_ref[at_t:at_t + 1, :]
            for r in range(CR):
                at = (b * CR + r) * modes
                column = jnp.sum(foot_ref[j, at:at + modes, :].astype(F32) * chosen, axis=1, keepdims=True)
                parts[r] = jnp.where(lane == at_t, column, parts[r])
    rest = 128 - CR * modes
    if rest:
        parts.append(jnp.zeros((rest, 128), F32))
    rows = jnp.concatenate(parts, axis=0).T
    out_ref[:mine, :] = rows[:mine] * scale
    out_ref[mine:mine + subs, :] = (sim * scale) * (weighted * scale)
    for tail_ref in tail_refs:
        out_ref[mine + subs:, :] = tail_ref[...]


def every_kernel(dims, no, at, *refs):
    refs, out_ref = refs[:-1], refs[-1]
    rows = sum(ref.shape[0] for ref in refs) // no
    for s, ref in enumerate(pieces(refs, no, rows)):
        out_ref[2 * s:2 * s + 2, :] = ref[at:at + ROWS, :][0:2].astype(jnp.int32)


def image_kernel(dims, no, first, last, ids_ref, all_ref, lat_ref, foot_ref, pick_ref, norm_ref, field_ref, *refs):
    nc, nb, modes, groups, band = dims
    if not first:
        prior_ref, refs = refs[0], refs[1:]
    ways = min(no, WAYS)
    refs, part_refs = refs[:-PARTS], refs[-PARTS:]
    kept = 6 + ways
    coef_refs, refs = refs[:-kept], refs[-kept:]
    sum_refs, refs = refs[-ways:], refs[:-ways]
    if last:
        out_ref, row_ref, mine_ref, alpha_ref, next_ref, held_ref = refs
    else:
        out_ref, row_ref, next_ref, vector_ref, alpha_ref, held_ref = refs
    mine = nc * nb
    periods = field_ref.shape[0]
    per_dev = row_ref.shape[0]
    subs = ROWS
    rows = sum(ref.shape[0] for ref in coef_refs) // no
    coef_refs = pieces(coef_refs, no, rows)
    for s in range(no):
        held_ref[s] = coef_refs[s][:mine, :]
    for sum_ref in sum_refs:
        sum_ref[...] = jnp.zeros_like(sum_ref)
    gain = jnp.sum(tree_sum(ref[mine:mine + subs, :] for ref in coef_refs), keepdims=True)
    alpha_ref[...] = jnp.broadcast_to(1.0 + gain, alpha_ref.shape)
    norm = norm_ref[0:1, :]
    scale = 1.0 / norm
    own = ids_ref[0, 3 * nb]

    def group(at, carry):
        found = [at * ways + i for i in range(ways)]
        for chunk in range(0, mine, CHUNK):
            left = [split(held_ref[s, chunk:chunk + CHUNK, :]) for s in found]
            left = jnp.concatenate(left, axis=1)
            for pair in range(0, CHUNK, 2):
                wide = lax.dot_general(
                    left,
                    pick_ref[:, pair * 128:(pair + 2) * 128],
                    (((0,), (0,)), ((), ())),
                    preferred_element_type=F32,
                )
                for at_t in range(2):
                    at_block = chunk + pair + at_t
                    totals = []
                    for i, s in enumerate(found):
                        row = all_ref[2 * s + 1, at_block] * CR
                        total = sum_refs[i][all_ref[2 * s, at_block]]
                        for r in range(CR):
                            start = i * 128 + r * modes
                            coef = wide[start:start + modes, at_t * 128:(at_t + 1) * 128]
                            total += coef * lat_ref[row + r]
                        totals.append(total)
                    for i, s in enumerate(found):
                        sum_refs[i][all_ref[2 * s, at_block]] = totals[i]
        return carry

    if no <= 4:
        for at in range(no // ways):
            group(at, 0)
    else:
        lax.fori_loop(0, no // ways, group, 0)
    for p in range(periods):
        vector = field_ref[p] * scale
        if not last:
            vector_ref[p] = vector
        rest = tree_sum(sum_ref[p] for sum_ref in sum_refs) - vector * gain
        if not first:
            rest -= prior_ref[p] * norm
        next_ref[p] = rest
    for l in range(per_dev):
        row_ref[l] = field_ref[own * per_dev + l] * scale
    if last:
        out_ref[...] = fold(next_ref)
        for l in range(per_dev):
            mine_ref[l] = next_ref[own * per_dev + l]
    else:
        forward(dims, next_ref, lat_ref, foot_ref, ids_ref, part_refs, out_ref)


def finish_kernel(factor, sums, *refs):
    sum_refs, refs = refs[:sums], refs[sums:]
    row_refs, refs = refs[:STEPS], refs[STEPS:]
    mine_ref, refs = refs[0], refs[1:]
    alphas, refs = refs[:STEPS], refs[STEPS:]
    norms, refs = refs[:STEPS - 1], refs[STEPS - 1:]
    out_ref, coef_ref = refs
    norm = jnp.sqrt(jnp.sum(added(sum_refs, ROWS), keepdims=True))
    for k in range(STEPS):
        out_ref[k] = row_refs[k][...] * factor
    out_ref[STEPS] = mine_ref[...] * (factor / norm)
    row = lax.broadcasted_iota(jnp.int32, coef_ref.shape, 0)
    col = lax.broadcasted_iota(jnp.int32, coef_ref.shape, 1)
    coefs = jnp.zeros(coef_ref.shape, F32)
    for k in range(STEPS):
        beta = norms[k][0:1, 0:1] if k < STEPS - 1 else norm
        coefs = jnp.where((row == 0) & (col == k), alphas[k][0:1, 0:1], coefs)
        coefs = jnp.where((row == 1) & (col == k), beta, coefs)
    coef_ref[...] = coefs


def permuted(size):
    return size <= 4 and size & (size - 1) == 0


def share(array, axis):
    size = lax.axis_size(axis)
    if not permuted(size):
        return [swap(jnp.broadcast_to(array[None], (size,) + array.shape), axis).reshape(-1, array.shape[1])]
    return [array] + [lax.ppermute(array, axis, [(d, d ^ s) for d in range(size)]) for s in range(1, size)]


def addends(array, axis):
    size = lax.axis_size(axis)
    if size != 8:
        return [swap(jnp.broadcast_to(array[None], (size,) + array.shape), axis).reshape(-1, array.shape[1])]
    other = lax.ppermute(array, axis, [(d, d ^ 1) for d in range(size)])
    both = call(add_kernel, jax.ShapeDtypeStruct(array.shape, F32), [VMEM] * 2, array, other)
    return [both] + [lax.ppermute(both, axis, [(d, d ^ s) for d in range(size)]) for s in (2, 4, 6)]


def swap(array, axis):
    return lax.all_to_all(array, axis, split_axis=0, concat_axis=0, tiled=True)


def body(start, lat_mats, footprints, blk_sub, blk_off, counts, rinv):
    per_dev, held, lat_rows = start.shape
    nc = lax.axis_size("cell")
    no = lax.axis_size("obs")
    lon_cols = held * nc
    band = lat_rows // nc
    groups = band // CR
    nb, ob, _ = footprints.shape
    subs = counts.shape[0]
    modes = -(-held // 16) * 16
    mine = nc * nb
    periods = per_dev * no
    dims = (nc, nb, modes, groups, band)
    shape = functools.partial(jax.ShapeDtypeStruct, dtype=F32)

    high, low = lon_table(lon_cols, nc, modes)
    if modes != held:
        start = jnp.pad(start, ((0, 0), (0, modes - held), (0, 0)))
        lat_mats = jnp.pad(lat_mats, ((0, modes - held), (0, 0), (0, 0)))
    place = lax.axis_index(("obs", "cell")).astype(jnp.int32).reshape(1)

    start = start.reshape(per_dev * modes, lat_rows)
    near = share(start, "obs")
    foot_rows = nb * CR * modes
    hats, weights = call(
        functools.partial(transform_kernel, dims),
        (jax.ShapeDtypeStruct((nc, foot_rows + 16, ob), BF16), shape((subs, ob))),
        [ANY] * 8,
        place, jnp.asarray(high), jnp.asarray(low), footprints, blk_off, blk_sub, counts, rinv.reshape(subs, ob),
        scratch=[
            pltpu.VMEM(high.shape, BF16),
            pltpu.VMEM(low.shape, BF16),
            pltpu.VMEM(footprints.shape, BF16),
            pltpu.SMEM((nb,), jnp.int32),
            pltpu.SMEM((nb,), jnp.int32),
            pltpu.SMEM((subs,), jnp.int32),
            pltpu.VMEM((subs, ob), F32),
            pltpu.SMEM((1,), jnp.int32),
            pltpu.SemaphoreType.DMA((8,)),
        ],
        limit=60,
    )
    came = swap(hats, "cell")
    lat, start, _ = lax.optimization_barrier((lat_mats, start, weights))
    lat, start, pick = call(
        fetch_kernel,
        (
            shape((lat_rows, modes, lat_rows)),
            shape(start.shape),
            jax.ShapeDtypeStruct((TERMS * CHUNK, CHUNK * 128), BF16),
        ),
        [ANY] * 2,
        lat, start,
        scratch=[pltpu.SemaphoreType.DMA((modes + 1,))],
        limit=50,
        cost=pl.CostEstimate(flops=0, transcendentals=0, bytes_accessed=8 * (lat.size + start.size)),
    )
    if permuted(no):
        near[0] = start

    field_shape = shape((periods, modes, lat_rows))
    small = shape((ROWS, 128))
    own_shape = shape((per_dev, modes, lat_rows))
    sims, field, foot, ids, choose, tail = call(
        functools.partial(first_kernel, dims, no),
        (
            shape((subs + ROWS, ob)),
            field_shape,
            jax.ShapeDtypeStruct((nc, foot_rows, ob), BF16),
            jax.ShapeDtypeStruct((nc, 128), jnp.int32),
            jax.ShapeDtypeStruct((mine, TERMS * subs), BF16),
            shape((ROWS, 128)),
        ),
        [VMEM] * (2 + len(near)),
        lat, came, *near,
        scratch=[pltpu.SMEM((nc, 128), jnp.int32), pltpu.SemaphoreType.DMA] + [pltpu.VMEM((subs, ob), F32)] * PARTS,
    )
    ways = min(no, WAYS)
    rows, alphas, norms = [], [], []
    vector = None
    for step in range(STEPS):
        first, last = step == 0, step == STEPS - 1
        parts = addends(sims, "cell")
        tails = [tail] if first else []
        coefs, norm = call(
            functools.partial(adjoint_kernel, dims, len(tails)),
            (shape((mine + subs + (ROWS if first else 0), 128)), small),
            [VMEM] * (3 + len(tails) + len(parts)),
            choose, weights, foot, *tails, *parts,
            scratch=[pltpu.VMEM((mine, ob), F32)],
        )
        coefs = share(coefs, "obs")
        if first:
            every = call(
                functools.partial(every_kernel, dims, no, mine + subs),
                jax.ShapeDtypeStruct((2 * no, 128), jnp.int32),
                [VMEM] * len(coefs),
                *coefs,
            )
        before = [] if first else [vector]
        sims, row, field, *vector, alpha = call(
            functools.partial(image_kernel, dims, no, first, last),
            (
                shape((ROWS if last else subs + ROWS, 128)),
                own_shape,
                own_shape if last else field_shape,
                *([] if last else [field_shape]),
                small,
            ),
            [SMEM] * 2 + [VMEM] * (5 + len(before) + len(coefs)),
            ids, every, lat, foot, pick, norm, field, *before, *coefs,
            scratch=[pltpu.VMEM(field_shape.shape, F32)] * last
            + [pltpu.VMEM((no, mine, 128), F32)]
            + [pltpu.VMEM(field_shape.shape, F32)] * ways
            + [pltpu.VMEM((subs, ob), F32)] * PARTS,
            limit=16,
        )
        vector = None if last else vector[0]
        rows.append(row)
        alphas.append(alpha)
        norms.append(norm)
    factor = math.sqrt(periods * lon_cols * lat_rows)
    parts = addends(sims, "cell")
    krylov, coeffs = call(
        functools.partial(finish_kernel, factor, len(parts)),
        (shape((STEPS + 1, per_dev, modes, lat_rows)), shape((2, STEPS))),
        [VMEM] * (len(parts) + STEPS + 1 + STEPS + STEPS - 1),
        *parts, *rows, field, *alphas, *norms[1:],
    )
    return krylov[:, :, :held], coeffs


def solution(mesh):
    placed = (
        P("obs", "cell", None),
        P("cell", None, None),
        P(("obs", "cell"), None, None),
        P(("obs", "cell")),
        P(("obs", "cell")),
        P("obs"),
        P("obs"),
    )
    return jax.shard_map(
        body,
        mesh=mesh,
        in_specs=placed,
        out_specs=(P(None, "obs", "cell", None), P()),
        check_vma=False,
    )
```

```python
import functools
import math

import jax
import jax.numpy as jnp
import ml_dtypes
import numpy as np
from jax import lax
from jax.experimental import pallas as pl
from jax.experimental.pallas import tpu as pltpu
from jax.sharding import PartitionSpec as P

CR = 2
WAYS = 4
PARTS = 4
CHUNK = 16
TERMS = 3
STEPS = 3
ROWS = 8
VMEM = pl.BlockSpec(memory_space=pltpu.VMEM)
SMEM = pl.BlockSpec(memory_space=pltpu.SMEM)
ANY = pl.BlockSpec(memory_space=pl.ANY)
F32 = jnp.float32
BF16 = jnp.bfloat16


def lon_table(order, parts, padded):
    index = np.arange(order)
    half = order // 2
    freq = np.where(index <= half, index, index - half)[:, None]
    phase = (freq * index[None, :] % order) * (2.0 * math.pi / order)
    factor = np.where((index == 0) | (index == half), math.sqrt(1.0 / order), math.sqrt(2.0 / order))
    table = np.where(index[:, None] <= half, np.cos(phase), np.sin(phase)) * factor[:, None]
    table = table.reshape(parts, order // parts, order)
    table = np.pad(table, ((0, 0), (0, padded - order // parts), (0, 0))).reshape(parts * padded, order)
    high = table.astype(np.float32).astype(ml_dtypes.bfloat16)
    low = (table - high.astype(np.float64)).astype(np.float32).astype(ml_dtypes.bfloat16)
    return high, low


def call(kernel, outs, specs, *args, scratch=(), limit=8, cost=None):
    return pl.pallas_call(
        kernel,
        out_shape=outs,
        in_specs=specs,
        out_specs=jax.tree.map(lambda _: VMEM, outs),
        scratch_shapes=scratch,
        cost_estimate=cost,
        compiler_params=pltpu.CompilerParams(vmem_limit_bytes=limit * 1024 * 1024),
    )(*args)


def tree_sum(parts):
    parts = list(parts)
    while len(parts) > 1:
        parts = [sum(parts[at:at + 2][1:], parts[at]) for at in range(0, len(parts), 2)]
    return parts[0]


def transform_kernel(dims, place_any, high_any, low_any, foot_any, off_any, sub_any, count_any, rinv_any, *refs):
    nc, nb, modes, groups, band = dims
    out_ref, weight_ref, high_ref, low_ref, foot_ref, off_ref, sub_ref, count_ref, rinv_ref, place_ref, sems = refs
    copies = [
        pltpu.make_async_copy(source, target, sems.at[at])
        for at, (source, target) in enumerate(
            [
                (foot_any, foot_ref),
                (high_any, high_ref),
                (low_any, low_ref),
                (off_any, off_ref),
                (sub_any, sub_ref),
                (count_any, count_ref),
                (rinv_any, rinv_ref),
                (place_any, place_ref),
            ]
        )
    ]
    for copy in copies:
        copy.start()
    ob = foot_ref.shape[1]
    lon = high_ref.shape[1]
    contract = (((1,), (1,)), ((), ()))
    copies[0].wait()
    copies[1].wait()
    feet = [foot_ref[:, :, r * lon:(r + 1) * lon].reshape(nb * ob, lon) for r in range(CR)]
    hats = [lax.dot_general(high_ref[...], foot, contract, preferred_element_type=F32) for foot in feet]
    copies[2].wait()
    for r in range(CR):
        hat = hats[r] + lax.dot_general(low_ref[...], feet[r], contract, preferred_element_type=F32)
        hat = hat.astype(BF16)
        for b in range(nb):
            at = (b * CR + r) * modes
            for c in range(nc):
                out_ref[c, at:at + modes, :] = hat[c * modes:(c + 1) * modes, b * ob:(b + 1) * ob]
    for copy in copies[3:]:
        copy.wait()
    cell = place_ref[0] % nc
    obs = place_ref[0] // nc
    lane = lax.broadcasted_iota(jnp.int32, (16, ob), 1)
    ids = jnp.zeros((16, ob), F32)
    for b in range(nb):
        off = off_ref[b]
        values = (off // groups, cell * (band // CR) + off % groups, sub_ref[b])
        for at, value in enumerate(values):
            ids = jnp.where(lane == at * nb + b, value.astype(F32), ids)
    ids = jnp.where(lane == 3 * nb, obs.astype(F32), ids).astype(BF16)
    for c in range(nc):
        out_ref[c, nb * CR * modes:, :] = ids
    row = lax.broadcasted_iota(jnp.int32, weight_ref.shape, 0)
    limit = jnp.zeros(weight_ref.shape, jnp.int32)
    for s in range(weight_ref.shape[0]):
        limit = jnp.where(row == s, count_ref[s], limit)
    lane = lax.broadcasted_iota(jnp.int32, weight_ref.shape, 1)
    weight_ref[...] = jnp.where(lane < limit, rinv_ref[...], 0.0)


def fetch_kernel(lat_any, start_any, lat_ref, start_ref, pick_ref, sems):
    modes = lat_any.shape[0]
    copies = [pltpu.make_async_copy(lat_any.at[m], lat_ref.at[:, m, :], sems.at[m]) for m in range(modes)]
    copies.append(pltpu.make_async_copy(start_any, start_ref, sems.at[modes]))
    for copy in copies:
        copy.start()
    line = lax.broadcasted_iota(jnp.int32, pick_ref.shape, 0)
    lane = lax.broadcasted_iota(jnp.int32, pick_ref.shape, 1)
    pick_ref[...] = jnp.where(line % CHUNK == lane // 128, 1.0, 0.0).astype(BF16)
    for copy in copies:
        copy.wait()


def fold(ref):
    periods, modes, _ = ref.shape
    total = jnp.zeros((ROWS, ref.shape[2]), F32)
    for p in range(periods):
        for at in range(0, modes, ROWS):
            part = ref[p, at:at + ROWS, :]
            total += part * part
    return total


def forward(dims, field_ref, lat_ref, foot_ref, ids_ref, part_refs, sim_ref):
    nc, nb, modes, groups, band = dims
    subs = sim_ref.shape[0] - ROWS
    for part_ref in part_refs:
        part_ref[...] = jnp.zeros_like(part_ref)
    found = []
    for j in range(nc):
        for b in range(nb):
            period = ids_ref[j, b]
            row = ids_ref[j, nb + b] * CR
            sub = ids_ref[j, 2 * nb + b]
            total = None
            for r in range(CR):
                column = jnp.sum(lat_ref[row + r] * field_ref[period], axis=1, keepdims=True)
                at = (b * CR + r) * modes
                term = foot_ref[j, at:at + modes, :].astype(F32) * column
                total = term if total is None else total + term
            found.append((sub, jnp.sum(total, axis=0, keepdims=True)))
    sim_ref[subs:, :] = fold(field_ref)
    for at in range(0, len(found), len(part_refs)):
        here = list(zip(part_refs, found[at:at + len(part_refs)]))
        sums = [part_ref[pl.ds(sub, 1), :] + line for part_ref, (sub, line) in here]
        for (part_ref, (sub, _)), line in zip(here, sums):
            part_ref[pl.ds(sub, 1), :] = line
    sim_ref[:subs, :] = tree_sum(part_ref[...] for part_ref in part_refs)


def pieces(refs, size, rows):
    found = []
    for ref in refs:
        found += [ref.at[at:at + rows] for at in range(0, ref.shape[0], rows)]
    assert len(found) == size
    return found


def added(refs, rows):
    return tree_sum(ref[...] for ref in pieces(refs, sum(ref.shape[0] for ref in refs) // rows, rows))


def add_kernel(one_ref, other_ref, out_ref):
    out_ref[...] = one_ref[...] + other_ref[...]


def first_kernel(dims, no, lat_ref, came_ref, *refs):
    nc, nb, modes, _, _ = dims
    refs, part_refs = refs[:-PARTS], refs[-PARTS:]
    near_refs, refs = refs[:-8], refs[-8:]
    out_ref, field_ref, foot_ref, all_ref, choose_ref, tail_ref, ids_ref, sem = refs
    rows = nb * CR * modes
    for j in range(nc):
        all_ref[j:j + 1, :] = came_ref[j, rows:rows + 16, :].astype(F32)[0:1].astype(jnp.int32)
    copy = pltpu.make_async_copy(all_ref, ids_ref, sem)
    copy.start()
    for j in range(nc):
        foot_ref[j] = came_ref[j, :rows, :]
    per_dev = field_ref.shape[0] // no
    copy.wait()
    own = ids_ref[0, 3 * nb]
    for s, near_ref in enumerate(pieces(near_refs, no, per_dev * modes)):
        for l in range(per_dev):
            field_ref[((own ^ s) if permuted(no) else s) * per_dev + l] = near_ref[l * modes:(l + 1) * modes, :]
    line = lax.broadcasted_iota(jnp.int32, choose_ref.shape, 0)
    lane = lax.broadcasted_iota(jnp.int32, choose_ref.shape, 1)
    tail_line = lax.broadcasted_iota(jnp.int32, tail_ref.shape, 0)
    tail_lane = lax.broadcasted_iota(jnp.int32, tail_ref.shape, 1)
    subs = jnp.zeros(choose_ref.shape, jnp.int32)
    tail = jnp.zeros(tail_ref.shape, jnp.int32)
    for j in range(nc):
        for b in range(nb):
            subs = jnp.where(line == j * nb + b, ids_ref[j, 2 * nb + b], subs)
            value = jnp.where(tail_line == 0, ids_ref[j, b], ids_ref[j, nb + b])
            tail = jnp.where(tail_lane == j * nb + b, value, tail)
    choose_ref[...] = jnp.where(lane % (choose_ref.shape[1] // TERMS) == subs, 1.0, 0.0).astype(BF16)
    tail_ref[...] = tail.astype(F32)
    forward(dims, field_ref, lat_ref, foot_ref, ids_ref, part_refs, out_ref)


def split(values):
    terms = []
    for _ in range(TERMS):
        terms.append(values.astype(BF16).astype(F32))
        values = values - terms[-1]
    return jnp.concatenate(terms, axis=0).astype(BF16)


def adjoint_kernel(dims, tails, choose_ref, weight_ref, foot_ref, *refs):
    nc, nb, modes, groups, band = dims
    tail_refs, refs = refs[:tails], refs[tails:]
    sim_refs, refs = refs[:-3], refs[-3:]
    out_ref, norm_ref, chosen_ref = refs
    subs = weight_ref.shape[0]
    mine = nc * nb
    total = added(sim_refs, subs + ROWS)
    norm = jnp.sqrt(jnp.sum(total[subs:], keepdims=True))
    norm_ref[...] = jnp.broadcast_to(norm, norm_ref.shape)
    scale = 1.0 / norm
    sim = total[:subs]
    weighted = sim * weight_ref[...]
    chosen_ref[...] = jnp.dot(choose_ref[...], split(weighted), preferred_element_type=F32)
    lane = lax.broadcasted_iota(jnp.int32, (modes, 128), 1)
    parts = [jnp.zeros((modes, 128), F32) for _ in range(CR)]
    for j in range(nc):
        for b in range(nb):
            at_t = j * nb + b
            chosen = chosen_ref[at_t:at_t + 1, :]
            for r in range(CR):
                at = (b * CR + r) * modes
                column = jnp.sum(foot_ref[j, at:at + modes, :].astype(F32) * chosen, axis=1, keepdims=True)
                parts[r] = jnp.where(lane == at_t, column, parts[r])
    rest = 128 - CR * modes
    if rest:
        parts.append(jnp.zeros((rest, 128), F32))
    rows = jnp.concatenate(parts, axis=0).T
    out_ref[:mine, :] = rows[:mine] * scale
    out_ref[mine:mine + subs, :] = (sim * scale) * (weighted * scale)
    for tail_ref in tail_refs:
        out_ref[mine + subs:, :] = tail_ref[...]


def every_kernel(dims, no, at, *refs):
    refs, out_ref = refs[:-1], refs[-1]
    rows = sum(ref.shape[0] for ref in refs) // no
    for s, ref in enumerate(pieces(refs, no, rows)):
        out_ref[2 * s:2 * s + 2, :] = ref[at:at + ROWS, :][0:2].astype(jnp.int32)


def image_kernel(dims, no, first, last, ids_ref, all_ref, lat_ref, foot_ref, pick_ref, norm_ref, field_ref, *refs):
    nc, nb, modes, groups, band = dims
    if not first:
        prior_ref, refs = refs[0], refs[1:]
    ways = min(no, WAYS)
    refs, part_refs = refs[:-PARTS], refs[-PARTS:]
    kept = 6 + ways
    coef_refs, refs = refs[:-kept], refs[-kept:]
    sum_refs, refs = refs[-ways:], refs[:-ways]
    if last:
        out_ref, row_ref, mine_ref, alpha_ref, next_ref, held_ref = refs
    else:
        out_ref, row_ref, next_ref, vector_ref, alpha_ref, held_ref = refs
    mine = nc * nb
    periods = field_ref.shape[0]
    per_dev = row_ref.shape[0]
    subs = ROWS
    rows = sum(ref.shape[0] for ref in coef_refs) // no
    coef_refs = pieces(coef_refs, no, rows)
    for s in range(no):
        held_ref[s] = coef_refs[s][:mine, :]
    for sum_ref in sum_refs:
        sum_ref[...] = jnp.zeros_like(sum_ref)
    gain = jnp.sum(tree_sum(ref[mine:mine + subs, :] for ref in coef_refs), keepdims=True)
    alpha_ref[...] = jnp.broadcast_to(1.0 + gain, alpha_ref.shape)
    norm = norm_ref[0:1, :]
    scale = 1.0 / norm
    own = ids_ref[0, 3 * nb]

    def group(at, carry):
        found = [at * ways + i for i in range(ways)]
        for chunk in range(0, mine, CHUNK):
            left = [split(held_ref[s, chunk:chunk + CHUNK, :]) for s in found]
            left = jnp.concatenate(left, axis=1)
            for pair in range(0, CHUNK, 2):
                wide = lax.dot_general(
                    left,
                    pick_ref[:, pair * 128:(pair + 2) * 128],
                    (((0,), (0,)), ((), ())),
                    preferred_element_type=F32,
                )
                for at_t in range(2):
                    at_block = chunk + pair + at_t
                    totals = []
                    for i, s in enumerate(found):
                        row = all_ref[2 * s + 1, at_block] * CR
                        total = sum_refs[i][all_ref[2 * s, at_block]]
                        for r in range(CR):
                            start = i * 128 + r * modes
                            coef = wide[start:start + modes, at_t * 128:(at_t + 1) * 128]
                            total += coef * lat_ref[row + r]
                        totals.append(total)
                    for i, s in enumerate(found):
                        sum_refs[i][all_ref[2 * s, at_block]] = totals[i]
        return carry

    if no <= 4:
        for at in range(no // ways):
            group(at, 0)
    else:
        lax.fori_loop(0, no // ways, group, 0)
    for p in range(periods):
        vector = field_ref[p] * scale
        if not last:
            vector_ref[p] = vector
        rest = tree_sum(sum_ref[p] for sum_ref in sum_refs) - vector * gain
        if not first:
            rest -= prior_ref[p] * norm
        next_ref[p] = rest
    for l in range(per_dev):
        row_ref[l] = field_ref[own * per_dev + l] * scale
    if last:
        out_ref[...] = fold(next_ref)
        for l in range(per_dev):
            mine_ref[l] = next_ref[own * per_dev + l]
    else:
        forward(dims, next_ref, lat_ref, foot_ref, ids_ref, part_refs, out_ref)


def finish_kernel(factor, sums, *refs):
    sum_refs, refs = refs[:sums], refs[sums:]
    row_refs, refs = refs[:STEPS], refs[STEPS:]
    mine_ref, refs = refs[0], refs[1:]
    alphas, refs = refs[:STEPS], refs[STEPS:]
    norms, refs = refs[:STEPS - 1], refs[STEPS - 1:]
    out_ref, coef_ref = refs
    norm = jnp.sqrt(jnp.sum(added(sum_refs, ROWS), keepdims=True))
    for k in range(STEPS):
        out_ref[k] = row_refs[k][...] * factor
    out_ref[STEPS] = mine_ref[...] * (factor / norm)
    row = lax.broadcasted_iota(jnp.int32, coef_ref.shape, 0)
    col = lax.broadcasted_iota(jnp.int32, coef_ref.shape, 1)
    coefs = jnp.zeros(coef_ref.shape, F32)
    for k in range(STEPS):
        beta = norms[k][0:1, 0:1] if k < STEPS - 1 else norm
        coefs = jnp.where((row == 0) & (col == k), alphas[k][0:1, 0:1], coefs)
        coefs = jnp.where((row == 1) & (col == k), beta, coefs)
    coef_ref[...] = coefs


def permuted(size):
    return size <= 4 and size & (size - 1) == 0


def share(array, axis):
    size = lax.axis_size(axis)
    if not permuted(size):
        return [swap(jnp.broadcast_to(array[None], (size,) + array.shape), axis).reshape(-1, array.shape[1])]
    came = [lax.ppermute(array, axis, [(d, d ^ s) for d in range(size)]) for s in range(size - 1, 0, -1)]
    return [array] + came[::-1]


def addends(array, axis):
    size = lax.axis_size(axis)
    if size != 8:
        return [swap(jnp.broadcast_to(array[None], (size,) + array.shape), axis).reshape(-1, array.shape[1])]
    other = lax.ppermute(array, axis, [(d, d ^ 1) for d in range(size)])
    both = call(add_kernel, jax.ShapeDtypeStruct(array.shape, F32), [VMEM] * 2, array, other)
    return [both] + [lax.ppermute(both, axis, [(d, d ^ s) for d in range(size)]) for s in (6, 4, 2)][::-1]


def swap(array, axis):
    return lax.all_to_all(array, axis, split_axis=0, concat_axis=0, tiled=True)


def body(start, lat_mats, footprints, blk_sub, blk_off, counts, rinv):
    per_dev, held, lat_rows = start.shape
    nc = lax.axis_size("cell")
    no = lax.axis_size("obs")
    lon_cols = held * nc
    band = lat_rows // nc
    groups = band // CR
    nb, ob, _ = footprints.shape
    subs = counts.shape[0]
    modes = -(-held // 16) * 16
    mine = nc * nb
    periods = per_dev * no
    dims = (nc, nb, modes, groups, band)
    shape = functools.partial(jax.ShapeDtypeStruct, dtype=F32)

    high, low = lon_table(lon_cols, nc, modes)
    if modes != held:
        start = jnp.pad(start, ((0, 0), (0, modes - held), (0, 0)))
        lat_mats = jnp.pad(lat_mats, ((0, modes - held), (0, 0), (0, 0)))
    place = lax.axis_index(("obs", "cell")).astype(jnp.int32).reshape(1)

    start = start.reshape(per_dev * modes, lat_rows)
    near = share(start, "obs")
    foot_rows = nb * CR * modes
    hats, weights = call(
        functools.partial(transform_kernel, dims),
        (jax.ShapeDtypeStruct((nc, foot_rows + 16, ob), BF16), shape((subs, ob))),
        [ANY] * 8,
        place, jnp.asarray(high), jnp.asarray(low), footprints, blk_off, blk_sub, counts, rinv.reshape(subs, ob),
        scratch=[
            pltpu.VMEM(high.shape, BF16),
            pltpu.VMEM(low.shape, BF16),
            pltpu.VMEM(footprints.shape, BF16),
            pltpu.SMEM((nb,), jnp.int32),
            pltpu.SMEM((nb,), jnp.int32),
            pltpu.SMEM((subs,), jnp.int32),
            pltpu.VMEM((subs, ob), F32),
            pltpu.SMEM((1,), jnp.int32),
            pltpu.SemaphoreType.DMA((8,)),
        ],
        limit=60,
    )
    came = swap(hats, "cell")
    lat, start, _ = lax.optimization_barrier((lat_mats, start, weights))
    lat, start, pick = call(
        fetch_kernel,
        (
            shape((lat_rows, modes, lat_rows)),
            shape(start.shape),
            jax.ShapeDtypeStruct((TERMS * CHUNK, CHUNK * 128), BF16),
        ),
        [ANY] * 2,
        lat, start,
        scratch=[pltpu.SemaphoreType.DMA((modes + 1,))],
        limit=50,
        cost=pl.CostEstimate(flops=0, transcendentals=0, bytes_accessed=8 * (lat.size + start.size)),
    )
    if permuted(no):
        near[0] = start

    field_shape = shape((periods, modes, lat_rows))
    small = shape((ROWS, 128))
    own_shape = shape((per_dev, modes, lat_rows))
    sims, field, foot, ids, choose, tail = call(
        functools.partial(first_kernel, dims, no),
        (
            shape((subs + ROWS, ob)),
            field_shape,
            jax.ShapeDtypeStruct((nc, foot_rows, ob), BF16),
            jax.ShapeDtypeStruct((nc, 128), jnp.int32),
            jax.ShapeDtypeStruct((mine, TERMS * subs), BF16),
            shape((ROWS, 128)),
        ),
        [VMEM] * (2 + len(near)),
        lat, came, *near,
        scratch=[pltpu.SMEM((nc, 128), jnp.int32), pltpu.SemaphoreType.DMA] + [pltpu.VMEM((subs, ob), F32)] * PARTS,
    )
    ways = min(no, WAYS)
    rows, alphas, norms = [], [], []
    vector = None
    for step in range(STEPS):
        first, last = step == 0, step == STEPS - 1
        parts = addends(sims, "cell")
        tails = [tail] if first else []
        coefs, norm = call(
            functools.partial(adjoint_kernel, dims, len(tails)),
            (shape((mine + subs + (ROWS if first else 0), 128)), small),
            [VMEM] * (3 + len(tails) + len(parts)),
            choose, weights, foot, *tails, *parts,
            scratch=[pltpu.VMEM((mine, ob), F32)],
        )
        coefs = share(coefs, "obs")
        if first:
            every = call(
                functools.partial(every_kernel, dims, no, mine + subs),
                jax.ShapeDtypeStruct((2 * no, 128), jnp.int32),
                [VMEM] * len(coefs),
                *coefs,
            )
        before = [] if first else [vector]
        sims, row, field, *vector, alpha = call(
            functools.partial(image_kernel, dims, no, first, last),
            (
                shape((ROWS if last else subs + ROWS, 128)),
                own_shape,
                own_shape if last else field_shape,
                *([] if last else [field_shape]),
                small,
            ),
            [SMEM] * 2 + [VMEM] * (5 + len(before) + len(coefs)),
            ids, every, lat, foot, pick, norm, field, *before, *coefs,
            scratch=[pltpu.VMEM(field_shape.shape, F32)] * last
            + [pltpu.VMEM((no, mine, 128), F32)]
            + [pltpu.VMEM(field_shape.shape, F32)] * ways
            + [pltpu.VMEM((subs, ob), F32)] * PARTS,
            limit=16,
        )
        vector = None if last else vector[0]
        rows.append(row)
        alphas.append(alpha)
        norms.append(norm)
    factor = math.sqrt(periods * lon_cols * lat_rows)
    parts = addends(sims, "cell")
    krylov, coeffs = call(
        functools.partial(finish_kernel, factor, len(parts)),
        (shape((STEPS + 1, per_dev, modes, lat_rows)), shape((2, STEPS))),
        [VMEM] * (len(parts) + STEPS + 1 + STEPS + STEPS - 1),
        *parts, *rows, field, *alphas, *norms[1:],
    )
    return krylov[:, :, :held], coeffs


def solution(mesh):
    placed = (
        P("obs", "cell", None),
        P("cell", None, None),
        P(("obs", "cell"), None, None),
        P(("obs", "cell")),
        P(("obs", "cell")),
        P("obs"),
        P("obs"),
    )
    return jax.shard_map(
        body,
        mesh=mesh,
        in_specs=placed,
        out_specs=(P(None, "obs", "cell", None), P()),
        check_vma=False,
    )
```
